128 devices in a mesh: prow: 8 (over y_hi, z), pcol: 16 (over x, y_lo, core).
Axes of the slice: x: 4, y: 4 (y_hi: 2, y_lo: 2; y = y_hi * 2 + y_lo), z: 4, core: 2. Of those that a mesh axis runs over, the one named last changes fastest.
Arguments:
- front_entries: float32 [12288, 12288], P('prow', 'pcol'), may hold values from -6 to 6
- diagonal: float32 [12288], replicated, may hold values from 120 to 240
- child_update: float32 [16384, 8192], P('prow', 'pcol'), may hold values from -6 to 6
- child_map: int32 [2, 64], replicated, may hold values from 0 to 95, as said below
Outputs:
- factored: float32 [12288, 12288], P('prow', 'pcol')
The draws below stay inside these ranges and needn't reach their ends.
Inputs may be any that keep to these rules, and one draw needn't show every extreme that they name: Each row of child_map names 64 distinct front blocks, and child_map[c, k] mod 16 = (k + r_c) mod 16 for a shift r_c of child c.
All inputs are finite; a program needn't handle non-finite values.
Results may differ from the reference program's by a relative error of at most 0.0001.
Values sent between devices are 32-bit elements; how exact they have to be, the bound alone decides.
No kernel may reach another device: no remote copies, remote signals or barrier semaphores. Data moves between devices by JAX's collectives and lax.ppermute only.
A program may use at most 192 MiB of HBM per device.

```python
import jax
import jax.numpy as jnp
from jax import lax

FRONT = 12288
CHILD = 8192
BLOCK = 128
PANEL = 512
PANELS = 2
N_PROW = 8
N_PCOL = 16


def shuffle_slots(one_key):
    return jax.random.permutation(one_key, FRONT // BLOCK // N_PCOL)


def draw_child_map(key, part):
    key = jax.random.fold_in(key, 7)
    shift_key = jax.random.fold_in(key, 1)
    slot_key = jax.random.fold_in(key, 2)
    child_blocks = CHILD // BLOCK
    slots_each = FRONT // BLOCK // N_PCOL
    shifts = jax.random.randint(shift_key, (2,), 0, N_PCOL)
    position = jnp.arange(child_blocks)
    residue = (shifts[:, None] + position[None, :]) % N_PCOL
    ranking = jnp.broadcast_to(position[None, :] // N_PCOL, (2, child_blocks))
    slot_keys = jax.random.split(slot_key, 2 * N_PCOL)
    tables = jax.vmap(shuffle_slots)(slot_keys).reshape(2, N_PCOL, slots_each)
    child_index = jnp.broadcast_to(jnp.arange(2)[:, None], (2, child_blocks))
    chosen = tables[child_index, residue, ranking]
    return (chosen * N_PCOL + residue).astype(jnp.int32)


def level_of(stream_key, extent, shards, low, top_value):
    def one(axis_at, shards_of):
        steps = jax.random.uniform(jax.random.fold_in(jax.random.fold_in(stream_key, 6), axis_at), (shards_of,), jnp.float32, low / len(shards), top_value / len(shards))
        return jnp.repeat(jnp.exp(steps), extent[axis_at] // shards_of).reshape((-1,) + (1,) * (len(extent) - axis_at - 1))

    loudness = one(*shards[0])
    for cut in shards[1:]:
        loudness = loudness * one(*cut)
    return loudness


def noise(own_key, shape, scale, limit, cuts=(), kind=jnp.bfloat16):
    factor_of = level_of(own_key, shape, cuts, -0.22, 0.18) if cuts else 1.0
    drawn = jax.random.normal(own_key, shape, jnp.float32) * scale * factor_of
    return jnp.minimum(jnp.maximum(drawn, -limit), limit).astype(kind)


def setup_inputs(seed: int = 0) -> dict:
    splits = jax.random.split(jax.random.key(seed), 5)
    return {
        "front_entries": noise(splits[0], (FRONT, FRONT), 0.6, 6.0, ((0, 8), (1, 16)), jnp.float32),
        "diagonal": jnp.clip(jax.random.uniform(splits[1], (FRONT,), jnp.float32, 120.0, 240.0), 120.0, 240.0),
        "child_update": noise(splits[2], (2 * CHILD, CHILD), 0.6, 6.0, ((0, 8), (1, 16)), jnp.float32),
        "child_map": draw_child_map(jax.random.fold_in(splits[4], 71), 0),
    }


def reference(front_entries, diagonal, child_update, child_map):
    front_blocks = FRONT // BLOCK
    child_blocks = CHILD // BLOCK
    highest = lax.Precision.HIGHEST
    numbers = jnp.arange(front_blocks)
    rows_each = front_blocks // N_PROW
    cols_each = front_blocks // N_PCOL
    row_stored = numbers % N_PROW * rows_each + numbers // N_PROW
    col_stored = numbers % N_PCOL * cols_each + numbers // N_PCOL
    row_global = numbers % rows_each * N_PROW + numbers // rows_each
    col_global = numbers % cols_each * N_PCOL + numbers // cols_each
    blocked = front_entries.reshape(front_blocks, BLOCK, front_blocks, BLOCK).transpose(0, 2, 1, 3)
    blocked = blocked[row_stored][:, col_stored]
    diag_blocks = diagonal.reshape(front_blocks, BLOCK)[:, :, None] * jnp.eye(BLOCK, dtype=jnp.float32)[None]
    blocked = blocked.at[numbers, numbers].add(diag_blocks)
    for child in range(2):
        update = child_update[child * CHILD:(child + 1) * CHILD]
        update = update.reshape(child_blocks, BLOCK, child_blocks, BLOCK).transpose(0, 2, 1, 3)
        targets = child_map[child].astype(jnp.int32)
        blocked = blocked.at[targets[:, None], targets[None, :]].add(update)
    matrix = blocked.transpose(0, 2, 1, 3).reshape(FRONT, FRONT)
    for panel_index in range(PANELS):
        lower_edge = panel_index * PANEL
        upper_edge = lower_edge + PANEL
        pivot_block = matrix[lower_edge:upper_edge, lower_edge:upper_edge]
        pivot_block = 0.5 * (pivot_block + pivot_block.T)
        factor = jnp.linalg.cholesky(pivot_block)
        below_rows = lax.linalg.triangular_solve(factor, matrix[upper_edge:, lower_edge:upper_edge], left_side=False, lower=True, transpose_a=True)
        product = jnp.einsum('ik,jk->ij', below_rows, below_rows, precision=highest)
        matrix = matrix.at[upper_edge:, upper_edge:].add(-product)
        matrix = matrix.at[lower_edge:upper_edge, lower_edge:upper_edge].set(factor)
        matrix = matrix.at[upper_edge:, lower_edge:upper_edge].set(below_rows)
        matrix = matrix.at[lower_edge:upper_edge, upper_edge:].set(0.0)
    blocked = matrix.reshape(front_blocks, BLOCK, front_blocks, BLOCK).transpose(0, 2, 1, 3)
    blocked = blocked[row_global][:, col_global]
    return blocked.transpose(0, 2, 1, 3).reshape(FRONT, FRONT)
```

```python
import functools

import jax
import jax.numpy as jnp
from jax import lax
from jax.experimental import pallas as pl
from jax.experimental.pallas import tpu as pltpu
from jax.sharding import PartitionSpec as P

BLOCK = 128
HEAD = 8
F32 = jnp.float32
BF16 = jnp.bfloat16
HIGHEST = lax.Precision.HIGHEST
MIB = 1024 * 1024

PLANE_GROUPS = [[16 * p + 4 * x + w for w in range(4) for p in range(8)] for x in range(4)]


def pack_rows(child, child_map):
    def kernel(map_ref, child_ref, out_ref, buf, turned, sems):
        c = lax.axis_index("prow") // 4
        shift = map_ref[c * 64] % 16

        def fetch(i):
            rows = pl.ds(pl.multiple_of(i * BLOCK, BLOCK), BLOCK)
            return pltpu.make_async_copy(child_ref.at[rows], buf.at[i], sems.at[0, i])

        def store(i):
            residue = (i + shift) % 16
            return pltpu.make_async_copy(
                turned.at[i], out_ref.at[:, residue % 8, residue // 8], sems.at[1, i]
            )

        def forward(i):
            fetch(i).wait()
            for w in range(4):
                b = (w - shift + 16) % 4
                turned[i, w] = buf[i, :, pl.ds(pl.multiple_of(b * BLOCK, BLOCK), BLOCK)]
            store(i).start()

        pl.loop(0, 16)(lambda i: fetch(i).start())
        pl.loop(0, 16)(forward)
        pl.loop(0, 16)(lambda i: store(i).wait())

    return pl.pallas_call(
        kernel,
        out_shape=jax.ShapeDtypeStruct((4, 8, 2, BLOCK, BLOCK), F32),
        in_specs=[pl.BlockSpec(memory_space=pltpu.SMEM), pl.BlockSpec(memory_space=pl.ANY)],
        out_specs=pl.BlockSpec(memory_space=pl.ANY),
        scratch_shapes=[
            pltpu.VMEM((16, BLOCK, 4 * BLOCK), F32),
            pltpu.VMEM((16, 4, BLOCK, BLOCK), F32),
            pltpu.SemaphoreType.DMA((2, 16)),
        ],
        compiler_params=pltpu.CompilerParams(vmem_limit_bytes=16 * MIB),
        cost_estimate=pl.CostEstimate(flops=0, bytes_accessed=8 * MIB, transcendentals=0),
        name="pack_rows",
    )(child_map, child)


def pack_cols(arrived, child_map):
    def kernel(map_ref, in_ref, *refs):
        out_refs, (buf, sems) = refs[:4], refs[4:]
        q = lax.axis_index("pcol")
        x, w = q // 4, q % 4

        def fetch(k):
            d, c = k // 2, k % 2
            column = 4 * ((x + d) % 4) + w
            a = ((column - map_ref[c * 64] % 16 + 16) % 16) // 4
            return pltpu.make_async_copy(in_ref.at[a, c], buf.at[k], sems.at[0, k])

        def store(k):
            return pltpu.make_async_copy(buf.at[k], out_refs[k // 2].at[k % 2], sems.at[1, k])

        for k in range(8):
            fetch(k).start()
        for k in range(8):
            fetch(k).wait()
            store(k).start()
        for k in range(8):
            store(k).wait()

    return pl.pallas_call(
        kernel,
        out_shape=[jax.ShapeDtypeStruct((2, 4, 2, BLOCK, BLOCK), F32)] * 4,
        in_specs=[pl.BlockSpec(memory_space=pltpu.SMEM), pl.BlockSpec(memory_space=pl.ANY)],
        out_specs=[pl.BlockSpec(memory_space=pl.ANY)] * 4,
        scratch_shapes=[
            pltpu.VMEM((8, 4, 2, BLOCK, BLOCK), F32), pltpu.SemaphoreType.DMA((2, 8))
        ],
        compiler_params=pltpu.CompilerParams(vmem_limit_bytes=16 * MIB),
        cost_estimate=pl.CostEstimate(flops=0, bytes_accessed=8 * MIB, transcendentals=0),
        name="pack_cols",
    )(child_map, arrived)


def diag_block(values):
    rows = lax.broadcasted_iota(jnp.int32, (BLOCK, BLOCK), 0)
    cols = lax.broadcasted_iota(jnp.int32, (BLOCK, BLOCK), 1)
    return jnp.where(rows == cols, jnp.broadcast_to(values, (BLOCK, BLOCK)), 0.0)


def local_row(map_ref, c, h, n, p):
    shift = map_ref[c * 64] % 16
    i = (p + 8 * n - shift + 16) % 16
    return map_ref[c * 64 + 16 * h + i] // 8


def local_col(map_ref, c, t, q):
    shift = map_ref[c * 64] % 16
    return map_ref[c * 64 + 16 * t + (q - shift + 16) % 16] // 16


def panel_terms(front, diagonal, arrived, child_map):
    def kernel(map_ref, front_ref, diag_ref, in_ref, *refs):
        out_refs, head_ref, (total, buf, sems) = refs[:4], refs[4], refs[5:]
        p, q = lax.axis_index("prow"), lax.axis_index("pcol")
        x, w = q // 4, q % 4
        chosen, copies = [], []
        for e in range(2):
            for c in range(2):
                at = (4 * e + w - map_ref[c * 64] % 16 + 16) % 16
                chosen.append(map_ref[c * 64 + 16 * x + at] // 16 == 0)
                copies.append(
                    pltpu.make_async_copy(
                        in_ref.at[at // 4, c], buf.at[2 * e + c], sems.at[2 * e + c]
                    )
                )
                copies[-1].start()
        total[...] = jnp.zeros_like(total)

        @pl.when(x < 2)
        def _():
            for l in range(12):
                total[l % 2 * 2 + x, l // 2] = front_ref[l * BLOCK : (l + 1) * BLOCK, :]

        @pl.when(p == q)
        def _():
            total[x, 0] += diag_block(diag_ref[pl.ds(q, 1), :])

        for k in range(4):
            e, c = k // 2, k % 2
            copies[k].wait()

            @pl.when(chosen[k])
            def _():
                def add(i):
                    l = local_row(map_ref, c, i // 2, i % 2, p)
                    total[l % 2 * 2 + e, l // 2] += buf[k, i // 2, i % 2]

                pl.loop(0, 8)(add)

        for d in range(4):
            out_refs[d][...] = total[(x + d) % 4]
        for e in range(2):
            head_ref[e] = total[e, 0]

    return pl.pallas_call(
        kernel,
        out_shape=[jax.ShapeDtypeStruct((6, BLOCK, BLOCK), F32)] * 4
        + [jax.ShapeDtypeStruct((2, BLOCK, BLOCK), F32)],
        grid=(1,),
        in_specs=[
            pl.BlockSpec(memory_space=pltpu.SMEM),
            pl.BlockSpec((12 * BLOCK, BLOCK), lambda i: (0, 0)),
            pl.BlockSpec((96, BLOCK), lambda i: (0, 0)),
            pl.BlockSpec(memory_space=pl.ANY),
        ],
        out_specs=[pl.BlockSpec((6, BLOCK, BLOCK), lambda i: (0, 0, 0))] * 4
        + [pl.BlockSpec((2, BLOCK, BLOCK), lambda i: (0, 0, 0))],
        scratch_shapes=[
            pltpu.VMEM((4, 6, BLOCK, BLOCK), F32),
            pltpu.VMEM((4, 4, 2, BLOCK, BLOCK), F32),
            pltpu.SemaphoreType.DMA((4,)),
        ],
        compiler_params=pltpu.CompilerParams(vmem_limit_bytes=24 * MIB),
        cost_estimate=pl.CostEstimate(flops=0, bytes_accessed=5 * MIB, transcendentals=0),
        name="panel_terms",
    )(child_map, front, diagonal, arrived)


NN = ((1,), (0,))
NT = ((1,), (1,))
TN = ((0,), (0,))


def dot(a, b, contract):
    dims = (contract, ((), ()))
    return lax.dot_general(a, b, dims, precision=HIGHEST, preferred_element_type=F32)


def dot1(a, b, contract):
    return lax.dot_general(a, b, (contract, ((), ())), preferred_element_type=F32)


def split(value):
    high = value.astype(BF16)
    return high, (value - high.astype(F32)).astype(BF16)


def dot3(a, b, contract):
    (ah, al), (bh, bl) = a, b
    return dot1(ah, bl, contract) + dot1(al, bh, contract) + dot1(ah, bh, contract)


def square_iotas(size):
    shape = (size, size)
    return lax.broadcasted_iota(jnp.int32, shape, 0), lax.broadcasted_iota(jnp.int32, shape, 1)


def newton_factor(a_ref, x_ref):
    ri, ci = square_iotas(a_ref.shape[0])
    one = jnp.where(ri == ci, 1.0, 0.0)

    def lower_half(e):
        return jnp.where(ri > ci, e, jnp.where(ri == ci, 0.5 * e, 0.0))

    a = a_ref[...]
    pivots = jnp.where(ri == ci, a, 0.0)
    scale = lax.rsqrt(jnp.sum(pivots, axis=0, keepdims=True))
    f = split(jnp.where(ri > ci, a * lax.rsqrt(jnp.sum(pivots, axis=1, keepdims=True)) * scale, 0.0))
    x = (one - (f[0].astype(F32) + f[1].astype(F32)) + dot1(f[0], f[0], NN)) * scale
    xs = split(x)
    e = dot3(split(dot3(xs, split(a), NN)), xs, NT) - one
    f = split(lower_half(e))
    g = dot3(f, xs, NN)
    x = x - g + dot1(f[0], g.astype(BF16), NN)
    t = dot(x, a, NN)
    e = dot(t, x, NT) - one
    f = split(lower_half(e))
    x_ref[...] = x - dot3(f, split(x), NN)
    a_ref[...] = jnp.where(ci >= ri, t - dot3(f, split(t), NN), 0.0)
    return jnp.max(jnp.sum(jnp.abs(e), axis=1, keepdims=True))


def direct_factor(t_ref):
    size = t_ref.shape[0]
    ri, ci = square_iotas(size)
    lane = lax.broadcasted_iota(jnp.int32, (1, 2 * size), 1)
    down = lax.broadcasted_iota(jnp.int32, (size, 1), 0)

    def step(j):
        row = t_ref[pl.ds(j, 1), :]
        row = row * lax.rsqrt(jnp.sum(jnp.where(lane == j, row, 0.0), axis=1, keepdims=True))
        col = jnp.broadcast_to(row[:, :size], (size, size))
        col = jnp.sum(jnp.where(ri == ci, col, 0.0), axis=1, keepdims=True)
        t_ref[...] = t_ref[...] - jnp.where(down > j, col, 0.0) * row
        t_ref[pl.ds(j, 1), :] = row

    pl.loop(0, size)(step)


def head_factor(gathered):
    size, wide = HEAD * BLOCK, 2 * BLOCK

    def kernel(*refs):
        in_refs, (wh_ref, wl_ref, own_ref), scratch = refs[:8], refs[8:11], refs[11:]
        m_ref, u_ref, w_ref, a_ref, x_ref, t_ref = scratch
        p, q = lax.axis_index("prow"), lax.axis_index("pcol")

        def place(k, in_ref, core_back, z_back):
            core = (q + core_back) % 2
            y = (2 * (p // 4) + (q // 2) % 2 - k // 2 + 4) % 4
            z = (p - z_back + 4) % 4
            row, col = y // 2 * 4 + z, k % 2 * 4 + y % 2 * 2 + core
            rows = pl.ds(pl.multiple_of(row * BLOCK, BLOCK), BLOCK)
            cols = pl.ds(pl.multiple_of(col * BLOCK, BLOCK), BLOCK)
            m_ref[rows, cols] = in_ref[k]

        for at in range(8):
            pl.loop(0, 8)(
                functools.partial(place, in_ref=in_refs[at], core_back=at // 4, z_back=at % 4)
            )
        for i in range(HEAD):
            for j in range(i, HEAD):
                rows, cols = slice(i * BLOCK, (i + 1) * BLOCK), slice(j * BLOCK, (j + 1) * BLOCK)
                value = m_ref[cols, rows].T
                if i // 4 == j // 4:
                    value = 0.5 * (m_ref[rows, cols] + value)
                u_ref[rows, cols] = value
                if i // 2 == j // 2 and i != j:
                    u_ref[cols, rows] = value.T
        ri, ci = square_iotas(wide)
        for s in range(0, size, wide):
            e = s + wide
            a_ref[...] = u_ref[s:e, s:e]
            off = newton_factor(a_ref, x_ref)

            @pl.when(jnp.logical_not(off < 5e-4))
            def _():
                t_ref[:, :wide] = u_ref[s:e, s:e]
                t_ref[:, wide:] = jnp.where(ri == ci, 1.0, 0.0)
                direct_factor(t_ref)
                a_ref[...] = jnp.where(ci >= ri, t_ref[:, :wide], 0.0)
                x_ref[...] = jnp.where(ri >= ci, t_ref[:, wide:], 0.0)

            u_ref[s:e, s:e] = a_ref[...]
            w_ref[s:e, s:e] = x_ref[...]
            inverse = split(x_ref[...])
            if s:
                w_ref[s:e, 0:s] = dot3(inverse, split(w_ref[s:e, 0:s]), NN)
            done = split(w_ref[s:e, 0:e])
            wh_ref[s:e, 0:e], wl_ref[s:e, 0:e] = done
            if e < size:
                wh_ref[s:e, e:] = jnp.zeros((wide, size - e), BF16)
                wl_ref[s:e, e:] = jnp.zeros((wide, size - e), BF16)
                right = dot3(inverse, split(u_ref[s:e, e:]), NN)
                u_ref[s:e, e:] = right
                right = split(right)
                for j in range(e, size, wide):
                    left = tuple(v[:, j - e : j - e + wide] for v in right)
                    rest = tuple(v[:, j - e :] for v in right)
                    u_ref[j : j + wide, j:] = u_ref[j : j + wide, j:] - dot3(left, rest, TN)
                    change = dot3(left, done, TN)
                    if s:
                        w_ref[j : j + wide, 0:s] = w_ref[j : j + wide, 0:s] - change[:, 0:s]
                    w_ref[j : j + wide, s:e] = -change[:, s:e]
        own_ref[...] = jnp.zeros((BLOCK, BLOCK), F32)

        @pl.when(q <= p)
        def _():
            rows = pl.ds(pl.multiple_of(q * BLOCK, BLOCK), BLOCK)
            cols = pl.ds(pl.multiple_of(p * BLOCK, BLOCK), BLOCK)
            own_ref[...] = u_ref[rows, cols].T

    vmem = pl.BlockSpec(memory_space=pltpu.VMEM)
    square = pltpu.VMEM((size, size), F32)
    return pl.pallas_call(
        kernel,
        out_shape=[
            jax.ShapeDtypeStruct((size, size), BF16),
            jax.ShapeDtypeStruct((size, size), BF16),
            jax.ShapeDtypeStruct((BLOCK, BLOCK), F32),
        ],
        in_specs=[vmem] * 8,
        out_specs=[vmem] * 3,
        scratch_shapes=[square] * 3
        + [pltpu.VMEM((wide, wide), F32)] * 2
        + [pltpu.VMEM((wide, 2 * wide), F32)],
        compiler_params=pltpu.CompilerParams(vmem_limit_bytes=40 * MIB),
        cost_estimate=pl.CostEstimate(
            flops=20_000_000_000, bytes_accessed=8 * MIB, transcendentals=0
        ),
        name="head_factor",
    )(*gathered)


def solve_columns(col_panel, inverse):
    size, wide = HEAD * BLOCK, 6 * BLOCK

    def kernel(wh, wl, in0, in1, in2, in3, oh_ref, ol_ref, ch, cl, yh, yl):
        p, q = lax.axis_index("prow"), lax.axis_index("pcol")
        for z_back, in_ref in enumerate((in0, in1, in2, in3)):
            for y_back in range(2):
                m = (p // 4 + y_back) % 2 * 4 + (p + 4 - z_back) % 4
                cols = pl.ds(pl.multiple_of(m * BLOCK, BLOCK), BLOCK)
                for s in range(6):
                    rows = slice(s * BLOCK, (s + 1) * BLOCK)
                    ch[rows, cols], cl[rows, cols] = split(in_ref[y_back, s])
        for i in range(0, size, 256):
            e = i + 256
            y = dot3((ch[:, 0:e], cl[:, 0:e]), (wh[i:e, 0:e], wl[i:e, 0:e]), NT)
            yh[:, i:e], yl[:, i:e] = split(y)
        for i in range(0, size, 256):
            e = i + 256
            z = dot3((yh[:, i:], yl[:, i:]), (wh[i:, i:e], wl[i:, i:e]), NN)
            oh_ref[:, i:e], ol_ref[:, i:e] = split(z)

        @pl.when(q < HEAD)
        def _():
            rows = pl.ds(pl.multiple_of(q * BLOCK, BLOCK), BLOCK)
            oh_ref[0:BLOCK, :] = -wh[rows, :]
            ol_ref[0:BLOCK, :] = -wl[rows, :]

    vmem = pl.BlockSpec(memory_space=pltpu.VMEM)
    return pl.pallas_call(
        kernel,
        out_shape=[jax.ShapeDtypeStruct((wide, size), BF16)] * 2,
        in_specs=[vmem] * 6,
        out_specs=[vmem] * 2,
        scratch_shapes=[pltpu.VMEM((wide, size), BF16)] * 4,
        compiler_params=pltpu.CompilerParams(vmem_limit_bytes=32 * MIB),
        cost_estimate=pl.CostEstimate(
            flops=8_000_000_000, bytes_accessed=10 * MIB, transcendentals=0
        ),
        name="solve_columns",
    )(*inverse, *col_panel)


def finish(front, diagonal, arrived, row_panel, solved, own, child_map):
    size, group, wide = HEAD * BLOCK, 4, 6 * BLOCK

    def kernel(
        map_ref, sh, sl, own_ref, diag_ref, in0, in1, in2, in3, row_ref, front_ref, out_ref
    ):
        step = pl.program_id(0)
        p, q = lax.axis_index("prow"), lax.axis_index("pcol")
        out_ref[...] = front_ref[...]
        for s in range(6):
            l = 2 * s + jnp.where(q >= 8, 1, 0)

            @pl.when((q % 8 == p) & (l // group == step))
            def _():
                rows = pl.ds(pl.multiple_of((l % group) * BLOCK, BLOCK), BLOCK)
                out_ref[rows, s * BLOCK : (s + 1) * BLOCK] += diag_block(
                    diag_ref[pl.ds(16 * s + q, 1), :]
                )

        def add(k, in_ref, t):
            c, h, n = k // 8, (k // 2) % 4, k % 2
            l = local_row(map_ref, c, h, n, p)
            s = local_col(map_ref, c, t, q)

            @pl.when(l // group == step)
            def _():
                rows = pl.ds(pl.multiple_of((l % group) * BLOCK, BLOCK), BLOCK)
                cols = pl.ds(pl.multiple_of(s * BLOCK, BLOCK), BLOCK)
                out_ref[rows, cols] += in_ref[c, h, n]

        for d, in_ref in enumerate((in0, in1, in2, in3)):
            pl.loop(0, 16)(functools.partial(add, in_ref=in_ref, t=(q // 4 + 4 - d) % 4))

        @pl.when(q < HEAD)
        def _():
            out_ref[:, 0:BLOCK] = jnp.zeros((group * BLOCK, BLOCK), F32)

        rows = []
        for k in range(group):
            rows.append(
                jnp.concatenate([row_ref[k % 2 * 8 + m, k // 2] for m in range(HEAD)], axis=1)
            )
        rows = split(jnp.concatenate(rows, axis=0))
        for j in range(0, wide, 256):
            e = j + 256
            out_ref[:, j:e] -= dot3(rows, (sh[j:e, :], sl[j:e, :]), NT)

        @pl.when(step == 0)
        def _():
            out_ref[0:BLOCK, :] = jnp.zeros((BLOCK, wide), F32)
            out_ref[0:BLOCK, 0:BLOCK] = own_ref[...]

    def whole(*shape):
        return pl.BlockSpec(shape, lambda i: (0,) * len(shape), pipeline_mode=pl.Buffered(1))

    return pl.pallas_call(
        kernel,
        out_shape=jax.ShapeDtypeStruct((12 * BLOCK, wide), F32),
        grid=(12 // group,),
        in_specs=[
            pl.BlockSpec(memory_space=pltpu.SMEM),
            whole(wide, size),
            whole(wide, size),
            whole(BLOCK, BLOCK),
            whole(96, BLOCK),
            *[whole(2, 4, 2, BLOCK, BLOCK)] * 4,
            pl.BlockSpec((16, group // 2, BLOCK, BLOCK), lambda i: (0, i, 0, 0)),
            pl.BlockSpec((group * BLOCK, wide), lambda i: (i, 0)),
        ],
        out_specs=pl.BlockSpec((group * BLOCK, wide), lambda i: (i, 0)),
        compiler_params=pltpu.CompilerParams(vmem_limit_bytes=60 * MIB),
        cost_estimate=pl.CostEstimate(
            flops=8_000_000_000, bytes_accessed=24 * MIB, transcendentals=0
        ),
        name="finish",
    )(child_map, *solved, own, diagonal, *arrived, row_panel, front)


def ahead_x(d):
    return [(4 * x + w, 4 * ((x + d) % 4) + w) for x in range(4) for w in range(4)]


def ahead_z(d):
    return [(4 * h + z, 4 * h + (z + d) % 4) for h in range(2) for z in range(4)]


def ahead_y(d):
    def rank(y, z, x, core):
        return (4 * (y // 2) + z) * 16 + 4 * x + 2 * (y % 2) + core

    return [
        (rank(y, z, x, core), rank((y + d) % 4, z, x, core))
        for y in range(4) for z in range(4) for x in range(4) for core in range(2)
    ]


OTHER_CORE = [(k, k ^ 1) for k in range(16)]
BOTH = ("prow", "pcol")


def gather_head(terms):
    held = terms
    for d in (1, 2, 3):
        held = held + lax.ppermute(terms, "pcol", ahead_x(d))
    summed = held
    along_y = [held] + [lax.ppermute(held, BOTH, ahead_y(d)) for d in (1, 2, 3)]
    held = jnp.concatenate(along_y, axis=0)
    along_z = [held] + [lax.ppermute(held, "prow", ahead_z(d)) for d in (1, 2, 3)]
    return summed, along_z, [lax.ppermute(part, "pcol", OTHER_CORE) for part in along_z]


def gather_columns(piece):
    turned = lax.ppermute(
        piece,
        BOTH,
        [
            (p * 16 + (2 * par + e) * 4 + w, (4 * e + w) * 16 + p + 8 * par)
            for p in range(8) for par in range(2) for e in range(2) for w in range(4)
        ],
    )
    other = lax.ppermute(turned, "prow", [(p, p ^ 4) for p in range(8)])
    held = jnp.stack([turned, other], axis=0)
    return [held] + [lax.ppermute(held, "prow", ahead_z(d)) for d in (1, 2, 3)]


def per_device(front, diagonal, child, child_map):
    child_map = child_map.reshape(128)
    diagonal = diagonal.reshape(96, BLOCK)
    sent = pack_rows(child, child_map).reshape(64, BLOCK, BLOCK)
    sent = lax.all_to_all(sent, BOTH, 0, 0, axis_index_groups=PLANE_GROUPS, tiled=True)
    sent = sent.reshape(4, 2, 4, 2, BLOCK, BLOCK)
    *terms, head_terms = panel_terms(front, diagonal, sent, child_map)
    summed, along_z, twins = gather_head(head_terms)
    summed, *terms = lax.optimization_barrier([summed, *terms])
    behind = [lax.ppermute(terms[d], "pcol", ahead_x(d)) for d in (1, 2, 3)]
    *behind, last = lax.optimization_barrier([*behind, along_z[3]])
    piece = terms[0] + behind[0] + behind[1] + behind[2]
    gathered = along_z[:3] + [last] + twins
    blocks = pack_cols(sent, child_map)
    piece, *ahead = lax.optimization_barrier([piece, *blocks[1:]])
    arrived = [blocks[0]]
    for d in (1, 2, 3):
        arrived.append(lax.ppermute(ahead[d - 1], "pcol", ahead_x(d)))
    row_panel = lax.all_gather(piece, "pcol")
    col_panel = gather_columns(piece)
    *inverse, own = head_factor(gathered)
    solved = solve_columns(col_panel, inverse)
    return finish(front, diagonal, arrived, row_panel, solved, own, child_map)


def solution(mesh):
    return jax.shard_map(
        per_device,
        mesh=mesh,
        in_specs=(P("prow", "pcol"), P(), P("prow", "pcol"), P()),
        out_specs=P("prow", "pcol"),
        check_vma=False,
    )
```

```python
import functools

import jax
import jax.numpy as jnp
from jax import lax
from jax.experimental import pallas as pl
from jax.experimental.pallas import tpu as pltpu
from jax.sharding import PartitionSpec as P

BLOCK = 128
HEAD = 8
F32 = jnp.float32
BF16 = jnp.bfloat16
HIGHEST = lax.Precision.HIGHEST
MIB = 1024 * 1024

PLANE_GROUPS = [[16 * p + 4 * x + w for w in range(4) for p in range(8)] for x in range(4)]


def pack_rows(child, child_map):
    def kernel(map_ref, child_ref, out_ref, buf, turned, sems):
        c = lax.axis_index("prow") // 4
        shift = map_ref[c * 64] % 16

        def fetch(i):
            rows = pl.ds(pl.multiple_of(i * BLOCK, BLOCK), BLOCK)
            return pltpu.make_async_copy(child_ref.at[rows], buf.at[i], sems.at[0, i])

        def store(i):
            residue = (i + shift) % 16
            return pltpu.make_async_copy(
                turned.at[i], out_ref.at[:, residue % 8, residue // 8], sems.at[1, i]
            )

        def forward(i):
            fetch(i).wait()
            for w in range(4):
                b = (w - shift + 16) % 4
                turned[i, w] = buf[i, :, pl.ds(pl.multiple_of(b * BLOCK, BLOCK), BLOCK)]
            store(i).start()

        pl.loop(0, 16)(lambda i: fetch(i).start())
        pl.loop(0, 16)(forward)
        pl.loop(0, 16)(lambda i: store(i).wait())

    return pl.pallas_call(
        kernel,
        out_shape=jax.ShapeDtypeStruct((4, 8, 2, BLOCK, BLOCK), F32),
        in_specs=[pl.BlockSpec(memory_space=pltpu.SMEM), pl.BlockSpec(memory_space=pl.ANY)],
        out_specs=pl.BlockSpec(memory_space=pl.ANY),
        scratch_shapes=[
            pltpu.VMEM((16, BLOCK, 4 * BLOCK), F32),
            pltpu.VMEM((16, 4, BLOCK, BLOCK), F32),
            pltpu.SemaphoreType.DMA((2, 16)),
        ],
        compiler_params=pltpu.CompilerParams(vmem_limit_bytes=16 * MIB),
        cost_estimate=pl.CostEstimate(flops=0, bytes_accessed=8 * MIB, transcendentals=0),
        name="pack_rows",
    )(child_map, child)


def pack_cols(arrived, child_map):
    def kernel(map_ref, in_ref, *refs):
        out_refs, (buf, sems) = refs[:4], refs[4:]
        q = lax.axis_index("pcol")
        x, w = q // 4, q % 4

        def fetch(k):
            d, c = k // 2, k % 2
            column = 4 * ((x + d) % 4) + w
            a = ((column - map_ref[c * 64] % 16 + 16) % 16) // 4
            return pltpu.make_async_copy(in_ref.at[a, c], buf.at[k], sems.at[0, k])

        def store(k):
            return pltpu.make_async_copy(buf.at[k], out_refs[k // 2].at[k % 2], sems.at[1, k])

        for k in range(8):
            fetch(k).start()
        for k in range(8):
            fetch(k).wait()
            store(k).start()
        for k in range(8):
            store(k).wait()

    return pl.pallas_call(
        kernel,
        out_shape=[jax.ShapeDtypeStruct((2, 4, 2, BLOCK, BLOCK), F32)] * 4,
        in_specs=[pl.BlockSpec(memory_space=pltpu.SMEM), pl.BlockSpec(memory_space=pl.ANY)],
        out_specs=[pl.BlockSpec(memory_space=pl.ANY)] * 4,
        scratch_shapes=[
            pltpu.VMEM((8, 4, 2, BLOCK, BLOCK), F32), pltpu.SemaphoreType.DMA((2, 8))
        ],
        compiler_params=pltpu.CompilerParams(vmem_limit_bytes=16 * MIB),
        cost_estimate=pl.CostEstimate(flops=0, bytes_accessed=8 * MIB, transcendentals=0),
        name="pack_cols",
    )(child_map, arrived)


def diag_block(values):
    rows = lax.broadcasted_iota(jnp.int32, (BLOCK, BLOCK), 0)
    cols = lax.broadcasted_iota(jnp.int32, (BLOCK, BLOCK), 1)
    return jnp.where(rows == cols, jnp.broadcast_to(values, (BLOCK, BLOCK)), 0.0)


def local_row(map_ref, c, h, n, p):
    shift = map_ref[c * 64] % 16
    i = (p + 8 * n - shift + 16) % 16
    return map_ref[c * 64 + 16 * h + i] // 8


def local_col(map_ref, c, t, q):
    shift = map_ref[c * 64] % 16
    return map_ref[c * 64 + 16 * t + (q - shift + 16) % 16] // 16


def panel_terms(front, diagonal, arrived, child_map):
    def kernel(map_ref, front_ref, diag_ref, in_ref, *refs):
        out_refs, head_ref, (total, buf, sems) = refs[:4], refs[4], refs[5:]
        p, q = lax.axis_index("prow"), lax.axis_index("pcol")
        x, w = q // 4, q % 4
        chosen, copies = [], []
        for e in range(2):
            for c in range(2):
                at = (4 * e + w - map_ref[c * 64] % 16 + 16) % 16
                chosen.append(map_ref[c * 64 + 16 * x + at] // 16 == 0)
                copies.append(
                    pltpu.make_async_copy(
                        in_ref.at[at // 4, c], buf.at[2 * e + c], sems.at[2 * e + c]
                    )
                )
                copies[-1].start()
        total[...] = jnp.zeros_like(total)

        @pl.when(x < 2)
        def _():
            for l in range(12):
                total[l % 2 * 2 + x, l // 2] = front_ref[l * BLOCK : (l + 1) * BLOCK, :]

        @pl.when(p == q)
        def _():
            total[x, 0] += diag_block(diag_ref[pl.ds(q, 1), :])

        for k in range(4):
            e, c = k // 2, k % 2
            copies[k].wait()

            @pl.when(chosen[k])
            def _():
                def add(i):
                    l = local_row(map_ref, c, i // 2, i % 2, p)
                    total[l % 2 * 2 + e, l // 2] += buf[k, i // 2, i % 2]

                pl.loop(0, 8)(add)

        for d in range(4):
            out_refs[d][...] = total[(x + d) % 4]
        for e in range(2):
            head_ref[e] = total[e, 0]

    return pl.pallas_call(
        kernel,
        out_shape=[jax.ShapeDtypeStruct((6, BLOCK, BLOCK), F32)] * 4
        + [jax.ShapeDtypeStruct((2, BLOCK, BLOCK), F32)],
        grid=(1,),
        in_specs=[
            pl.BlockSpec(memory_space=pltpu.SMEM),
            pl.BlockSpec((12 * BLOCK, BLOCK), lambda i: (0, 0)),
            pl.BlockSpec((96, BLOCK), lambda i: (0, 0)),
            pl.BlockSpec(memory_space=pl.ANY),
        ],
        out_specs=[pl.BlockSpec((6, BLOCK, BLOCK), lambda i: (0, 0, 0))] * 4
        + [pl.BlockSpec((2, BLOCK, BLOCK), lambda i: (0, 0, 0))],
        scratch_shapes=[
            pltpu.VMEM((4, 6, BLOCK, BLOCK), F32),
            pltpu.VMEM((4, 4, 2, BLOCK, BLOCK), F32),
            pltpu.SemaphoreType.DMA((4,)),
        ],
        compiler_params=pltpu.CompilerParams(vmem_limit_bytes=24 * MIB),
        cost_estimate=pl.CostEstimate(flops=0, bytes_accessed=5 * MIB, transcendentals=0),
        name="panel_terms",
    )(child_map, front, diagonal, arrived)


NN = ((1,), (0,))
NT = ((1,), (1,))
TN = ((0,), (0,))


def dot(a, b, contract):
    dims = (contract, ((), ()))
    return lax.dot_general(a, b, dims, precision=HIGHEST, preferred_element_type=F32)


def dot1(a, b, contract):
    return lax.dot_general(a, b, (contract, ((), ())), preferred_element_type=F32)


def split(value):
    high = value.astype(BF16)
    return high, (value - high.astype(F32)).astype(BF16)


def dot3(a, b, contract):
    (ah, al), (bh, bl) = a, b
    return dot1(ah, bl, contract) + dot1(al, bh, contract) + dot1(ah, bh, contract)


def square_iotas(size):
    shape = (size, size)
    return lax.broadcasted_iota(jnp.int32, shape, 0), lax.broadcasted_iota(jnp.int32, shape, 1)


def newton_factor(a_ref, x_ref):
    ri, ci = square_iotas(a_ref.shape[0])
    one = jnp.where(ri == ci, 1.0, 0.0)

    def lower_half(e):
        return jnp.where(ri > ci, e, jnp.where(ri == ci, 0.5 * e, 0.0))

    a = a_ref[...]
    pivots = jnp.where(ri == ci, a, 0.0)
    scale = lax.rsqrt(jnp.sum(pivots, axis=0, keepdims=True))
    f = split(jnp.where(ri > ci, a * lax.rsqrt(jnp.sum(pivots, axis=1, keepdims=True)) * scale, 0.0))
    x = (one - (f[0].astype(F32) + f[1].astype(F32)) + dot1(f[0], f[0], NN)) * scale
    xs = split(x)
    e = dot3(split(dot3(xs, split(a), NN)), xs, NT) - one
    f = split(lower_half(e))
    g = dot3(f, xs, NN)
    x = x - g + dot1(f[0], g.astype(BF16), NN)
    t = dot(x, a, NN)
    e = dot(t, x, NT) - one
    f = split(lower_half(e))
    x_ref[...] = x - dot3(f, split(x), NN)
    a_ref[...] = jnp.where(ci >= ri, t - dot3(f, split(t), NN), 0.0)
    return jnp.max(jnp.sum(jnp.abs(e), axis=1, keepdims=True))


def direct_factor(t_ref):
    size = t_ref.shape[0]
    ri, ci = square_iotas(size)
    lane = lax.broadcasted_iota(jnp.int32, (1, 2 * size), 1)
    down = lax.broadcasted_iota(jnp.int32, (size, 1), 0)

    def step(j):
        row = t_ref[pl.ds(j, 1), :]
        row = row * lax.rsqrt(jnp.sum(jnp.where(lane == j, row, 0.0), axis=1, keepdims=True))
        col = jnp.broadcast_to(row[:, :size], (size, size))
        col = jnp.sum(jnp.where(ri == ci, col, 0.0), axis=1, keepdims=True)
        t_ref[...] = t_ref[...] - jnp.where(down > j, col, 0.0) * row
        t_ref[pl.ds(j, 1), :] = row

    pl.loop(0, size)(step)


def head_factor(gathered):
    size, wide = HEAD * BLOCK, 2 * BLOCK

    def kernel(*refs):
        in_refs, (wh_ref, wl_ref, own_ref), scratch = refs[:8], refs[8:11], refs[11:]
        m_ref, u_ref, w_ref, a_ref, x_ref, t_ref = scratch
        p, q = lax.axis_index("prow"), lax.axis_index("pcol")

        def place(k, in_ref, core_back, z_back):
            core = (q + core_back) % 2
            y = (2 * (p // 4) + (q // 2) % 2 - k // 2 + 4) % 4
            z = (p - z_back + 4) % 4
            row, col = y // 2 * 4 + z, k % 2 * 4 + y % 2 * 2 + core
            rows = pl.ds(pl.multiple_of(row * BLOCK, BLOCK), BLOCK)
            cols = pl.ds(pl.multiple_of(col * BLOCK, BLOCK), BLOCK)
            m_ref[rows, cols] = in_ref[k]

        for at in range(8):
            pl.loop(0, 8)(
                functools.partial(place, in_ref=in_refs[at], core_back=at // 4, z_back=at % 4)
            )
        for i in range(HEAD):
            for j in range(i, HEAD):
                rows, cols = slice(i * BLOCK, (i + 1) * BLOCK), slice(j * BLOCK, (j + 1) * BLOCK)
                value = m_ref[cols, rows].T
                if i // 4 == j // 4:
                    value = 0.5 * (m_ref[rows, cols] + value)
                u_ref[rows, cols] = value
                if i // 2 == j // 2 and i != j:
                    u_ref[cols, rows] = value.T
        ri, ci = square_iotas(wide)
        for s in range(0, size, wide):
            e = s + wide
            a_ref[...] = u_ref[s:e, s:e]
            off = newton_factor(a_ref, x_ref)

            @pl.when(jnp.logical_not(off < 5e-4))
            def _():
                t_ref[:, :wide] = u_ref[s:e, s:e]
                t_ref[:, wide:] = jnp.where(ri == ci, 1.0, 0.0)
                direct_factor(t_ref)
                a_ref[...] = jnp.where(ci >= ri, t_ref[:, :wide], 0.0)
                x_ref[...] = jnp.where(ri >= ci, t_ref[:, wide:], 0.0)

            u_ref[s:e, s:e] = a_ref[...]
            w_ref[s:e, s:e] = x_ref[...]
            inverse = split(x_ref[...])
            if s:
                w_ref[s:e, 0:s] = dot3(inverse, split(w_ref[s:e, 0:s]), NN)
            done = split(w_ref[s:e, 0:e])
            wh_ref[s:e, 0:e], wl_ref[s:e, 0:e] = done
            if e < size:
                wh_ref[s:e, e:] = jnp.zeros((wide, size - e), BF16)
                wl_ref[s:e, e:] = jnp.zeros((wide, size - e), BF16)
                right = dot3(inverse, split(u_ref[s:e, e:]), NN)
                u_ref[s:e, e:] = right
                right = split(right)
                for j in range(e, size, wide):
                    left = tuple(v[:, j - e : j - e + wide] for v in right)
                    rest = tuple(v[:, j - e :] for v in right)
                    u_ref[j : j + wide, j:] = u_ref[j : j + wide, j:] - dot3(left, rest, TN)
                    change = dot3(left, done, TN)
                    if s:
                        w_ref[j : j + wide, 0:s] = w_ref[j : j + wide, 0:s] - change[:, 0:s]
                    w_ref[j : j + wide, s:e] = -change[:, s:e]
        own_ref[...] = jnp.zeros((BLOCK, BLOCK), F32)

        @pl.when(q <= p)
        def _():
            rows = pl.ds(pl.multiple_of(q * BLOCK, BLOCK), BLOCK)
            cols = pl.ds(pl.multiple_of(p * BLOCK, BLOCK), BLOCK)
            own_ref[...] = u_ref[rows, cols].T

    vmem = pl.BlockSpec(memory_space=pltpu.VMEM)
    square = pltpu.VMEM((size, size), F32)
    return pl.pallas_call(
        kernel,
        out_shape=[
            jax.ShapeDtypeStruct((size, size), BF16),
            jax.ShapeDtypeStruct((size, size), BF16),
            jax.ShapeDtypeStruct((BLOCK, BLOCK), F32),
        ],
        in_specs=[vmem] * 8,
        out_specs=[vmem] * 3,
        scratch_shapes=[square] * 3
        + [pltpu.VMEM((wide, wide), F32)] * 2
        + [pltpu.VMEM((wide, 2 * wide), F32)],
        compiler_params=pltpu.CompilerParams(vmem_limit_bytes=40 * MIB),
        cost_estimate=pl.CostEstimate(
            flops=20_000_000_000, bytes_accessed=8 * MIB, transcendentals=0
        ),
        name="head_factor",
    )(*gathered)


def solve_columns(col_panel, inverse):
    size, wide = HEAD * BLOCK, 6 * BLOCK

    def kernel(wh, wl, in0, in1, in2, in3, oh_ref, ol_ref, ch, cl, yh, yl):
        p, q = lax.axis_index("prow"), lax.axis_index("pcol")
        for z_back, in_ref in enumerate((in0, in1, in2, in3)):
            for y_back in range(2):
                m = (p // 4 + y_back) % 2 * 4 + (p + 4 - z_back) % 4
                cols = pl.ds(pl.multiple_of(m * BLOCK, BLOCK), BLOCK)
                for s in range(6):
                    rows = slice(s * BLOCK, (s + 1) * BLOCK)
                    ch[rows, cols], cl[rows, cols] = split(in_ref[y_back, s])
        for i in range(0, size, 256):
            e = i + 256
            y = dot3((ch[:, 0:e], cl[:, 0:e]), (wh[i:e, 0:e], wl[i:e, 0:e]), NT)
            yh[:, i:e], yl[:, i:e] = split(y)
        for i in range(0, size, 256):
            e = i + 256
            z = dot3((yh[:, i:], yl[:, i:]), (wh[i:, i:e], wl[i:, i:e]), NN)
            oh_ref[:, i:e], ol_ref[:, i:e] = split(z)

        @pl.when(q < HEAD)
        def _():
            rows = pl.ds(pl.multiple_of(q * BLOCK, BLOCK), BLOCK)
            oh_ref[0:BLOCK, :] = -wh[rows, :]
            ol_ref[0:BLOCK, :] = -wl[rows, :]

    vmem = pl.BlockSpec(memory_space=pltpu.VMEM)
    return pl.pallas_call(
        kernel,
        out_shape=[jax.ShapeDtypeStruct((wide, size), BF16)] * 2,
        in_specs=[vmem] * 6,
        out_specs=[vmem] * 2,
        scratch_shapes=[pltpu.VMEM((wide, size), BF16)] * 4,
        compiler_params=pltpu.CompilerParams(vmem_limit_bytes=32 * MIB),
        cost_estimate=pl.CostEstimate(
            flops=8_000_000_000, bytes_accessed=10 * MIB, transcendentals=0
        ),
        name="solve_columns",
    )(*inverse, *col_panel)


def finish(front, diagonal, arrived, row_panel, solved, own, child_map):
    size, group, wide = HEAD * BLOCK, 4, 6 * BLOCK

    def kernel(
        map_ref, sh, sl, own_ref, diag_ref, in0, in1, in2, in3, row_ref, front_ref, out_ref
    ):
        step = pl.program_id(0)
        p, q = lax.axis_index("prow"), lax.axis_index("pcol")
        out_ref[...] = front_ref[...]
        for s in range(6):
            l = 2 * s + jnp.where(q >= 8, 1, 0)

            @pl.when((q % 8 == p) & (l // group == step))
            def _():
                rows = pl.ds(pl.multiple_of((l % group) * BLOCK, BLOCK), BLOCK)
                out_ref[rows, s * BLOCK : (s + 1) * BLOCK] += diag_block(
                    diag_ref[pl.ds(16 * s + q, 1), :]
                )

        in_refs = (in0, in1, in2, in3)
        for c in range(2):
            places = [local_col(map_ref, c, (q // 4 + 4 - d) % 4, q) for d in range(4)]

            def add(k):
                l = local_row(map_ref, c, k // 2, k % 2, p)

                @pl.when(l // group == step)
                def _():
                    rows = pl.ds(pl.multiple_of((l % group) * BLOCK, BLOCK), BLOCK)
                    for d in range(4):
                        cols = pl.ds(pl.multiple_of(places[d] * BLOCK, BLOCK), BLOCK)
                        out_ref[rows, cols] += in_refs[d][c, k // 2, k % 2]

            pl.loop(0, 8)(add)

        @pl.when(q < HEAD)
        def _():
            out_ref[:, 0:BLOCK] = jnp.zeros((group * BLOCK, BLOCK), F32)

        rows = []
        for k in range(group):
            rows.append(
                jnp.concatenate([row_ref[k % 2 * 8 + m, k // 2] for m in range(HEAD)], axis=1)
            )
        rows = split(jnp.concatenate(rows, axis=0))
        for j in range(0, wide, 256):
            e = j + 256
            out_ref[:, j:e] -= dot3(rows, (sh[j:e, :], sl[j:e, :]), NT)

        @pl.when(step == 0)
        def _():
            out_ref[0:BLOCK, :] = jnp.zeros((BLOCK, wide), F32)
            out_ref[0:BLOCK, 0:BLOCK] = own_ref[...]

    def whole(*shape):
        return pl.BlockSpec(shape, lambda i: (0,) * len(shape), pipeline_mode=pl.Buffered(1))

    return pl.pallas_call(
        kernel,
        out_shape=jax.ShapeDtypeStruct((12 * BLOCK, wide), F32),
        grid=(12 // group,),
        in_specs=[
            pl.BlockSpec(memory_space=pltpu.SMEM),
            whole(wide, size),
            whole(wide, size),
            whole(BLOCK, BLOCK),
            whole(96, BLOCK),
            *[whole(2, 4, 2, BLOCK, BLOCK)] * 4,
            pl.BlockSpec((16, group // 2, BLOCK, BLOCK), lambda i: (0, i, 0, 0)),
            pl.BlockSpec((group * BLOCK, wide), lambda i: (i, 0)),
        ],
        out_specs=pl.BlockSpec((group * BLOCK, wide), lambda i: (i, 0)),
        compiler_params=pltpu.CompilerParams(vmem_limit_bytes=60 * MIB),
        cost_estimate=pl.CostEstimate(
            flops=8_000_000_000, bytes_accessed=24 * MIB, transcendentals=0
        ),
        name="finish",
    )(child_map, *solved, own, diagonal, *arrived, row_panel, front)


def ahead_x(d):
    return [(4 * x + w, 4 * ((x + d) % 4) + w) for x in range(4) for w in range(4)]


def ahead_z(d):
    return [(4 * h + z, 4 * h + (z + d) % 4) for h in range(2) for z in range(4)]


def ahead_y(d):
    def rank(y, z, x, core):
        return (4 * (y // 2) + z) * 16 + 4 * x + 2 * (y % 2) + core

    return [
        (rank(y, z, x, core), rank((y + d) % 4, z, x, core))
        for y in range(4) for z in range(4) for x in range(4) for core in range(2)
    ]


OTHER_CORE = [(k, k ^ 1) for k in range(16)]
BOTH = ("prow", "pcol")


def gather_head(terms):
    held = terms
    for d in (1, 2, 3):
        held = held + lax.ppermute(terms, "pcol", ahead_x(d))
    summed = held
    along_y = [held] + [lax.ppermute(held, BOTH, ahead_y(d)) for d in (1, 2, 3)]
    held = jnp.concatenate(along_y, axis=0)
    along_z = [held] + [lax.ppermute(held, "prow", ahead_z(d)) for d in (1, 2, 3)]
    return summed, along_z, [lax.ppermute(part, "pcol", OTHER_CORE) for part in along_z]


def gather_columns(piece):
    turned = lax.ppermute(
        piece,
        BOTH,
        [
            (p * 16 + (2 * par + e) * 4 + w, (4 * e + w) * 16 + p + 8 * par)
            for p in range(8) for par in range(2) for e in range(2) for w in range(4)
        ],
    )
    other = lax.ppermute(turned, "prow", [(p, p ^ 4) for p in range(8)])
    held = jnp.stack([turned, other], axis=0)
    return [held] + [lax.ppermute(held, "prow", ahead_z(d)) for d in (1, 2, 3)]


def per_device(front, diagonal, child, child_map):
    child_map = child_map.reshape(128)
    diagonal = diagonal.reshape(96, BLOCK)
    sent = pack_rows(child, child_map).reshape(64, BLOCK, BLOCK)
    sent = lax.all_to_all(sent, BOTH, 0, 0, axis_index_groups=PLANE_GROUPS, tiled=True)
    sent = sent.reshape(4, 2, 4, 2, BLOCK, BLOCK)
    *terms, head_terms = panel_terms(front, diagonal, sent, child_map)
    summed, along_z, twins = gather_head(head_terms)
    summed, *terms = lax.optimization_barrier([summed, *terms])
    behind = [lax.ppermute(terms[d], "pcol", ahead_x(d)) for d in (1, 2, 3)]
    behind, along_z = lax.optimization_barrier((behind, along_z))
    piece = terms[0] + behind[0] + behind[1] + behind[2]
    gathered = along_z + twins
    blocks = pack_cols(sent, child_map)
    piece, *ahead = lax.optimization_barrier([piece, *blocks[1:]])
    arrived = [blocks[0]]
    for d in (1, 2, 3):
        arrived.append(lax.ppermute(ahead[d - 1], "pcol", ahead_x(d)))
    row_panel = lax.all_gather(piece, "pcol")
    col_panel = gather_columns(piece)
    *inverse, own = head_factor(gathered)
    solved = solve_columns(col_panel, inverse)
    return finish(front, diagonal, arrived, row_panel, solved, own, child_map)


def solution(mesh):
    return jax.shard_map(
        per_device,
        mesh=mesh,
        in_specs=(P("prow", "pcol"), P(), P("prow", "pcol"), P()),
        out_specs=P("prow", "pcol"),
        check_vma=False,
    )
```

```python
import functools

import jax
import jax.numpy as jnp
from jax import lax
from jax.experimental import pallas as pl
from jax.experimental.pallas import tpu as pltpu
from jax.sharding import PartitionSpec as P

BLOCK = 128
HEAD = 8
F32 = jnp.float32
BF16 = jnp.bfloat16
HIGHEST = lax.Precision.HIGHEST
MIB = 1024 * 1024

PLANE_GROUPS = [[16 * p + 4 * x + w for w in range(4) for p in range(8)] for x in range(4)]


def pack_rows(child, child_map):
    def kernel(map_ref, child_ref, even_ref, odd_ref, buf, turned, sems):
        c = lax.axis_index("prow") // 4
        shift = map_ref[c * 64] % 16

        def fetch(k):
            i = (k - shift + 16) % 16
            rows = pl.ds(pl.multiple_of(i * BLOCK, BLOCK), BLOCK)
            return pltpu.make_async_copy(child_ref.at[rows], buf.at[k], sems.at[0, k])

        def store(k, out_ref):
            return pltpu.make_async_copy(turned.at[k], out_ref.at[:, k % 8], sems.at[1, k])

        def forward(k, out_ref):
            fetch(k).wait()
            for w in range(4):
                b = (w - shift + 16) % 4
                turned[k, w] = buf[k, :, pl.ds(pl.multiple_of(b * BLOCK, BLOCK), BLOCK)]
            store(k, out_ref).start()

        pl.loop(0, 16)(lambda k: fetch(k).start())
        pl.loop(0, 8)(lambda k: forward(k, even_ref))
        pl.loop(8, 16)(lambda k: forward(k, odd_ref))
        pl.loop(0, 8)(lambda k: store(k, even_ref).wait())
        pl.loop(8, 16)(lambda k: store(k, odd_ref).wait())

    return pl.pallas_call(
        kernel,
        out_shape=[jax.ShapeDtypeStruct((4, 8, BLOCK, BLOCK), F32)] * 2,
        in_specs=[pl.BlockSpec(memory_space=pltpu.SMEM), pl.BlockSpec(memory_space=pl.ANY)],
        out_specs=[pl.BlockSpec(memory_space=pl.ANY)] * 2,
        scratch_shapes=[
            pltpu.VMEM((16, BLOCK, 4 * BLOCK), F32),
            pltpu.VMEM((16, 4, BLOCK, BLOCK), F32),
            pltpu.SemaphoreType.DMA((2, 16)),
        ],
        compiler_params=pltpu.CompilerParams(vmem_limit_bytes=16 * MIB),
        cost_estimate=pl.CostEstimate(flops=1, bytes_accessed=1, transcendentals=0),
        name="pack_rows",
    )(child_map, child)


def pack_cols(arrived, child_map):
    def kernel(map_ref, in_ref, *refs):
        out_refs, (buf, sems) = refs[:4], refs[4:]
        q = lax.axis_index("pcol")
        x, w = q // 4, q % 4

        def fetch(k):
            d, c = k // 2, k % 2
            column = 4 * ((x + d) % 4) + w
            a = ((column - map_ref[c * 64] % 16 + 16) % 16) // 4
            return pltpu.make_async_copy(in_ref.at[a, c], buf.at[k], sems.at[0, k])

        def store(k):
            return pltpu.make_async_copy(buf.at[k], out_refs[k // 2].at[k % 2], sems.at[1, k])

        for k in range(8):
            fetch(k).start()
        for k in range(8):
            fetch(k).wait()
            store(k).start()
        for k in range(8):
            store(k).wait()

    return pl.pallas_call(
        kernel,
        out_shape=[jax.ShapeDtypeStruct((2, 4, BLOCK, BLOCK), F32)] * 4,
        in_specs=[pl.BlockSpec(memory_space=pltpu.SMEM), pl.BlockSpec(memory_space=pl.ANY)],
        out_specs=[pl.BlockSpec(memory_space=pl.ANY)] * 4,
        scratch_shapes=[
            pltpu.VMEM((8, 4, BLOCK, BLOCK), F32), pltpu.SemaphoreType.DMA((2, 8))
        ],
        compiler_params=pltpu.CompilerParams(vmem_limit_bytes=16 * MIB),
        cost_estimate=pl.CostEstimate(flops=1, bytes_accessed=1, transcendentals=0),
        name="pack_cols",
    )(child_map, arrived)


def diag_block(values):
    rows = lax.broadcasted_iota(jnp.int32, (BLOCK, BLOCK), 0)
    cols = lax.broadcasted_iota(jnp.int32, (BLOCK, BLOCK), 1)
    return jnp.where(rows == cols, jnp.broadcast_to(values, (BLOCK, BLOCK)), 0.0)


def local_row(map_ref, c, h, n, p):
    shift = map_ref[c * 64] % 16
    i = (p + 8 * n - shift + 16) % 16
    return map_ref[c * 64 + 16 * h + i] // 8


def local_col(map_ref, c, t, q):
    shift = map_ref[c * 64] % 16
    return map_ref[c * 64 + 16 * t + (q - shift + 16) % 16] // 16


def panel_terms(front, diagonal, arrived, child_map, n):
    def kernel(map_ref, front_ref, diag_ref, in_ref, *refs):
        out_refs, head_ref, (total, buf, sems) = refs[:4], refs[4], refs[5:]
        p, q = lax.axis_index("prow"), lax.axis_index("pcol")
        x, w = q // 4, q % 4
        chosen, copies = [], []
        for e in range(2):
            for c in range(2):
                at = (4 * e + w - map_ref[c * 64] % 16 + 16) % 16
                chosen.append(map_ref[c * 64 + 16 * x + at] // 16 == 0)
                copies.append(
                    pltpu.make_async_copy(
                        in_ref.at[at // 4, c], buf.at[2 * e + c], sems.at[2 * e + c]
                    )
                )
                copies[-1].start()
        total[...] = jnp.zeros_like(total)

        @pl.when(x < 2)
        def _():
            for l in range(6):
                at = (2 * l + n) * BLOCK
                total[x, l] = front_ref[at : at + BLOCK, :]

        if n == 0:

            @pl.when(p == q)
            def _():
                total[x, 0] += diag_block(diag_ref[pl.ds(q, 1), :])

        for k in range(4):
            e, c = k // 2, k % 2
            copies[k].wait()

            @pl.when(chosen[k])
            def _():
                def add(h):
                    total[e, local_row(map_ref, c, h, n, p) // 2] += buf[k, h]

                pl.loop(0, 4)(add)

        for d in range(4):
            out_refs[d][...] = total[(x + d) % 2]
        for e in range(2):
            head_ref[e] = total[e, 0]

    return pl.pallas_call(
        kernel,
        out_shape=[jax.ShapeDtypeStruct((6, BLOCK, BLOCK), F32)] * 4
        + [jax.ShapeDtypeStruct((2, BLOCK, BLOCK), F32)],
        grid=(1,),
        in_specs=[
            pl.BlockSpec(memory_space=pltpu.SMEM),
            pl.BlockSpec((12 * BLOCK, BLOCK), lambda i: (0, 0)),
            pl.BlockSpec((96, BLOCK), lambda i: (0, 0)),
            pl.BlockSpec(memory_space=pl.ANY),
        ],
        out_specs=[pl.BlockSpec((6, BLOCK, BLOCK), lambda i: (0, 0, 0))] * 4
        + [pl.BlockSpec((2, BLOCK, BLOCK), lambda i: (0, 0, 0))],
        scratch_shapes=[
            pltpu.VMEM((2, 6, BLOCK, BLOCK), F32),
            pltpu.VMEM((4, 4, BLOCK, BLOCK), F32),
            pltpu.SemaphoreType.DMA((4,)),
        ],
        compiler_params=pltpu.CompilerParams(vmem_limit_bytes=24 * MIB),
        cost_estimate=pl.CostEstimate(flops=1, bytes_accessed=1, transcendentals=0),
        name="panel_terms",
    )(child_map, front, diagonal, arrived)


NN = ((1,), (0,))
NT = ((1,), (1,))
TN = ((0,), (0,))


def dot(a, b, contract):
    dims = (contract, ((), ()))
    return lax.dot_general(a, b, dims, precision=HIGHEST, preferred_element_type=F32)


def dot1(a, b, contract):
    return lax.dot_general(a, b, (contract, ((), ())), preferred_element_type=F32)


def split(value):
    high = value.astype(BF16)
    return high, (value - high.astype(F32)).astype(BF16)


def dot3(a, b, contract):
    (ah, al), (bh, bl) = a, b
    return dot1(ah, bl, contract) + dot1(al, bh, contract) + dot1(ah, bh, contract)


def square_iotas(size):
    shape = (size, size)
    return lax.broadcasted_iota(jnp.int32, shape, 0), lax.broadcasted_iota(jnp.int32, shape, 1)


def newton_factor(a_ref, x_ref):
    ri, ci = square_iotas(a_ref.shape[0])
    one = jnp.where(ri == ci, 1.0, 0.0)

    def lower_half(e):
        return jnp.where(ri > ci, e, jnp.where(ri == ci, 0.5 * e, 0.0))

    a = a_ref[...]
    pivots = jnp.where(ri == ci, a, 0.0)
    scale = lax.rsqrt(jnp.sum(pivots, axis=0, keepdims=True))
    f = split(jnp.where(ri > ci, a * lax.rsqrt(jnp.sum(pivots, axis=1, keepdims=True)) * scale, 0.0))
    x = (one - (f[0].astype(F32) + f[1].astype(F32)) + dot1(f[0], f[0], NN)) * scale
    xs = split(x)
    e = dot3(split(dot3(xs, split(a), NN)), xs, NT) - one
    f = split(lower_half(e))
    g = dot3(f, xs, NN)
    x = x - g + dot1(f[0], g.astype(BF16), NN)
    t = dot(x, a, NN)
    e = dot(t, x, NT) - one
    f = split(lower_half(e))
    x_ref[...] = x - dot3(f, split(x), NN)
    a_ref[...] = jnp.where(ci >= ri, t - dot3(f, split(t), NN), 0.0)
    return jnp.max(jnp.sum(jnp.abs(e), axis=1, keepdims=True))


def direct_factor(t_ref):
    size = t_ref.shape[0]
    ri, ci = square_iotas(size)
    lane = lax.broadcasted_iota(jnp.int32, (1, 2 * size), 1)
    down = lax.broadcasted_iota(jnp.int32, (size, 1), 0)

    def step(j):
        row = t_ref[pl.ds(j, 1), :]
        row = row * lax.rsqrt(jnp.sum(jnp.where(lane == j, row, 0.0), axis=1, keepdims=True))
        col = jnp.broadcast_to(row[:, :size], (size, size))
        col = jnp.sum(jnp.where(ri == ci, col, 0.0), axis=1, keepdims=True)
        t_ref[...] = t_ref[...] - jnp.where(down > j, col, 0.0) * row
        t_ref[pl.ds(j, 1), :] = row

    pl.loop(0, size)(step)


def head_factor(gathered):
    size, wide = HEAD * BLOCK, 2 * BLOCK

    def kernel(*refs):
        in_refs, (wh_ref, wl_ref, own_ref), scratch = refs[:8], refs[8:11], refs[11:]
        m_ref, u_ref, w_ref, a_ref, x_ref, t_ref = scratch
        p, q = lax.axis_index("prow"), lax.axis_index("pcol")

        def place(k, in_ref, core_back, z_back):
            core = (q + core_back) % 2
            y = (2 * (p // 4) + (q // 2) % 2 - k // 2 + 4) % 4
            z = (p - z_back + 4) % 4
            row, col = y // 2 * 4 + z, k % 2 * 4 + y % 2 * 2 + core
            rows = pl.ds(pl.multiple_of(row * BLOCK, BLOCK), BLOCK)
            cols = pl.ds(pl.multiple_of(col * BLOCK, BLOCK), BLOCK)
            m_ref[rows, cols] = in_ref[k]

        for at in range(8):
            pl.loop(0, 8)(
                functools.partial(place, in_ref=in_refs[at], core_back=at // 4, z_back=at % 4)
            )
        for i in range(HEAD):
            for j in range(i, HEAD):
                rows, cols = slice(i * BLOCK, (i + 1) * BLOCK), slice(j * BLOCK, (j + 1) * BLOCK)
                value = m_ref[cols, rows].T
                if i // 4 == j // 4:
                    value = 0.5 * (m_ref[rows, cols] + value)
                u_ref[rows, cols] = value
                if i // 2 == j // 2 and i != j:
                    u_ref[cols, rows] = value.T
        ri, ci = square_iotas(wide)
        for s in range(0, size, wide):
            e = s + wide
            a_ref[...] = u_ref[s:e, s:e]
            off = newton_factor(a_ref, x_ref)

            @pl.when(jnp.logical_not(off < 5e-4))
            def _():
                t_ref[:, :wide] = u_ref[s:e, s:e]
                t_ref[:, wide:] = jnp.where(ri == ci, 1.0, 0.0)
                direct_factor(t_ref)
                a_ref[...] = jnp.where(ci >= ri, t_ref[:, :wide], 0.0)
                x_ref[...] = jnp.where(ri >= ci, t_ref[:, wide:], 0.0)

            u_ref[s:e, s:e] = a_ref[...]
            w_ref[s:e, s:e] = x_ref[...]
            inverse = split(x_ref[...])
            if s:
                w_ref[s:e, 0:s] = dot3(inverse, split(w_ref[s:e, 0:s]), NN)
            done = split(w_ref[s:e, 0:e])
            wh_ref[s:e, 0:e], wl_ref[s:e, 0:e] = done
            if e < size:
                wh_ref[s:e, e:] = jnp.zeros((wide, size - e), BF16)
                wl_ref[s:e, e:] = jnp.zeros((wide, size - e), BF16)
                right = dot3(inverse, split(u_ref[s:e, e:]), NN)
                u_ref[s:e, e:] = right
                right = split(right)
                for j in range(e, size, wide):
                    left = tuple(v[:, j - e : j - e + wide] for v in right)
                    rest = tuple(v[:, j - e :] for v in right)
                    u_ref[j : j + wide, j:] = u_ref[j : j + wide, j:] - dot3(left, rest, TN)
                    change = dot3(left, done, TN)
                    if s:
                        w_ref[j : j + wide, 0:s] = w_ref[j : j + wide, 0:s] - change[:, 0:s]
                    w_ref[j : j + wide, s:e] = -change[:, s:e]
        own_ref[...] = jnp.zeros((BLOCK, BLOCK), F32)

        @pl.when(q <= p)
        def _():
            rows = pl.ds(pl.multiple_of(q * BLOCK, BLOCK), BLOCK)
            cols = pl.ds(pl.multiple_of(p * BLOCK, BLOCK), BLOCK)
            own_ref[...] = u_ref[rows, cols].T

    vmem = pl.BlockSpec(memory_space=pltpu.VMEM)
    square = pltpu.VMEM((size, size), F32)
    return pl.pallas_call(
        kernel,
        out_shape=[
            jax.ShapeDtypeStruct((size, size), BF16),
            jax.ShapeDtypeStruct((size, size), BF16),
            jax.ShapeDtypeStruct((BLOCK, BLOCK), F32),
        ],
        in_specs=[vmem] * 8,
        out_specs=[vmem] * 3,
        scratch_shapes=[square] * 3
        + [pltpu.VMEM((wide, wide), F32)] * 2
        + [pltpu.VMEM((wide, 2 * wide), F32)],
        compiler_params=pltpu.CompilerParams(vmem_limit_bytes=40 * MIB),
        cost_estimate=pl.CostEstimate(flops=1, bytes_accessed=1, transcendentals=0),
        name="head_factor",
    )(*gathered)


def solve_columns(col_panel, inverse):
    size, wide = HEAD * BLOCK, 6 * BLOCK

    def kernel(wh, wl, in0, in1, in2, in3, oh_ref, ol_ref, ch, cl, yh, yl):
        p, q = lax.axis_index("prow"), lax.axis_index("pcol")
        for z_back, in_ref in enumerate((in0, in1, in2, in3)):
            for y_back in range(2):
                m = (p // 4 + y_back) % 2 * 4 + (p + 4 - z_back) % 4
                cols = pl.ds(pl.multiple_of(m * BLOCK, BLOCK), BLOCK)
                for s in range(6):
                    rows = slice(s * BLOCK, (s + 1) * BLOCK)
                    ch[rows, cols], cl[rows, cols] = split(in_ref[y_back, s])
        for i in range(0, size, 256):
            e = i + 256
            y = dot3((ch[:, 0:e], cl[:, 0:e]), (wh[i:e, 0:e], wl[i:e, 0:e]), NT)
            yh[:, i:e], yl[:, i:e] = split(y)
        for i in range(0, size, 256):
            e = i + 256
            z = dot3((yh[:, i:], yl[:, i:]), (wh[i:, i:e], wl[i:, i:e]), NN)
            oh_ref[:, i:e], ol_ref[:, i:e] = split(z)

        @pl.when(q < HEAD)
        def _():
            rows = pl.ds(pl.multiple_of(q * BLOCK, BLOCK), BLOCK)
            oh_ref[0:BLOCK, :] = -wh[rows, :]
            ol_ref[0:BLOCK, :] = -wl[rows, :]

    vmem = pl.BlockSpec(memory_space=pltpu.VMEM)
    return pl.pallas_call(
        kernel,
        out_shape=[jax.ShapeDtypeStruct((wide, size), BF16)] * 2,
        in_specs=[vmem] * 6,
        out_specs=[vmem] * 2,
        scratch_shapes=[pltpu.VMEM((wide, size), BF16)] * 4,
        compiler_params=pltpu.CompilerParams(vmem_limit_bytes=32 * MIB),
        cost_estimate=pl.CostEstimate(flops=1, bytes_accessed=1, transcendentals=0),
        name="solve_columns",
    )(*inverse, *col_panel)


def finish(front, diagonal, arrived, row_panel, solved, own, child_map):
    size, group, wide = HEAD * BLOCK, 4, 6 * BLOCK

    def kernel(
        map_ref, sh, sl, own_ref, diag_ref, *refs
    ):
        in_refs, (row_ref, front_ref, out_ref) = refs[:8], refs[8:]
        step = pl.program_id(0)
        p, q = lax.axis_index("prow"), lax.axis_index("pcol")
        out_ref[...] = front_ref[...]
        for s in range(6):
            l = 2 * s + jnp.where(q >= 8, 1, 0)

            @pl.when((q % 8 == p) & (l // group == step))
            def _():
                rows = pl.ds(pl.multiple_of((l % group) * BLOCK, BLOCK), BLOCK)
                out_ref[rows, s * BLOCK : (s + 1) * BLOCK] += diag_block(
                    diag_ref[pl.ds(16 * s + q, 1), :]
                )

        for c in range(2):
            places = [local_col(map_ref, c, (q // 4 + 4 - d) % 4, q) for d in range(4)]

            def add(k, n):
                l = local_row(map_ref, c, k, n, p)

                @pl.when(l // group == step)
                def _():
                    rows = pl.ds(pl.multiple_of((l % group) * BLOCK, BLOCK), BLOCK)
                    for d in range(4):
                        cols = pl.ds(pl.multiple_of(places[d] * BLOCK, BLOCK), BLOCK)
                        out_ref[rows, cols] += in_refs[4 * n + d][c, k]

            for n in range(2):
                pl.loop(0, 4)(functools.partial(add, n=n))

        @pl.when(q < HEAD)
        def _():
            out_ref[:, 0:BLOCK] = jnp.zeros((group * BLOCK, BLOCK), F32)

        rows = []
        for k in range(group):
            rows.append(
                jnp.concatenate([row_ref[k % 2 * 8 + m, k // 2] for m in range(HEAD)], axis=1)
            )
        rows = split(jnp.concatenate(rows, axis=0))
        for j in range(0, wide, 256):
            e = j + 256
            out_ref[:, j:e] -= dot3(rows, (sh[j:e, :], sl[j:e, :]), NT)

        @pl.when(step == 0)
        def _():
            out_ref[0:BLOCK, :] = jnp.zeros((BLOCK, wide), F32)
            out_ref[0:BLOCK, 0:BLOCK] = own_ref[...]

    vmem = pl.BlockSpec(memory_space=pltpu.VMEM)

    def whole(*shape):
        return pl.BlockSpec(shape, lambda i: (0,) * len(shape), pipeline_mode=pl.Buffered(1))

    return pl.pallas_call(
        kernel,
        out_shape=jax.ShapeDtypeStruct((12 * BLOCK, wide), F32),
        grid=(12 // group,),
        in_specs=[
            pl.BlockSpec(memory_space=pltpu.SMEM),
            vmem,
            vmem,
            whole(BLOCK, BLOCK),
            whole(96, BLOCK),
            *[vmem] * 8,
            pl.BlockSpec((16, group // 2, BLOCK, BLOCK), lambda i: (0, i, 0, 0)),
            pl.BlockSpec((group * BLOCK, wide), lambda i: (i, 0)),
        ],
        out_specs=pl.BlockSpec((group * BLOCK, wide), lambda i: (i, 0)),
        compiler_params=pltpu.CompilerParams(vmem_limit_bytes=52 * MIB),
        cost_estimate=pl.CostEstimate(flops=1, bytes_accessed=1, transcendentals=0),
        name="finish",
    )(child_map, *solved, own, diagonal, *arrived, row_panel, front)


def ahead_x(d):
    return [(4 * x + w, 4 * ((x + d) % 4) + w) for x in range(4) for w in range(4)]


def ahead_z(d):
    return [(4 * h + z, 4 * h + (z + d) % 4) for h in range(2) for z in range(4)]


def ahead_y(d):
    def rank(y, z, x, core):
        return (4 * (y // 2) + z) * 16 + 4 * x + 2 * (y % 2) + core

    return [
        (rank(y, z, x, core), rank((y + d) % 4, z, x, core))
        for y in range(4) for z in range(4) for x in range(4) for core in range(2)
    ]


OTHER_CORE = [(k, k ^ 1) for k in range(16)]
BOTH = ("prow", "pcol")


def gather_head(terms):
    held = terms
    for d in (1, 2, 3):
        held = held + lax.ppermute(terms, "pcol", ahead_x(d))
    summed = held
    along_y = [held] + [lax.ppermute(held, BOTH, ahead_y(d)) for d in (1, 2, 3)]
    held = jnp.concatenate(along_y, axis=0)
    along_z = [held] + [lax.ppermute(held, "prow", ahead_z(d)) for d in (1, 2, 3)]
    return summed, along_z, [lax.ppermute(part, "pcol", OTHER_CORE) for part in along_z]


def gather_columns(piece):
    turned = lax.ppermute(
        piece,
        BOTH,
        [
            (p * 16 + (2 * par + e) * 4 + w, (4 * e + w) * 16 + p + 8 * par)
            for p in range(8) for par in range(2) for e in range(2) for w in range(4)
        ],
    )
    other = lax.ppermute(turned, "prow", [(p, p ^ 4) for p in range(8)])
    held = jnp.stack([turned, other], axis=0)
    return [held] + [lax.ppermute(held, "prow", ahead_z(d)) for d in (1, 2, 3)]


def per_device(front, diagonal, child, child_map):
    x = lax.axis_index("pcol") // 4
    child_map = child_map.reshape(128)
    diagonal = diagonal.reshape(96, BLOCK)

    def exchange(sent):
        sent = lax.all_to_all(
            sent.reshape(32, BLOCK, BLOCK), BOTH, 0, 0, axis_index_groups=PLANE_GROUPS, tiled=True
        )
        return sent.reshape(4, 2, 4, BLOCK, BLOCK)

    def collect(terms, n):
        parts = [terms[0]]
        for d in (1, 2, 3):
            pairs = [pair for pair in ahead_x(d) if pair[1] // 8 == n]
            parts.append(lax.ppermute(terms[d], "pcol", pairs))
        return parts

    def forward(blocks):
        return [blocks[0]] + [lax.ppermute(blocks[d], "pcol", ahead_x(d)) for d in (1, 2, 3)]

    even, odd = pack_rows(child, child_map)
    even = exchange(even)
    even, odd = lax.optimization_barrier((even, odd))
    odd = exchange(odd)
    *terms, head_terms = panel_terms(front, diagonal, even, child_map, 0)
    summed, along_z, twins = gather_head(head_terms)
    parts = collect(terms, 0)
    first = parts[0] + parts[1] + parts[2] + parts[3]
    first, *blocks = lax.optimization_barrier([first, *pack_cols(even, child_map)])
    arrived = forward(blocks)
    odd, arrived, along_z = lax.optimization_barrier((odd, arrived, along_z))
    *terms, _ = panel_terms(front, diagonal, odd, child_map, 1)
    parts = collect(terms, 1)
    *inverse, own = head_factor(along_z + twins)
    parts, inverse = lax.optimization_barrier((parts, inverse))
    second = parts[0] + parts[1] + parts[2] + parts[3]
    piece = jnp.where(x < 2, first, second)
    row_panel = lax.all_gather(piece, "pcol")
    col_panel = gather_columns(piece)
    piece, *blocks = lax.optimization_barrier([piece, *pack_cols(odd, child_map)])
    arrived = arrived + forward(blocks)
    solved = solve_columns(col_panel, inverse)
    return finish(front, diagonal, arrived, row_panel, solved, own, child_map)


def solution(mesh):
    return jax.shard_map(
        per_device,
        mesh=mesh,
        in_specs=(P("prow", "pcol"), P(), P("prow", "pcol"), P()),
        out_specs=P("prow", "pcol"),
        check_vma=False,
    )
```

```python
import functools

import jax
import jax.numpy as jnp
from jax import lax
from jax.experimental import pallas as pl
from jax.experimental.pallas import tpu as pltpu
from jax.sharding import PartitionSpec as P

BLOCK = 128
HEAD = 8
F32 = jnp.float32
BF16 = jnp.bfloat16
HIGHEST = lax.Precision.HIGHEST
MIB = 1024 * 1024

PLANE_GROUPS = [[16 * p + 4 * x + w for w in range(4) for p in range(8)] for x in range(4)]


def pack_rows(child, child_map):
    def kernel(map_ref, child_ref, out_ref, buf, turned, sems):
        c = lax.axis_index("prow") // 4
        shift = map_ref[c * 64] % 16

        def fetch(i):
            rows = pl.ds(pl.multiple_of(i * BLOCK, BLOCK), BLOCK)
            return pltpu.make_async_copy(child_ref.at[rows], buf.at[i], sems.at[0, i])

        def store(i):
            residue = (i + shift) % 16
            return pltpu.make_async_copy(
                turned.at[i], out_ref.at[:, residue % 8, residue // 8], sems.at[1, i]
            )

        def forward(i):
            fetch(i).wait()
            for w in range(4):
                b = (w - shift + 16) % 4
                turned[i, w] = buf[i, :, pl.ds(pl.multiple_of(b * BLOCK, BLOCK), BLOCK)]
            store(i).start()

        pl.loop(0, 16)(lambda i: fetch(i).start())
        pl.loop(0, 16)(forward)
        pl.loop(0, 16)(lambda i: store(i).wait())

    return pl.pallas_call(
        kernel,
        out_shape=jax.ShapeDtypeStruct((4, 8, 2, BLOCK, BLOCK), F32),
        in_specs=[pl.BlockSpec(memory_space=pltpu.SMEM), pl.BlockSpec(memory_space=pl.ANY)],
        out_specs=pl.BlockSpec(memory_space=pl.ANY),
        scratch_shapes=[
            pltpu.VMEM((16, BLOCK, 4 * BLOCK), F32),
            pltpu.VMEM((16, 4, BLOCK, BLOCK), F32),
            pltpu.SemaphoreType.DMA((2, 16)),
        ],
        compiler_params=pltpu.CompilerParams(vmem_limit_bytes=16 * MIB),
        cost_estimate=pl.CostEstimate(flops=0, bytes_accessed=8 * MIB, transcendentals=0),
        name="pack_rows",
    )(child_map, child)


def pack_cols(arrived, child_map):
    def kernel(map_ref, in_ref, *refs):
        out_refs, (buf, sems) = refs[:4], refs[4:]
        q = lax.axis_index("pcol")
        x, w = q // 4, q % 4

        def fetch(k):
            d, c = k // 2, k % 2
            column = 4 * ((x + d) % 4) + w
            a = ((column - map_ref[c * 64] % 16 + 16) % 16) // 4
            return pltpu.make_async_copy(in_ref.at[a, c], buf.at[k], sems.at[0, k])

        def store(k):
            return pltpu.make_async_copy(buf.at[k], out_refs[k // 2].at[k % 2], sems.at[1, k])

        for k in range(8):
            fetch(k).start()
        for k in range(8):
            fetch(k).wait()
            store(k).start()
        for k in range(8):
            store(k).wait()

    return pl.pallas_call(
        kernel,
        out_shape=[jax.ShapeDtypeStruct((2, 4, 2, BLOCK, BLOCK), F32)] * 4,
        in_specs=[pl.BlockSpec(memory_space=pltpu.SMEM), pl.BlockSpec(memory_space=pl.ANY)],
        out_specs=[pl.BlockSpec(memory_space=pltpu.HBM)] * 4,
        scratch_shapes=[
            pltpu.VMEM((8, 4, 2, BLOCK, BLOCK), F32), pltpu.SemaphoreType.DMA((2, 8))
        ],
        compiler_params=pltpu.CompilerParams(vmem_limit_bytes=16 * MIB),
        cost_estimate=pl.CostEstimate(flops=0, bytes_accessed=8 * MIB, transcendentals=0),
        name="pack_cols",
    )(child_map, arrived)


def diag_block(values):
    rows = lax.broadcasted_iota(jnp.int32, (BLOCK, BLOCK), 0)
    cols = lax.broadcasted_iota(jnp.int32, (BLOCK, BLOCK), 1)
    return jnp.where(rows == cols, jnp.broadcast_to(values, (BLOCK, BLOCK)), 0.0)


def local_row(map_ref, c, h, n, p):
    shift = map_ref[c * 64] % 16
    i = (p + 8 * n - shift + 16) % 16
    return map_ref[c * 64 + 16 * h + i] // 8


def local_col(map_ref, c, t, q):
    shift = map_ref[c * 64] % 16
    return map_ref[c * 64 + 16 * t + (q - shift + 16) % 16] // 16


def panel_terms(front, diagonal, arrived, child_map):
    def kernel(map_ref, front_ref, diag_ref, in_ref, *refs):
        out_refs, head_ref, (total, buf, sems) = refs[:4], refs[4], refs[5:]
        p, q = lax.axis_index("prow"), lax.axis_index("pcol")
        x, w = q // 4, q % 4
        chosen, copies = [], []
        for e in range(2):
            for c in range(2):
                at = (4 * e + w - map_ref[c * 64] % 16 + 16) % 16
                chosen.append(map_ref[c * 64 + 16 * x + at] // 16 == 0)
                copies.append(
                    pltpu.make_async_copy(
                        in_ref.at[at // 4, c], buf.at[2 * e + c], sems.at[2 * e + c]
                    )
                )
                copies[-1].start()
        total[...] = jnp.zeros_like(total)

        @pl.when(x < 2)
        def _():
            for l in range(12):
                total[l % 2 * 2 + x, l // 2] = front_ref[l * BLOCK : (l + 1) * BLOCK, :]

        @pl.when(p == q)
        def _():
            total[x, 0] += diag_block(diag_ref[pl.ds(q, 1), :])

        for k in range(4):
            e, c = k // 2, k % 2
            copies[k].wait()

            @pl.when(chosen[k])
            def _():
                def add(i):
                    l = local_row(map_ref, c, i // 2, i % 2, p)
                    total[l % 2 * 2 + e, l // 2] += buf[k, i // 2, i % 2]

                pl.loop(0, 8)(add)

        for d in range(4):
            out_refs[d][...] = total[(x + d) % 4]
        for e in range(2):
            head_ref[e] = total[e, 0]

    return pl.pallas_call(
        kernel,
        out_shape=[jax.ShapeDtypeStruct((6, BLOCK, BLOCK), F32)] * 4
        + [jax.ShapeDtypeStruct((2, BLOCK, BLOCK), F32)],
        grid=(1,),
        in_specs=[
            pl.BlockSpec(memory_space=pltpu.SMEM),
            pl.BlockSpec((12 * BLOCK, BLOCK), lambda i: (0, 0)),
            pl.BlockSpec((96, BLOCK), lambda i: (0, 0)),
            pl.BlockSpec(memory_space=pl.ANY),
        ],
        out_specs=[pl.BlockSpec((6, BLOCK, BLOCK), lambda i: (0, 0, 0))] * 4
        + [pl.BlockSpec((2, BLOCK, BLOCK), lambda i: (0, 0, 0))],
        scratch_shapes=[
            pltpu.VMEM((4, 6, BLOCK, BLOCK), F32),
            pltpu.VMEM((4, 4, 2, BLOCK, BLOCK), F32),
            pltpu.SemaphoreType.DMA((4,)),
        ],
        compiler_params=pltpu.CompilerParams(vmem_limit_bytes=24 * MIB),
        cost_estimate=pl.CostEstimate(flops=0, bytes_accessed=5 * MIB, transcendentals=0),
        name="panel_terms",
    )(child_map, front, diagonal, arrived)


NN = ((1,), (0,))
NT = ((1,), (1,))
TN = ((0,), (0,))


def dot(a, b, contract):
    dims = (contract, ((), ()))
    return lax.dot_general(a, b, dims, precision=HIGHEST, preferred_element_type=F32)


def dot1(a, b, contract):
    return lax.dot_general(a, b, (contract, ((), ())), preferred_element_type=F32)


def split(value):
    high = value.astype(BF16)
    return high, (value - high.astype(F32)).astype(BF16)


def dot3(a, b, contract):
    (ah, al), (bh, bl) = a, b
    return dot1(ah, bl, contract) + dot1(al, bh, contract) + dot1(ah, bh, contract)


def square_iotas(size):
    shape = (size, size)
    return lax.broadcasted_iota(jnp.int32, shape, 0), lax.broadcasted_iota(jnp.int32, shape, 1)


def newton_factor(a_ref, x_ref):
    ri, ci = square_iotas(a_ref.shape[0])
    one = jnp.where(ri == ci, 1.0, 0.0)

    def lower_half(e):
        return jnp.where(ri > ci, e, jnp.where(ri == ci, 0.5 * e, 0.0))

    a = a_ref[...]
    pivots = jnp.where(ri == ci, a, 0.0)
    scale = lax.rsqrt(jnp.sum(pivots, axis=0, keepdims=True))
    f = split(jnp.where(ri > ci, a * lax.rsqrt(jnp.sum(pivots, axis=1, keepdims=True)) * scale, 0.0))
    x = (one - (f[0].astype(F32) + f[1].astype(F32)) + dot1(f[0], f[0], NN)) * scale
    xs = split(x)
    e = dot3(split(dot3(xs, split(a), NN)), xs, NT) - one
    f = split(lower_half(e))
    g = dot3(f, xs, NN)
    x = x - g + dot1(f[0], g.astype(BF16), NN)
    t = dot(x, a, NN)
    e = dot(t, x, NT) - one
    f = split(lower_half(e))
    x_ref[...] = x - dot3(f, split(x), NN)
    a_ref[...] = jnp.where(ci >= ri, t - dot3(f, split(t), NN), 0.0)
    return jnp.max(jnp.sum(jnp.abs(e), axis=1, keepdims=True))


def direct_factor(t_ref):
    size = t_ref.shape[0]
    ri, ci = square_iotas(size)
    lane = lax.broadcasted_iota(jnp.int32, (1, 2 * size), 1)
    down = lax.broadcasted_iota(jnp.int32, (size, 1), 0)

    def step(j):
        row = t_ref[pl.ds(j, 1), :]
        row = row * lax.rsqrt(jnp.sum(jnp.where(lane == j, row, 0.0), axis=1, keepdims=True))
        col = jnp.broadcast_to(row[:, :size], (size, size))
        col = jnp.sum(jnp.where(ri == ci, col, 0.0), axis=1, keepdims=True)
        t_ref[...] = t_ref[...] - jnp.where(down > j, col, 0.0) * row
        t_ref[pl.ds(j, 1), :] = row

    pl.loop(0, size)(step)


def head_factor(gathered):
    size, wide = HEAD * BLOCK, 2 * BLOCK

    def kernel(*refs):
        in_refs, (wh_ref, wl_ref, own_ref), scratch = refs[:8], refs[8:11], refs[11:]
        m_ref, u_ref, w_ref, a_ref, x_ref, t_ref = scratch
        p, q = lax.axis_index("prow"), lax.axis_index("pcol")

        def place(k, in_ref, core_back, y_back):
            core = (q + core_back) % 2
            y = (2 * (p // 4) + (q // 2) % 2 - y_back + 4) % 4
            z = (p - k // 2 + 4) % 4
            row, col = y // 2 * 4 + z, k % 2 * 4 + y % 2 * 2 + core
            rows = pl.ds(pl.multiple_of(row * BLOCK, BLOCK), BLOCK)
            cols = pl.ds(pl.multiple_of(col * BLOCK, BLOCK), BLOCK)
            m_ref[rows, cols] = in_ref[k]

        for at in range(8):
            pl.loop(0, 8)(
                functools.partial(place, in_ref=in_refs[at], core_back=at // 4, y_back=at % 4)
            )
        for i in range(HEAD):
            for j in range(i, HEAD):
                rows, cols = slice(i * BLOCK, (i + 1) * BLOCK), slice(j * BLOCK, (j + 1) * BLOCK)
                value = m_ref[cols, rows].T
                if i // 4 == j // 4:
                    value = 0.5 * (m_ref[rows, cols] + value)
                u_ref[rows, cols] = value
                if i // 2 == j // 2 and i != j:
                    u_ref[cols, rows] = value.T
        ri, ci = square_iotas(wide)
        for s in range(0, size, wide):
            e = s + wide
            a_ref[...] = u_ref[s:e, s:e]
            off = newton_factor(a_ref, x_ref)

            @pl.when(jnp.logical_not(off < 5e-4))
            def _():
                t_ref[:, :wide] = u_ref[s:e, s:e]
                t_ref[:, wide:] = jnp.where(ri == ci, 1.0, 0.0)
                direct_factor(t_ref)
                a_ref[...] = jnp.where(ci >= ri, t_ref[:, :wide], 0.0)
                x_ref[...] = jnp.where(ri >= ci, t_ref[:, wide:], 0.0)

            u_ref[s:e, s:e] = a_ref[...]
            w_ref[s:e, s:e] = x_ref[...]
            inverse = split(x_ref[...])
            if s:
                w_ref[s:e, 0:s] = dot3(inverse, split(w_ref[s:e, 0:s]), NN)
            done = split(w_ref[s:e, 0:e])
            wh_ref[s:e, 0:e], wl_ref[s:e, 0:e] = done
            if e < size:
                wh_ref[s:e, e:] = jnp.zeros((wide, size - e), BF16)
                wl_ref[s:e, e:] = jnp.zeros((wide, size - e), BF16)
                right = dot3(inverse, split(u_ref[s:e, e:]), NN)
                u_ref[s:e, e:] = right
                right = split(right)
                for j in range(e, size, wide):
                    left = tuple(v[:, j - e : j - e + wide] for v in right)
                    rest = tuple(v[:, j - e :] for v in right)
                    u_ref[j : j + wide, j:] = u_ref[j : j + wide, j:] - dot3(left, rest, TN)
                    change = dot3(left, done, TN)
                    if s:
                        w_ref[j : j + wide, 0:s] = w_ref[j : j + wide, 0:s] - change[:, 0:s]
                    w_ref[j : j + wide, s:e] = -change[:, s:e]
        own_ref[...] = jnp.zeros((BLOCK, BLOCK), F32)

        @pl.when(q <= p)
        def _():
            rows = pl.ds(pl.multiple_of(q * BLOCK, BLOCK), BLOCK)
            cols = pl.ds(pl.multiple_of(p * BLOCK, BLOCK), BLOCK)
            own_ref[...] = u_ref[rows, cols].T

    vmem = pl.BlockSpec(memory_space=pltpu.VMEM)
    square = pltpu.VMEM((size, size), F32)
    return pl.pallas_call(
        kernel,
        out_shape=[
            jax.ShapeDtypeStruct((size, size), BF16),
            jax.ShapeDtypeStruct((size, size), BF16),
            jax.ShapeDtypeStruct((BLOCK, BLOCK), F32),
        ],
        in_specs=[vmem] * 8,
        out_specs=[vmem] * 3,
        scratch_shapes=[square] * 3
        + [pltpu.VMEM((wide, wide), F32)] * 2
        + [pltpu.VMEM((wide, 2 * wide), F32)],
        compiler_params=pltpu.CompilerParams(vmem_limit_bytes=40 * MIB),
        cost_estimate=pl.CostEstimate(
            flops=20_000_000_000, bytes_accessed=8 * MIB, transcendentals=0
        ),
        name="head_factor",
    )(*gathered)


def solve_columns(col_panel, inverse):
    size, wide = HEAD * BLOCK, 6 * BLOCK

    def kernel(wh, wl, *refs):
        in_refs, out_refs, (ch, cl, yh, yl, sems) = refs[:8], refs[8:10], refs[10:]
        p, q = lax.axis_index("prow"), lax.axis_index("pcol")
        for k, in_ref in enumerate(in_refs):
            m = (p // 4 + k // 4) % 2 * 4 + (p + 4 - k % 4) % 4
            cols = pl.ds(pl.multiple_of(m * BLOCK, BLOCK), BLOCK)
            for s in range(6):
                rows = slice(s * BLOCK, (s + 1) * BLOCK)
                ch[rows, cols], cl[rows, cols] = split(in_ref[s])
        for i in range(0, size, 256):
            e = i + 256
            y = dot3((ch[:, 0:e], cl[:, 0:e]), (wh[i:e, 0:e], wl[i:e, 0:e]), NT)
            yh[:, i:e], yl[:, i:e] = split(y)
        for i in range(0, size, 256):
            e = i + 256
            z = dot3((yh[:, i:], yl[:, i:]), (wh[i:, i:e], wl[i:, i:e]), NN)
            ch[:, i:e], cl[:, i:e] = split(z)

        @pl.when(q < HEAD)
        def _():
            rows = pl.ds(pl.multiple_of(q * BLOCK, BLOCK), BLOCK)
            ch[0:BLOCK, :] = -wh[rows, :]
            cl[0:BLOCK, :] = -wl[rows, :]

        stores = [
            pltpu.make_async_copy(ch, out_refs[0], sems.at[0]),
            pltpu.make_async_copy(cl, out_refs[1], sems.at[1]),
        ]
        for store in stores:
            store.start()
        for store in stores:
            store.wait()

    vmem = pl.BlockSpec(memory_space=pltpu.VMEM)
    return pl.pallas_call(
        kernel,
        out_shape=[jax.ShapeDtypeStruct((wide, size), BF16)] * 2,
        in_specs=[vmem] * 10,
        out_specs=[pl.BlockSpec(memory_space=pltpu.HBM)] * 2,
        scratch_shapes=[pltpu.VMEM((wide, size), BF16)] * 4 + [pltpu.SemaphoreType.DMA((2,))],
        compiler_params=pltpu.CompilerParams(vmem_limit_bytes=32 * MIB),
        cost_estimate=pl.CostEstimate(
            flops=8_000_000_000, bytes_accessed=10 * MIB, transcendentals=0
        ),
        name="solve_columns",
    )(*inverse, *col_panel)


def finish(front, diagonal, arrived, row_panel, solved, own, child_map):
    size, group, wide = HEAD * BLOCK, 4, 6 * BLOCK

    def kernel(
        map_ref, own_ref, diag_ref, row_ref, front_ref, *refs
    ):
        sources, out_ref, (sh, sl, *in_refs), sems = refs[:6], refs[6], refs[7:13], refs[13]
        step = pl.program_id(0)

        def load(k):
            return pltpu.make_async_copy(sources[k], (sh, sl, *in_refs)[k], sems.at[k])

        @pl.when(step == 0)
        def _():
            for k in range(6):
                load(k).start()

        p, q = lax.axis_index("prow"), lax.axis_index("pcol")
        out_ref[...] = front_ref[...]
        for s in range(6):
            l = 2 * s + jnp.where(q >= 8, 1, 0)

            @pl.when((q % 8 == p) & (l // group == step))
            def _():
                rows = pl.ds(pl.multiple_of((l % group) * BLOCK, BLOCK), BLOCK)
                out_ref[rows, s * BLOCK : (s + 1) * BLOCK] += diag_block(
                    diag_ref[pl.ds(16 * s + q, 1), :]
                )

        @pl.when(step == 0)
        def _():
            for k in range(6):
                load(k).wait()

        for c in range(2):
            places = [local_col(map_ref, c, (q // 4 + 4 - d) % 4, q) for d in range(4)]

            def add(k):
                l = local_row(map_ref, c, k // 2, k % 2, p)

                @pl.when(l // group == step)
                def _():
                    rows = pl.ds(pl.multiple_of((l % group) * BLOCK, BLOCK), BLOCK)
                    for d in range(4):
                        cols = pl.ds(pl.multiple_of(places[d] * BLOCK, BLOCK), BLOCK)
                        out_ref[rows, cols] += in_refs[d][c, k // 2, k % 2]

            pl.loop(0, 8)(add)

        @pl.when(q < HEAD)
        def _():
            out_ref[:, 0:BLOCK] = jnp.zeros((group * BLOCK, BLOCK), F32)

        rows = []
        for k in range(group):
            rows.append(
                jnp.concatenate([row_ref[k % 2 * 8 + m, k // 2] for m in range(HEAD)], axis=1)
            )
        rows = split(jnp.concatenate(rows, axis=0))
        for j in range(0, wide, 256):
            e = j + 256
            out_ref[:, j:e] -= dot3(rows, (sh[j:e, :], sl[j:e, :]), NT)

        @pl.when(step == 0)
        def _():
            out_ref[0:BLOCK, :] = jnp.zeros((BLOCK, wide), F32)
            out_ref[0:BLOCK, 0:BLOCK] = own_ref[...]

    def whole(*shape):
        return pl.BlockSpec(shape, lambda i: (0,) * len(shape), pipeline_mode=pl.Buffered(1))

    return pl.pallas_call(
        kernel,
        out_shape=jax.ShapeDtypeStruct((12 * BLOCK, wide), F32),
        grid=(12 // group,),
        in_specs=[
            pl.BlockSpec(memory_space=pltpu.SMEM),
            whole(BLOCK, BLOCK),
            whole(96, BLOCK),
            pl.BlockSpec((16, group // 2, BLOCK, BLOCK), lambda i: (0, i, 0, 0)),
            pl.BlockSpec((group * BLOCK, wide), lambda i: (i, 0)),
            *[pl.BlockSpec(memory_space=pltpu.HBM)] * 6,
        ],
        out_specs=pl.BlockSpec((group * BLOCK, wide), lambda i: (i, 0)),
        scratch_shapes=[pltpu.VMEM((wide, size), BF16)] * 2
        + [pltpu.VMEM((2, 4, 2, BLOCK, BLOCK), F32)] * 4
        + [pltpu.SemaphoreType.DMA((6,))],
        compiler_params=pltpu.CompilerParams(vmem_limit_bytes=60 * MIB),
        cost_estimate=pl.CostEstimate(
            flops=8_000_000_000, bytes_accessed=24 * MIB, transcendentals=0
        ),
        name="finish",
    )(child_map, own, diagonal, row_panel, front, *solved, *arrived)


def ahead_x(d):
    return [(4 * x + w, 4 * ((x + d) % 4) + w) for x in range(4) for w in range(4)]


def ahead_z(d):
    return [(4 * h + z, 4 * h + (z + d) % 4) for h in range(2) for z in range(4)]


def ahead_y(d):
    def rank(y, z, x, core):
        return (4 * (y // 2) + z) * 16 + 4 * x + 2 * (y % 2) + core

    return [
        (rank(y, z, x, core), rank((y + d) % 4, z, x, core))
        for y in range(4) for z in range(4) for x in range(4) for core in range(2)
    ]


OTHER_CORE = [(k, k ^ 1) for k in range(16)]
BOTH = ("prow", "pcol")


def sum_head(terms):
    held = terms
    for d in (1, 2, 3):
        held = held + lax.ppermute(terms, "pcol", ahead_x(d))
    return all_z(held)


def gather_head(along_z):
    held = jnp.concatenate(along_z, axis=0)
    along_y = [held] + [lax.ppermute(held, BOTH, ahead_y(d)) for d in (1, 2, 3)]
    return along_y + [lax.ppermute(part, "pcol", OTHER_CORE) for part in along_y]


def all_z(value):
    return [value] + [lax.ppermute(value, "prow", ahead_z(d)) for d in (1, 2, 3)]


def turn(piece):
    return lax.ppermute(
        piece,
        BOTH,
        [
            (p * 16 + (2 * par + e) * 4 + w, (4 * e + w) * 16 + p + 8 * par)
            for p in range(8) for par in range(2) for e in range(2) for w in range(4)
        ],
    )


def per_device(front, diagonal, child, child_map):
    child_map = child_map.reshape(128)
    diagonal = diagonal.reshape(96, BLOCK)
    sent = pack_rows(child, child_map).reshape(64, BLOCK, BLOCK)
    sent = lax.all_to_all(sent, BOTH, 0, 0, axis_index_groups=PLANE_GROUPS, tiled=True)
    sent = sent.reshape(4, 2, 4, 2, BLOCK, BLOCK)
    *terms, head_terms = panel_terms(front, diagonal, sent, child_map)
    behind = [lax.ppermute(terms[d], "pcol", ahead_x(d)) for d in (1, 2, 3)]
    head = sum_head(head_terms)
    blocks = pack_cols(sent, child_map)
    behind, head = lax.optimization_barrier((behind, head))
    piece = terms[0] + behind[0] + behind[1] + behind[2]
    piece, *ahead = lax.optimization_barrier([piece, *blocks[1:]])
    arrived = [blocks[0]]
    for d in (1, 2, 3):
        arrived.append(lax.ppermute(ahead[d - 1], "pcol", ahead_x(d)))
    row_panel = lax.all_gather(piece, "pcol")
    turned = turn(piece)
    turned, head = lax.optimization_barrier((turned, head))
    other = lax.ppermute(turned, "prow", [(p, p ^ 4) for p in range(8)])
    col_panel = all_z(turned)
    col_panel += all_z(other)
    *inverse, own = head_factor(gather_head(head))
    solved = solve_columns(col_panel, inverse)
    return finish(front, diagonal, arrived, row_panel, solved, own, child_map)


def solution(mesh):
    return jax.shard_map(
        per_device,
        mesh=mesh,
        in_specs=(P("prow", "pcol"), P(), P("prow", "pcol"), P()),
        out_specs=P("prow", "pcol"),
        check_vma=False,
    )
```

```python
import functools

import jax
import jax.numpy as jnp
from jax import lax
from jax.experimental import pallas as pl
from jax.experimental.pallas import tpu as pltpu
from jax.sharding import PartitionSpec as P

BLOCK = 128
HEAD = 8
F32 = jnp.float32
BF16 = jnp.bfloat16
HIGHEST = lax.Precision.HIGHEST
MIB = 1024 * 1024

PLANE_GROUPS = [[16 * p + 4 * x + w for w in range(4) for p in range(8)] for x in range(4)]


def pack_rows(child, child_map):
    def kernel(map_ref, child_ref, out_ref, buf, turned, sems):
        c = lax.axis_index("prow") // 4
        shift = map_ref[c * 64] % 16

        def fetch(i):
            rows = pl.ds(pl.multiple_of(i * BLOCK, BLOCK), BLOCK)
            return pltpu.make_async_copy(child_ref.at[rows], buf.at[i], sems.at[0, i])

        def store(i):
            residue = (i + shift) % 16
            return pltpu.make_async_copy(
                turned.at[i], out_ref.at[:, residue % 8, residue // 8], sems.at[1, i]
            )

        def forward(i):
            fetch(i).wait()
            for w in range(4):
                b = (w - shift + 16) % 4
                turned[i, w] = buf[i, :, pl.ds(pl.multiple_of(b * BLOCK, BLOCK), BLOCK)]
            store(i).start()

        pl.loop(0, 16)(lambda i: fetch(i).start())
        pl.loop(0, 16)(forward)
        pl.loop(0, 16)(lambda i: store(i).wait())

    return pl.pallas_call(
        kernel,
        out_shape=jax.ShapeDtypeStruct((4, 8, 2, BLOCK, BLOCK), F32),
        in_specs=[pl.BlockSpec(memory_space=pltpu.SMEM), pl.BlockSpec(memory_space=pl.ANY)],
        out_specs=pl.BlockSpec(memory_space=pl.ANY),
        scratch_shapes=[
            pltpu.VMEM((16, BLOCK, 4 * BLOCK), F32),
            pltpu.VMEM((16, 4, BLOCK, BLOCK), F32),
            pltpu.SemaphoreType.DMA((2, 16)),
        ],
        compiler_params=pltpu.CompilerParams(vmem_limit_bytes=16 * MIB),
        cost_estimate=pl.CostEstimate(flops=0, bytes_accessed=8 * MIB, transcendentals=0),
        name="pack_rows",
    )(child_map, child)


def pack_cols(arrived, child_map):
    def kernel(map_ref, in_ref, *refs):
        out_refs, (buf, sems) = refs[:4], refs[4:]
        q = lax.axis_index("pcol")
        x, w = q // 4, q % 4

        def fetch(k):
            d, c = k // 2, k % 2
            column = 4 * ((x + d) % 4) + w
            a = ((column - map_ref[c * 64] % 16 + 16) % 16) // 4
            return pltpu.make_async_copy(in_ref.at[a, c], buf.at[k], sems.at[0, k])

        def store(k):
            return pltpu.make_async_copy(buf.at[k], out_refs[k // 2].at[k % 2], sems.at[1, k])

        for k in range(8):
            fetch(k).start()
        for k in range(8):
            fetch(k).wait()
            store(k).start()
        for k in range(8):
            store(k).wait()

    return pl.pallas_call(
        kernel,
        out_shape=[jax.ShapeDtypeStruct((2, 4, 2, BLOCK, BLOCK), F32)] * 4,
        in_specs=[pl.BlockSpec(memory_space=pltpu.SMEM), pl.BlockSpec(memory_space=pl.ANY)],
        out_specs=[pl.BlockSpec(memory_space=pltpu.HBM)] * 4,
        scratch_shapes=[
            pltpu.VMEM((8, 4, 2, BLOCK, BLOCK), F32), pltpu.SemaphoreType.DMA((2, 8))
        ],
        compiler_params=pltpu.CompilerParams(vmem_limit_bytes=16 * MIB),
        cost_estimate=pl.CostEstimate(flops=0, bytes_accessed=8 * MIB, transcendentals=0),
        name="pack_cols",
    )(child_map, arrived)


def diag_block(values):
    rows = lax.broadcasted_iota(jnp.int32, (BLOCK, BLOCK), 0)
    cols = lax.broadcasted_iota(jnp.int32, (BLOCK, BLOCK), 1)
    return jnp.where(rows == cols, jnp.broadcast_to(values, (BLOCK, BLOCK)), 0.0)


def local_row(map_ref, c, h, n, p):
    shift = map_ref[c * 64] % 16
    i = (p + 8 * n - shift + 16) % 16
    return map_ref[c * 64 + 16 * h + i] // 8


def local_col(map_ref, c, t, q):
    shift = map_ref[c * 64] % 16
    return map_ref[c * 64 + 16 * t + (q - shift + 16) % 16] // 16


def panel_terms(front, diagonal, arrived, child_map):
    def kernel(map_ref, front_ref, diag_ref, in_ref, *refs):
        out_refs, head_ref, (total, buf, sems) = refs[:4], refs[4], refs[5:]
        p, q = lax.axis_index("prow"), lax.axis_index("pcol")
        x, w = q // 4, q % 4
        chosen, copies = [], []
        for e in range(2):
            for c in range(2):
                at = (4 * e + w - map_ref[c * 64] % 16 + 16) % 16
                chosen.append(map_ref[c * 64 + 16 * x + at] // 16 == 0)
                copies.append(
                    pltpu.make_async_copy(
                        in_ref.at[at // 4, c], buf.at[2 * e + c], sems.at[2 * e + c]
                    )
                )
                copies[-1].start()
        total[...] = jnp.zeros_like(total)

        @pl.when(x < 2)
        def _():
            for l in range(12):
                total[l % 2 * 2 + x, l // 2] = front_ref[l * BLOCK : (l + 1) * BLOCK, :]

        @pl.when(p == q)
        def _():
            total[x, 0] += diag_block(diag_ref[pl.ds(q, 1), :])

        for k in range(4):
            e, c = k // 2, k % 2
            copies[k].wait()

            @pl.when(chosen[k])
            def _():
                def add(i):
                    l = local_row(map_ref, c, i // 2, i % 2, p)
                    total[l % 2 * 2 + e, l // 2] += buf[k, i // 2, i % 2]

                pl.loop(0, 8)(add)

        for d in range(4):
            out_refs[d][...] = total[(x + d) % 4]
        for e in range(2):
            head_ref[e] = total[e, 0]

    return pl.pallas_call(
        kernel,
        out_shape=[jax.ShapeDtypeStruct((6, BLOCK, BLOCK), F32)] * 4
        + [jax.ShapeDtypeStruct((2, BLOCK, BLOCK), F32)],
        grid=(1,),
        in_specs=[
            pl.BlockSpec(memory_space=pltpu.SMEM),
            pl.BlockSpec((12 * BLOCK, BLOCK), lambda i: (0, 0)),
            pl.BlockSpec((96, BLOCK), lambda i: (0, 0)),
            pl.BlockSpec(memory_space=pl.ANY),
        ],
        out_specs=[pl.BlockSpec((6, BLOCK, BLOCK), lambda i: (0, 0, 0))] * 4
        + [pl.BlockSpec((2, BLOCK, BLOCK), lambda i: (0, 0, 0))],
        scratch_shapes=[
            pltpu.VMEM((4, 6, BLOCK, BLOCK), F32),
            pltpu.VMEM((4, 4, 2, BLOCK, BLOCK), F32),
            pltpu.SemaphoreType.DMA((4,)),
        ],
        compiler_params=pltpu.CompilerParams(vmem_limit_bytes=24 * MIB),
        cost_estimate=pl.CostEstimate(flops=0, bytes_accessed=5 * MIB, transcendentals=0),
        name="panel_terms",
    )(child_map, front, diagonal, arrived)


NN = ((1,), (0,))
NT = ((1,), (1,))
TN = ((0,), (0,))


def dot(a, b, contract):
    dims = (contract, ((), ()))
    return lax.dot_general(a, b, dims, precision=HIGHEST, preferred_element_type=F32)


def dot1(a, b, contract):
    return lax.dot_general(a, b, (contract, ((), ())), preferred_element_type=F32)


def split(value):
    high = value.astype(BF16)
    return high, (value - high.astype(F32)).astype(BF16)


def dot3(a, b, contract):
    (ah, al), (bh, bl) = a, b
    return dot1(ah, bl, contract) + dot1(al, bh, contract) + dot1(ah, bh, contract)


def square_iotas(size):
    shape = (size, size)
    return lax.broadcasted_iota(jnp.int32, shape, 0), lax.broadcasted_iota(jnp.int32, shape, 1)


def newton_factor(a_ref, x_ref):
    ri, ci = square_iotas(a_ref.shape[0])
    one = jnp.where(ri == ci, 1.0, 0.0)

    def lower_half(e):
        return jnp.where(ri > ci, e, jnp.where(ri == ci, 0.5 * e, 0.0))

    a = a_ref[...]
    pivots = jnp.where(ri == ci, a, 0.0)
    scale = lax.rsqrt(jnp.sum(pivots, axis=0, keepdims=True))
    f = split(jnp.where(ri > ci, a * lax.rsqrt(jnp.sum(pivots, axis=1, keepdims=True)) * scale, 0.0))
    x = (one - (f[0].astype(F32) + f[1].astype(F32)) + dot1(f[0], f[0], NN)) * scale
    xs = split(x)
    e = dot3(split(dot3(xs, split(a), NN)), xs, NT) - one
    f = split(lower_half(e))
    g = dot3(f, xs, NN)
    x = x - g + dot1(f[0], g.astype(BF16), NN)
    t = dot(x, a, NN)
    e = dot(t, x, NT) - one
    f = split(lower_half(e))
    x_ref[...] = x - dot3(f, split(x), NN)
    a_ref[...] = jnp.where(ci >= ri, t - dot3(f, split(t), NN), 0.0)
    return jnp.max(jnp.sum(jnp.abs(e), axis=1, keepdims=True))


def direct_factor(t_ref):
    size = t_ref.shape[0]
    ri, ci = square_iotas(size)
    lane = lax.broadcasted_iota(jnp.int32, (1, 2 * size), 1)
    down = lax.broadcasted_iota(jnp.int32, (size, 1), 0)

    def step(j):
        row = t_ref[pl.ds(j, 1), :]
        row = row * lax.rsqrt(jnp.sum(jnp.where(lane == j, row, 0.0), axis=1, keepdims=True))
        col = jnp.broadcast_to(row[:, :size], (size, size))
        col = jnp.sum(jnp.where(ri == ci, col, 0.0), axis=1, keepdims=True)
        t_ref[...] = t_ref[...] - jnp.where(down > j, col, 0.0) * row
        t_ref[pl.ds(j, 1), :] = row

    pl.loop(0, size)(step)


def head_factor(gathered):
    size, wide = HEAD * BLOCK, 2 * BLOCK

    def kernel(*refs):
        in_refs, (wh_ref, wl_ref, own_ref), scratch = refs[:8], refs[8:11], refs[11:]
        m_ref, u_ref, w_ref, a_ref, x_ref, t_ref = scratch
        p, q = lax.axis_index("prow"), lax.axis_index("pcol")

        def place(k, in_ref, core_back, y_back):
            core = (q + core_back) % 2
            y = (2 * (p // 4) + (q // 2) % 2 - y_back + 4) % 4
            z = (p - k // 2 + 4) % 4
            row, col = y // 2 * 4 + z, k % 2 * 4 + y % 2 * 2 + core
            rows = pl.ds(pl.multiple_of(row * BLOCK, BLOCK), BLOCK)
            cols = pl.ds(pl.multiple_of(col * BLOCK, BLOCK), BLOCK)
            m_ref[rows, cols] = in_ref[k]

        for at in range(8):
            pl.loop(0, 8)(
                functools.partial(place, in_ref=in_refs[at], core_back=at // 4, y_back=at % 4)
            )
        for i in range(HEAD):
            for j in range(i, HEAD):
                rows, cols = slice(i * BLOCK, (i + 1) * BLOCK), slice(j * BLOCK, (j + 1) * BLOCK)
                value = m_ref[cols, rows].T
                if i // 4 == j // 4:
                    value = 0.5 * (m_ref[rows, cols] + value)
                u_ref[rows, cols] = value
                if i // 2 == j // 2 and i != j:
                    u_ref[cols, rows] = value.T
        ri, ci = square_iotas(wide)
        for s in range(0, size, wide):
            e = s + wide
            a_ref[...] = u_ref[s:e, s:e]
            off = newton_factor(a_ref, x_ref)

            @pl.when(jnp.logical_not(off < 5e-4))
            def _():
                t_ref[:, :wide] = u_ref[s:e, s:e]
                t_ref[:, wide:] = jnp.where(ri == ci, 1.0, 0.0)
                direct_factor(t_ref)
                a_ref[...] = jnp.where(ci >= ri, t_ref[:, :wide], 0.0)
                x_ref[...] = jnp.where(ri >= ci, t_ref[:, wide:], 0.0)

            u_ref[s:e, s:e] = a_ref[...]
            w_ref[s:e, s:e] = x_ref[...]
            inverse = split(x_ref[...])
            if s:
                w_ref[s:e, 0:s] = dot3(inverse, split(w_ref[s:e, 0:s]), NN)
            done = split(w_ref[s:e, 0:e])
            wh_ref[s:e, 0:e], wl_ref[s:e, 0:e] = done
            if e < size:
                wh_ref[s:e, e:] = jnp.zeros((wide, size - e), BF16)
                wl_ref[s:e, e:] = jnp.zeros((wide, size - e), BF16)
                right = dot3(inverse, split(u_ref[s:e, e:]), NN)
                u_ref[s:e, e:] = right
                right = split(right)
                for j in range(e, size, wide):
                    left = tuple(v[:, j - e : j - e + wide] for v in right)
                    rest = tuple(v[:, j - e :] for v in right)
                    u_ref[j : j + wide, j:] = u_ref[j : j + wide, j:] - dot3(left, rest, TN)
                    change = dot3(left, done, TN)
                    if s:
                        w_ref[j : j + wide, 0:s] = w_ref[j : j + wide, 0:s] - change[:, 0:s]
                    w_ref[j : j + wide, s:e] = -change[:, s:e]
        own_ref[...] = jnp.zeros((BLOCK, BLOCK), F32)

        @pl.when(q <= p)
        def _():
            rows = pl.ds(pl.multiple_of(q * BLOCK, BLOCK), BLOCK)
            cols = pl.ds(pl.multiple_of(p * BLOCK, BLOCK), BLOCK)
            own_ref[...] = u_ref[rows, cols].T

    vmem = pl.BlockSpec(memory_space=pltpu.VMEM)
    square = pltpu.VMEM((size, size), F32)
    return pl.pallas_call(
        kernel,
        out_shape=[
            jax.ShapeDtypeStruct((size, size), BF16),
            jax.ShapeDtypeStruct((size, size), BF16),
            jax.ShapeDtypeStruct((BLOCK, BLOCK), F32),
        ],
        in_specs=[vmem] * 8,
        out_specs=[vmem] * 3,
        scratch_shapes=[square] * 3
        + [pltpu.VMEM((wide, wide), F32)] * 2
        + [pltpu.VMEM((wide, 2 * wide), F32)],
        compiler_params=pltpu.CompilerParams(vmem_limit_bytes=40 * MIB),
        cost_estimate=pl.CostEstimate(
            flops=20_000_000_000, bytes_accessed=8 * MIB, transcendentals=0
        ),
        name="head_factor",
    )(*gathered)


def solve_columns(col_panel, inverse):
    size, wide = HEAD * BLOCK, 6 * BLOCK

    def kernel(wh, wl, *refs):
        in_refs, out_refs, (ch, cl, yh, yl, sems) = refs[:8], refs[8:10], refs[10:]
        p, q = lax.axis_index("prow"), lax.axis_index("pcol")
        for k, in_ref in enumerate(in_refs):
            m = (p // 4 + k // 4) % 2 * 4 + (p + 4 - k % 4) % 4
            cols = pl.ds(pl.multiple_of(m * BLOCK, BLOCK), BLOCK)
            for s in range(6):
                rows = slice(s * BLOCK, (s + 1) * BLOCK)
                ch[rows, cols], cl[rows, cols] = split(in_ref[s])
        for i in range(0, size, 256):
            e = i + 256
            y = dot3((ch[:, 0:e], cl[:, 0:e]), (wh[i:e, 0:e], wl[i:e, 0:e]), NT)
            yh[:, i:e], yl[:, i:e] = split(y)
        for i in range(0, size, 256):
            e = i + 256
            z = dot3((yh[:, i:], yl[:, i:]), (wh[i:, i:e], wl[i:, i:e]), NN)
            ch[:, i:e], cl[:, i:e] = split(z)

        @pl.when(q < HEAD)
        def _():
            rows = pl.ds(pl.multiple_of(q * BLOCK, BLOCK), BLOCK)
            ch[0:BLOCK, :] = -wh[rows, :]
            cl[0:BLOCK, :] = -wl[rows, :]

        stores = [
            pltpu.make_async_copy(ch, out_refs[0], sems.at[0]),
            pltpu.make_async_copy(cl, out_refs[1], sems.at[1]),
        ]
        for store in stores:
            store.start()
        for store in stores:
            store.wait()

    vmem = pl.BlockSpec(memory_space=pltpu.VMEM)
    return pl.pallas_call(
        kernel,
        out_shape=[jax.ShapeDtypeStruct((wide, size), BF16)] * 2,
        in_specs=[vmem] * 10,
        out_specs=[pl.BlockSpec(memory_space=pltpu.HBM)] * 2,
        scratch_shapes=[pltpu.VMEM((wide, size), BF16)] * 4 + [pltpu.SemaphoreType.DMA((2,))],
        compiler_params=pltpu.CompilerParams(vmem_limit_bytes=32 * MIB),
        cost_estimate=pl.CostEstimate(
            flops=8_000_000_000, bytes_accessed=10 * MIB, transcendentals=0
        ),
        name="solve_columns",
    )(*inverse, *col_panel)


def finish(front, diagonal, arrived, row_panel, solved, own, child_map):
    size, group, wide = HEAD * BLOCK, 4, 6 * BLOCK

    def kernel(
        map_ref, own_ref, diag_ref, row_ref, front_ref, *refs
    ):
        sources, out_ref, (sh, sl, *in_refs), sems = refs[:6], refs[6], refs[7:13], refs[13]
        step = pl.program_id(0)

        def load(k):
            return pltpu.make_async_copy(sources[k], (sh, sl, *in_refs)[k], sems.at[k])

        @pl.when(step == 0)
        def _():
            for k in range(6):
                load(k).start()

        p, q = lax.axis_index("prow"), lax.axis_index("pcol")
        out_ref[...] = front_ref[...]
        for s in range(6):
            l = 2 * s + jnp.where(q >= 8, 1, 0)

            @pl.when((q % 8 == p) & (l // group == step))
            def _():
                rows = pl.ds(pl.multiple_of((l % group) * BLOCK, BLOCK), BLOCK)
                out_ref[rows, s * BLOCK : (s + 1) * BLOCK] += diag_block(
                    diag_ref[pl.ds(16 * s + q, 1), :]
                )

        @pl.when(step == 0)
        def _():
            for k in range(6):
                load(k).wait()

        for c in range(2):
            places = [local_col(map_ref, c, (q // 4 + 4 - d) % 4, q) for d in range(4)]

            def add(k):
                l = local_row(map_ref, c, k // 2, k % 2, p)

                @pl.when(l // group == step)
                def _():
                    rows = pl.ds(pl.multiple_of((l % group) * BLOCK, BLOCK), BLOCK)
                    for d in range(4):
                        cols = pl.ds(pl.multiple_of(places[d] * BLOCK, BLOCK), BLOCK)
                        out_ref[rows, cols] += in_refs[d][c, k // 2, k % 2]

            pl.loop(0, 8)(add)

        @pl.when(q < HEAD)
        def _():
            out_ref[:, 0:BLOCK] = jnp.zeros((group * BLOCK, BLOCK), F32)

        rows = []
        for k in range(group):
            rows.append(
                jnp.concatenate([row_ref[k % 2 * 8 + m, k // 2] for m in range(HEAD)], axis=1)
            )
        rows = split(jnp.concatenate(rows, axis=0))
        for j in range(0, wide, 256):
            e = j + 256
            out_ref[:, j:e] -= dot3(rows, (sh[j:e, :], sl[j:e, :]), NT)

        @pl.when(step == 0)
        def _():
            out_ref[0:BLOCK, :] = jnp.zeros((BLOCK, wide), F32)
            out_ref[0:BLOCK, 0:BLOCK] = own_ref[...]

    def whole(*shape):
        return pl.BlockSpec(shape, lambda i: (0,) * len(shape), pipeline_mode=pl.Buffered(1))

    return pl.pallas_call(
        kernel,
        out_shape=jax.ShapeDtypeStruct((12 * BLOCK, wide), F32),
        grid=(12 // group,),
        in_specs=[
            pl.BlockSpec(memory_space=pltpu.SMEM),
            whole(BLOCK, BLOCK),
            whole(96, BLOCK),
            pl.BlockSpec((16, group // 2, BLOCK, BLOCK), lambda i: (0, i, 0, 0)),
            pl.BlockSpec((group * BLOCK, wide), lambda i: (i, 0)),
            *[pl.BlockSpec(memory_space=pltpu.HBM)] * 6,
        ],
        out_specs=pl.BlockSpec((group * BLOCK, wide), lambda i: (i, 0)),
        scratch_shapes=[pltpu.VMEM((wide, size), BF16)] * 2
        + [pltpu.VMEM((2, 4, 2, BLOCK, BLOCK), F32)] * 4
        + [pltpu.SemaphoreType.DMA((6,))],
        compiler_params=pltpu.CompilerParams(vmem_limit_bytes=60 * MIB),
        cost_estimate=pl.CostEstimate(
            flops=8_000_000_000, bytes_accessed=24 * MIB, transcendentals=0
        ),
        name="finish",
    )(child_map, own, diagonal, row_panel, front, *solved, *arrived)


def ahead_x(d):
    return [(4 * x + w, 4 * ((x + d) % 4) + w) for x in range(4) for w in range(4)]


def ahead_z(d):
    return [(4 * h + z, 4 * h + (z + d) % 4) for h in range(2) for z in range(4)]


def ahead_y(d):
    def rank(y, z, x, core):
        return (4 * (y // 2) + z) * 16 + 4 * x + 2 * (y % 2) + core

    return [
        (rank(y, z, x, core), rank((y + d) % 4, z, x, core))
        for y in range(4) for z in range(4) for x in range(4) for core in range(2)
    ]


OTHER_CORE = [(k, k ^ 1) for k in range(16)]
BOTH = ("prow", "pcol")


def sum_head(terms):
    held = terms
    for d in (1, 2, 3):
        held = held + lax.ppermute(terms, "pcol", ahead_x(d))
    return all_z(held)


def gather_head(along_z, beside):
    held = jnp.concatenate(along_z, axis=0)
    along_y = [held] + [lax.ppermute(held, BOTH, ahead_y(d)) for d in (1, 2, 3)]
    along_y, beside = lax.optimization_barrier((along_y, beside))
    return along_y + [lax.ppermute(part, "pcol", OTHER_CORE) for part in along_y], beside


def all_z(value):
    return [value] + [lax.ppermute(value, "prow", ahead_z(d)) for d in (1, 2, 3)]


def turn(piece):
    return lax.ppermute(
        piece,
        BOTH,
        [
            (p * 16 + (2 * par + e) * 4 + w, (4 * e + w) * 16 + p + 8 * par)
            for p in range(8) for par in range(2) for e in range(2) for w in range(4)
        ],
    )


def per_device(front, diagonal, child, child_map):
    child_map = child_map.reshape(128)
    diagonal = diagonal.reshape(96, BLOCK)
    sent = pack_rows(child, child_map).reshape(64, BLOCK, BLOCK)
    sent = lax.all_to_all(sent, BOTH, 0, 0, axis_index_groups=PLANE_GROUPS, tiled=True)
    sent = sent.reshape(4, 2, 4, 2, BLOCK, BLOCK)
    *terms, head_terms = panel_terms(front, diagonal, sent, child_map)
    behind = [lax.ppermute(terms[d], "pcol", ahead_x(d)) for d in (1, 2, 3)]
    head = sum_head(head_terms)
    blocks = pack_cols(sent, child_map)
    behind, head = lax.optimization_barrier((behind, head))
    piece = terms[0] + behind[0] + behind[1] + behind[2]
    arrived = [blocks[0]]
    for d in (1, 2, 3):
        arrived.append(lax.ppermute(blocks[d], "pcol", ahead_x(d)))
    row_panel = lax.all_gather(piece, "pcol")
    turned = turn(piece)
    turned, head = lax.optimization_barrier((turned, head))
    other = lax.ppermute(turned, "prow", [(p, p ^ 4) for p in range(8)])
    col_panel = all_z(turned)
    gathered, (arrived[1], arrived[3], col_panel, other) = gather_head(
        head, (arrived[1], arrived[3], col_panel, other)
    )
    col_panel += all_z(other)
    gathered, arrived = lax.optimization_barrier((gathered, arrived))
    *inverse, own = head_factor(gathered)
    solved = solve_columns(col_panel, inverse)
    return finish(front, diagonal, arrived, row_panel, solved, own, child_map)


def solution(mesh):
    return jax.shard_map(
        per_device,
        mesh=mesh,
        in_specs=(P("prow", "pcol"), P(), P("prow", "pcol"), P()),
        out_specs=P("prow", "pcol"),
        check_vma=False,
    )
```

```python
import functools

import jax
import jax.numpy as jnp
from jax import lax
from jax.experimental import pallas as pl
from jax.experimental.pallas import tpu as pltpu
from jax.sharding import PartitionSpec as P

BLOCK = 128
HEAD = 8
F32 = jnp.float32
BF16 = jnp.bfloat16
HIGHEST = lax.Precision.HIGHEST
MIB = 1024 * 1024

X_GROUPS = [[4 * x + w for x in range(4)] for w in range(4)]
PLANE_GROUPS = [[16 * p + 4 * x + w for w in range(4) for p in range(8)] for x in range(4)]


def pack_rows(child, child_map):
    def kernel(map_ref, child_ref, out_ref, buf, turned, sems):
        c = lax.axis_index("prow") // 4
        shift = map_ref[c * 64] % 16

        def fetch(i):
            rows = pl.ds(pl.multiple_of(i * BLOCK, BLOCK), BLOCK)
            return pltpu.make_async_copy(child_ref.at[rows], buf.at[i], sems.at[0, i])

        def store(i):
            residue = (i + shift) % 16
            return pltpu.make_async_copy(
                turned.at[i], out_ref.at[:, residue % 8, residue // 8], sems.at[1, i]
            )

        def forward(i):
            fetch(i).wait()
            for w in range(4):
                b = (w - shift + 16) % 4
                turned[i, w] = buf[i, :, pl.ds(pl.multiple_of(b * BLOCK, BLOCK), BLOCK)]
            store(i).start()

        pl.loop(0, 16)(lambda i: fetch(i).start())
        pl.loop(0, 16)(forward)
        pl.loop(0, 16)(lambda i: store(i).wait())

    return pl.pallas_call(
        kernel,
        out_shape=jax.ShapeDtypeStruct((4, 8, 2, BLOCK, BLOCK), F32),
        in_specs=[pl.BlockSpec(memory_space=pltpu.SMEM), pl.BlockSpec(memory_space=pl.ANY)],
        out_specs=pl.BlockSpec(memory_space=pl.ANY),
        scratch_shapes=[
            pltpu.VMEM((16, BLOCK, 4 * BLOCK), F32),
            pltpu.VMEM((16, 4, BLOCK, BLOCK), F32),
            pltpu.SemaphoreType.DMA((2, 16)),
        ],
        compiler_params=pltpu.CompilerParams(vmem_limit_bytes=16 * MIB),
        cost_estimate=pl.CostEstimate(flops=0, bytes_accessed=8 * MIB, transcendentals=0),
        name="pack_rows",
    )(child_map, child)


def pack_cols(arrived, child_map):
    def kernel(map_ref, in_ref, out_ref, buf, sems):
        w = lax.axis_index("pcol") % 4

        def fetch(k):
            c = k % 2
            column = 4 * (k // 2) + w
            a = ((column - map_ref[c * 64] % 16 + 16) % 16) // 4
            return pltpu.make_async_copy(in_ref.at[a, c], buf.at[k], sems.at[0, k])

        def store(k):
            return pltpu.make_async_copy(buf.at[k], out_ref.at[k // 2, k % 2], sems.at[1, k])

        for k in range(8):
            fetch(k).start()
        for k in range(8):
            fetch(k).wait()
            store(k).start()
        for k in range(8):
            store(k).wait()

    return pl.pallas_call(
        kernel,
        out_shape=jax.ShapeDtypeStruct((4, 2, 4, 2, BLOCK, BLOCK), F32),
        in_specs=[pl.BlockSpec(memory_space=pltpu.SMEM), pl.BlockSpec(memory_space=pl.ANY)],
        out_specs=pl.BlockSpec(memory_space=pltpu.HBM),
        scratch_shapes=[
            pltpu.VMEM((8, 4, 2, BLOCK, BLOCK), F32), pltpu.SemaphoreType.DMA((2, 8))
        ],
        compiler_params=pltpu.CompilerParams(vmem_limit_bytes=16 * MIB),
        cost_estimate=pl.CostEstimate(flops=0, bytes_accessed=8 * MIB, transcendentals=0),
        name="pack_cols",
    )(child_map, arrived)


def diag_block(values):
    rows = lax.broadcasted_iota(jnp.int32, (BLOCK, BLOCK), 0)
    cols = lax.broadcasted_iota(jnp.int32, (BLOCK, BLOCK), 1)
    return jnp.where(rows == cols, jnp.broadcast_to(values, (BLOCK, BLOCK)), 0.0)


def local_row(map_ref, c, h, n, p):
    shift = map_ref[c * 64] % 16
    i = (p + 8 * n - shift + 16) % 16
    return map_ref[c * 64 + 16 * h + i] // 8


def local_col(map_ref, c, t, q):
    shift = map_ref[c * 64] % 16
    return map_ref[c * 64 + 16 * t + (q - shift + 16) % 16] // 16


def panel_terms(front, diagonal, arrived, child_map):
    def kernel(map_ref, front_ref, diag_ref, in_ref, *refs):
        out_refs, head_ref, (total, buf, sems) = refs[:4], refs[4], refs[5:]
        p, q = lax.axis_index("prow"), lax.axis_index("pcol")
        x, w = q // 4, q % 4
        chosen, copies = [], []
        for e in range(2):
            for c in range(2):
                at = (4 * e + w - map_ref[c * 64] % 16 + 16) % 16
                chosen.append(map_ref[c * 64 + 16 * x + at] // 16 == 0)
                copies.append(
                    pltpu.make_async_copy(
                        in_ref.at[at // 4, c], buf.at[2 * e + c], sems.at[2 * e + c]
                    )
                )
                copies[-1].start()
        total[...] = jnp.zeros_like(total)

        @pl.when(x < 2)
        def _():
            for l in range(12):
                total[l % 2 * 2 + x, l // 2] = front_ref[l * BLOCK : (l + 1) * BLOCK, :]

        @pl.when(p == q)
        def _():
            total[x, 0] += diag_block(diag_ref[pl.ds(q, 1), :])

        for k in range(4):
            e, c = k // 2, k % 2
            copies[k].wait()

            @pl.when(chosen[k])
            def _():
                def add(i):
                    l = local_row(map_ref, c, i // 2, i % 2, p)
                    total[l % 2 * 2 + e, l // 2] += buf[k, i // 2, i % 2]

                pl.loop(0, 8)(add)

        for d in range(4):
            out_refs[d][...] = total[(x + d) % 4]
        for e in range(2):
            head_ref[e] = total[e, 0]

    return pl.pallas_call(
        kernel,
        out_shape=[jax.ShapeDtypeStruct((6, BLOCK, BLOCK), F32)] * 4
        + [jax.ShapeDtypeStruct((2, BLOCK, BLOCK), F32)],
        grid=(1,),
        in_specs=[
            pl.BlockSpec(memory_space=pltpu.SMEM),
            pl.BlockSpec((12 * BLOCK, BLOCK), lambda i: (0, 0)),
            pl.BlockSpec((96, BLOCK), lambda i: (0, 0)),
            pl.BlockSpec(memory_space=pl.ANY),
        ],
        out_specs=[pl.BlockSpec((6, BLOCK, BLOCK), lambda i: (0, 0, 0))] * 4
        + [pl.BlockSpec((2, BLOCK, BLOCK), lambda i: (0, 0, 0))],
        scratch_shapes=[
            pltpu.VMEM((4, 6, BLOCK, BLOCK), F32),
            pltpu.VMEM((4, 4, 2, BLOCK, BLOCK), F32),
            pltpu.SemaphoreType.DMA((4,)),
        ],
        compiler_params=pltpu.CompilerParams(vmem_limit_bytes=24 * MIB),
        cost_estimate=pl.CostEstimate(flops=0, bytes_accessed=5 * MIB, transcendentals=0),
        name="panel_terms",
    )(child_map, front, diagonal, arrived)


def panel_column(front, diagonal, arrived, child_map):
    def kernel(map_ref, front_ref, diag_ref, in_ref, out_ref, buf, sems):
        p, q = lax.axis_index("prow"), lax.axis_index("pcol")
        found, copies = [], []
        for c in range(2):
            slot = jnp.int32(-1)
            for t in range(4):
                slot = jnp.where(local_col(map_ref, c, t, q) == 0, t, slot)
            found.append(slot)
            at = jnp.maximum(slot, 0)
            copy = pltpu.make_async_copy(in_ref.at[at, c], buf.at[c], sems.at[c])
            copy.start()
            copies.append(copy)
        for l in range(12):
            out_ref[l % 2, l // 2] = front_ref[l * BLOCK : (l + 1) * BLOCK, :]

        @pl.when(p == q)
        def _():
            out_ref[0, 0] += diag_block(diag_ref[pl.ds(q, 1), :])

        for c in range(2):
            copies[c].wait()

            @pl.when(found[c] >= 0)
            def _():
                def add(k):
                    l = local_row(map_ref, c, k // 2, k % 2, p)
                    out_ref[l % 2, l // 2] += buf[c, k // 2, k % 2]

                pl.loop(0, 8)(add)

    return pl.pallas_call(
        kernel,
        out_shape=jax.ShapeDtypeStruct((2, 6, BLOCK, BLOCK), F32),
        grid=(1,),
        in_specs=[
            pl.BlockSpec(memory_space=pltpu.SMEM),
            pl.BlockSpec((12 * BLOCK, BLOCK), lambda i: (0, 0)),
            pl.BlockSpec((96, BLOCK), lambda i: (0, 0)),
            pl.BlockSpec(memory_space=pl.ANY),
        ],
        out_specs=pl.BlockSpec((2, 6, BLOCK, BLOCK), lambda i: (0, 0, 0, 0)),
        scratch_shapes=[pltpu.VMEM((2, 4, 2, BLOCK, BLOCK), F32), pltpu.SemaphoreType.DMA((2,))],
        compiler_params=pltpu.CompilerParams(vmem_limit_bytes=24 * MIB),
        cost_estimate=pl.CostEstimate(flops=0, bytes_accessed=3 * MIB, transcendentals=0),
        name="panel_column",
    )(child_map, front, diagonal, arrived)


NN = ((1,), (0,))
NT = ((1,), (1,))
TN = ((0,), (0,))


def dot(a, b, contract):
    dims = (contract, ((), ()))
    return lax.dot_general(a, b, dims, precision=HIGHEST, preferred_element_type=F32)


def dot1(a, b, contract):
    return lax.dot_general(a, b, (contract, ((), ())), preferred_element_type=F32)


def split(value):
    high = value.astype(BF16)
    return high, (value - high.astype(F32)).astype(BF16)


def dot3(a, b, contract):
    (ah, al), (bh, bl) = a, b
    return dot1(ah, bl, contract) + dot1(al, bh, contract) + dot1(ah, bh, contract)


def square_iotas(size):
    shape = (size, size)
    return lax.broadcasted_iota(jnp.int32, shape, 0), lax.broadcasted_iota(jnp.int32, shape, 1)


def newton_factor(a_ref, x_ref):
    ri, ci = square_iotas(a_ref.shape[0])
    one = jnp.where(ri == ci, 1.0, 0.0)

    def lower_half(e):
        return jnp.where(ri > ci, e, jnp.where(ri == ci, 0.5 * e, 0.0))

    a = a_ref[...]
    pivots = jnp.where(ri == ci, a, 0.0)
    scale = lax.rsqrt(jnp.sum(pivots, axis=0, keepdims=True))
    f = split(jnp.where(ri > ci, a * lax.rsqrt(jnp.sum(pivots, axis=1, keepdims=True)) * scale, 0.0))
    x = (one - (f[0].astype(F32) + f[1].astype(F32)) + dot1(f[0], f[0], NN)) * scale
    xs = split(x)
    e = dot3(split(dot3(xs, split(a), NN)), xs, NT) - one
    f = split(lower_half(e))
    g = dot3(f, xs, NN)
    x = x - g + dot1(f[0], g.astype(BF16), NN)
    t = dot(x, a, NN)
    e = dot(t, x, NT) - one
    f = split(lower_half(e))
    x_ref[...] = x - dot3(f, split(x), NN)
    a_ref[...] = jnp.where(ci >= ri, t - dot3(f, split(t), NN), 0.0)
    return jnp.max(jnp.sum(jnp.abs(e), axis=1, keepdims=True))


def direct_factor(t_ref):
    size = t_ref.shape[0]
    ri, ci = square_iotas(size)
    lane = lax.broadcasted_iota(jnp.int32, (1, 2 * size), 1)
    down = lax.broadcasted_iota(jnp.int32, (size, 1), 0)

    def step(j):
        row = t_ref[pl.ds(j, 1), :]
        row = row * lax.rsqrt(jnp.sum(jnp.where(lane == j, row, 0.0), axis=1, keepdims=True))
        col = jnp.broadcast_to(row[:, :size], (size, size))
        col = jnp.sum(jnp.where(ri == ci, col, 0.0), axis=1, keepdims=True)
        t_ref[...] = t_ref[...] - jnp.where(down > j, col, 0.0) * row
        t_ref[pl.ds(j, 1), :] = row

    pl.loop(0, size)(step)


def head_factor(gathered):
    size, wide = HEAD * BLOCK, 2 * BLOCK

    def kernel(*refs):
        in_refs, (wh_ref, wl_ref, own_ref), scratch = refs[:8], refs[8:11], refs[11:]
        m_ref, u_ref, w_ref, a_ref, x_ref, t_ref = scratch
        p, q = lax.axis_index("prow"), lax.axis_index("pcol")

        def place(k, in_ref, core_back, y_back):
            core = (q + core_back) % 2
            y = (2 * (p // 4) + (q // 2) % 2 - y_back + 4) % 4
            z = (p - k // 2 + 4) % 4
            row, col = y // 2 * 4 + z, k % 2 * 4 + y % 2 * 2 + core
            rows = pl.ds(pl.multiple_of(row * BLOCK, BLOCK), BLOCK)
            cols = pl.ds(pl.multiple_of(col * BLOCK, BLOCK), BLOCK)
            m_ref[rows, cols] = in_ref[k]

        for at in range(8):
            pl.loop(0, 8)(
                functools.partial(place, in_ref=in_refs[at], core_back=at // 4, y_back=at % 4)
            )
        for i in range(HEAD):
            for j in range(i, HEAD):
                rows, cols = slice(i * BLOCK, (i + 1) * BLOCK), slice(j * BLOCK, (j + 1) * BLOCK)
                value = m_ref[cols, rows].T
                if i // 4 == j // 4:
                    value = 0.5 * (m_ref[rows, cols] + value)
                u_ref[rows, cols] = value
                if i // 2 == j // 2 and i != j:
                    u_ref[cols, rows] = value.T
        ri, ci = square_iotas(wide)
        for s in range(0, size, wide):
            e = s + wide
            a_ref[...] = u_ref[s:e, s:e]
            off = newton_factor(a_ref, x_ref)

            @pl.when(jnp.logical_not(off < 5e-4))
            def _():
                t_ref[:, :wide] = u_ref[s:e, s:e]
                t_ref[:, wide:] = jnp.where(ri == ci, 1.0, 0.0)
                direct_factor(t_ref)
                a_ref[...] = jnp.where(ci >= ri, t_ref[:, :wide], 0.0)
                x_ref[...] = jnp.where(ri >= ci, t_ref[:, wide:], 0.0)

            u_ref[s:e, s:e] = a_ref[...]
            w_ref[s:e, s:e] = x_ref[...]
            inverse = split(x_ref[...])
            if s:
                w_ref[s:e, 0:s] = dot3(inverse, split(w_ref[s:e, 0:s]), NN)
            done = split(w_ref[s:e, 0:e])
            wh_ref[s:e, 0:e], wl_ref[s:e, 0:e] = done
            if e < size:
                wh_ref[s:e, e:] = jnp.zeros((wide, size - e), BF16)
                wl_ref[s:e, e:] = jnp.zeros((wide, size - e), BF16)
                right = dot3(inverse, split(u_ref[s:e, e:]), NN)
                u_ref[s:e, e:] = right
                right = split(right)
                for j in range(e, size, wide):
                    left = tuple(v[:, j - e : j - e + wide] for v in right)
                    rest = tuple(v[:, j - e :] for v in right)
                    u_ref[j : j + wide, j:] = u_ref[j : j + wide, j:] - dot3(left, rest, TN)
                    change = dot3(left, done, TN)
                    if s:
                        w_ref[j : j + wide, 0:s] = w_ref[j : j + wide, 0:s] - change[:, 0:s]
                    w_ref[j : j + wide, s:e] = -change[:, s:e]
        own_ref[...] = jnp.zeros((BLOCK, BLOCK), F32)

        @pl.when(q <= p)
        def _():
            rows = pl.ds(pl.multiple_of(q * BLOCK, BLOCK), BLOCK)
            cols = pl.ds(pl.multiple_of(p * BLOCK, BLOCK), BLOCK)
            own_ref[...] = u_ref[rows, cols].T

    vmem = pl.BlockSpec(memory_space=pltpu.VMEM)
    square = pltpu.VMEM((size, size), F32)
    return pl.pallas_call(
        kernel,
        out_shape=[
            jax.ShapeDtypeStruct((size, size), BF16),
            jax.ShapeDtypeStruct((size, size), BF16),
            jax.ShapeDtypeStruct((BLOCK, BLOCK), F32),
        ],
        in_specs=[vmem] * 8,
        out_specs=[vmem] * 3,
        scratch_shapes=[square] * 3
        + [pltpu.VMEM((wide, wide), F32)] * 2
        + [pltpu.VMEM((wide, 2 * wide), F32)],
        compiler_params=pltpu.CompilerParams(vmem_limit_bytes=40 * MIB),
        cost_estimate=pl.CostEstimate(
            flops=20_000_000_000, bytes_accessed=8 * MIB, transcendentals=0
        ),
        name="head_factor",
    )(*gathered)


def solve_columns(col_panel, inverse):
    size, wide = HEAD * BLOCK, 6 * BLOCK

    def kernel(wh, wl, *refs):
        in_refs, out_refs, (ch, cl, yh, yl, sems) = refs[:8], refs[8:10], refs[10:]
        p, q = lax.axis_index("prow"), lax.axis_index("pcol")
        for k, in_ref in enumerate(in_refs):
            m = (p // 4 + k // 4) % 2 * 4 + (p + 4 - k % 4) % 4
            cols = pl.ds(pl.multiple_of(m * BLOCK, BLOCK), BLOCK)
            for s in range(6):
                rows = slice(s * BLOCK, (s + 1) * BLOCK)
                ch[rows, cols], cl[rows, cols] = split(in_ref[s])
        for i in range(0, size, 256):
            e = i + 256
            y = dot3((ch[:, 0:e], cl[:, 0:e]), (wh[i:e, 0:e], wl[i:e, 0:e]), NT)
            yh[:, i:e], yl[:, i:e] = split(y)
        for i in range(0, size, 256):
            e = i + 256
            z = dot3((yh[:, i:], yl[:, i:]), (wh[i:, i:e], wl[i:, i:e]), NN)
            ch[:, i:e], cl[:, i:e] = split(z)

        @pl.when(q < HEAD)
        def _():
            rows = pl.ds(pl.multiple_of(q * BLOCK, BLOCK), BLOCK)
            ch[0:BLOCK, :] = -wh[rows, :]
            cl[0:BLOCK, :] = -wl[rows, :]

        stores = [
            pltpu.make_async_copy(ch, out_refs[0], sems.at[0]),
            pltpu.make_async_copy(cl, out_refs[1], sems.at[1]),
        ]
        for store in stores:
            store.start()
        for store in stores:
            store.wait()

    vmem = pl.BlockSpec(memory_space=pltpu.VMEM)
    return pl.pallas_call(
        kernel,
        out_shape=[jax.ShapeDtypeStruct((wide, size), BF16)] * 2,
        in_specs=[vmem] * 10,
        out_specs=[pl.BlockSpec(memory_space=pltpu.HBM)] * 2,
        scratch_shapes=[pltpu.VMEM((wide, size), BF16)] * 4 + [pltpu.SemaphoreType.DMA((2,))],
        compiler_params=pltpu.CompilerParams(vmem_limit_bytes=32 * MIB),
        cost_estimate=pl.CostEstimate(
            flops=8_000_000_000, bytes_accessed=10 * MIB, transcendentals=0
        ),
        name="solve_columns",
    )(*inverse, *col_panel)


def finish(front, diagonal, arrived, row_panel, solved, own, child_map):
    size, group, wide = HEAD * BLOCK, 4, 6 * BLOCK

    def kernel(
        map_ref, own_ref, diag_ref, row_ref, front_ref, *refs
    ):
        sources, out_ref, targets, sems = refs[:3], refs[3], refs[4:7], refs[7]
        sh, sl, blocks = targets
        step = pl.program_id(0)

        def load(k):
            return pltpu.make_async_copy(sources[k], targets[k], sems.at[k])

        @pl.when(step == 0)
        def _():
            for k in range(3):
                load(k).start()

        p, q = lax.axis_index("prow"), lax.axis_index("pcol")
        out_ref[...] = front_ref[...]
        for s in range(6):
            l = 2 * s + jnp.where(q >= 8, 1, 0)

            @pl.when((q % 8 == p) & (l // group == step))
            def _():
                rows = pl.ds(pl.multiple_of((l % group) * BLOCK, BLOCK), BLOCK)
                out_ref[rows, s * BLOCK : (s + 1) * BLOCK] += diag_block(
                    diag_ref[pl.ds(16 * s + q, 1), :]
                )

        @pl.when(step == 0)
        def _():
            for k in range(3):
                load(k).wait()

        for c in range(2):
            places = [local_col(map_ref, c, t, q) for t in range(4)]

            def add(k):
                l = local_row(map_ref, c, k // 2, k % 2, p)

                @pl.when(l // group == step)
                def _():
                    rows = pl.ds(pl.multiple_of((l % group) * BLOCK, BLOCK), BLOCK)
                    for t in range(4):
                        cols = pl.ds(pl.multiple_of(places[t] * BLOCK, BLOCK), BLOCK)
                        out_ref[rows, cols] += blocks[t, c, k // 2, k % 2]

            pl.loop(0, 8)(add)

        @pl.when(q < HEAD)
        def _():
            out_ref[:, 0:BLOCK] = jnp.zeros((group * BLOCK, BLOCK), F32)

        rows = []
        for k in range(group):
            rows.append(
                jnp.concatenate([row_ref[k % 2 * 8 + m, k // 2] for m in range(HEAD)], axis=1)
            )
        rows = split(jnp.concatenate(rows, axis=0))
        for j in range(0, wide, 256):
            e = j + 256
            out_ref[:, j:e] -= dot3(rows, (sh[j:e, :], sl[j:e, :]), NT)

        @pl.when(step == 0)
        def _():
            out_ref[0:BLOCK, :] = jnp.zeros((BLOCK, wide), F32)
            out_ref[0:BLOCK, 0:BLOCK] = own_ref[...]

    def whole(*shape):
        return pl.BlockSpec(shape, lambda i: (0,) * len(shape), pipeline_mode=pl.Buffered(1))

    return pl.pallas_call(
        kernel,
        out_shape=jax.ShapeDtypeStruct((12 * BLOCK, wide), F32),
        grid=(12 // group,),
        in_specs=[
            pl.BlockSpec(memory_space=pltpu.SMEM),
            whole(BLOCK, BLOCK),
            whole(96, BLOCK),
            pl.BlockSpec((16, group // 2, BLOCK, BLOCK), lambda i: (0, i, 0, 0)),
            pl.BlockSpec((group * BLOCK, wide), lambda i: (i, 0)),
            *[pl.BlockSpec(memory_space=pltpu.HBM)] * 3,
        ],
        out_specs=pl.BlockSpec((group * BLOCK, wide), lambda i: (i, 0)),
        scratch_shapes=[pltpu.VMEM((wide, size), BF16)] * 2
        + [pltpu.VMEM((4, 2, 4, 2, BLOCK, BLOCK), F32), pltpu.SemaphoreType.DMA((3,))],
        compiler_params=pltpu.CompilerParams(vmem_limit_bytes=60 * MIB),
        cost_estimate=pl.CostEstimate(
            flops=8_000_000_000, bytes_accessed=24 * MIB, transcendentals=0
        ),
        name="finish",
    )(child_map, own, diagonal, row_panel, front, *solved, arrived)


def ahead_x(d):
    return [(4 * x + w, 4 * ((x + d) % 4) + w) for x in range(4) for w in range(4)]


def ahead_z(d):
    return [(4 * h + z, 4 * h + (z + d) % 4) for h in range(2) for z in range(4)]


def ahead_y(d):
    def rank(y, z, x, core):
        return (4 * (y // 2) + z) * 16 + 4 * x + 2 * (y % 2) + core

    return [
        (rank(y, z, x, core), rank((y + d) % 4, z, x, core))
        for y in range(4) for z in range(4) for x in range(4) for core in range(2)
    ]


OTHER_CORE = [(k, k ^ 1) for k in range(16)]
BOTH = ("prow", "pcol")


def sum_head(terms):
    held = terms
    for d in (1, 2, 3):
        held = held + lax.ppermute(terms, "pcol", ahead_x(d))
    return all_z(held)


def gather_head(along_z):
    held = jnp.concatenate(along_z, axis=0)
    along_y = [held] + [lax.ppermute(held, BOTH, ahead_y(d)) for d in (1, 2, 3)]
    return along_y + [lax.ppermute(part, "pcol", OTHER_CORE) for part in along_y]


def all_z(value):
    return [value] + [lax.ppermute(value, "prow", ahead_z(d)) for d in (1, 2, 3)]


def turn(piece):
    return lax.ppermute(
        piece,
        BOTH,
        [
            (p * 16 + (2 * par + e) * 4 + w, (4 * e + w) * 16 + p + 8 * par)
            for p in range(8) for par in range(2) for e in range(2) for w in range(4)
        ],
    )


def per_device(front, diagonal, child, child_map):
    x = lax.axis_index("pcol") // 4
    child_map = child_map.reshape(128)
    diagonal = diagonal.reshape(96, BLOCK)
    sent = pack_rows(child, child_map).reshape(64, BLOCK, BLOCK)
    sent = lax.all_to_all(sent, BOTH, 0, 0, axis_index_groups=PLANE_GROUPS, tiled=True)
    sent = sent.reshape(4, 2, 4, 2, BLOCK, BLOCK)
    blocks = pack_cols(sent, child_map).reshape(64, BLOCK, BLOCK)
    *_, head_terms = panel_terms(front, diagonal, sent, child_map)
    blocks, head_terms = lax.optimization_barrier((blocks, head_terms))
    arrived = lax.all_to_all(blocks, "pcol", 0, 0, axis_index_groups=X_GROUPS, tiled=True)
    arrived = arrived.reshape(4, 2, 4, 2, BLOCK, BLOCK)
    *inverse, own = head_factor(gather_head(sum_head(head_terms)))
    arrived, inverse = lax.optimization_barrier((arrived, inverse))
    column = panel_column(front, diagonal, arrived, child_map)
    odd = lax.ppermute(
        column[1], "pcol", [(4 * k + w, 4 * (k + 2) + w) for k in (0, 1) for w in range(4)]
    )
    piece = jnp.where(x < 2, column[0], odd)
    row_panel = lax.all_gather(piece, "pcol")
    turned = turn(piece)
    other = lax.ppermute(turned, "prow", [(p, p ^ 4) for p in range(8)])
    col_panel = all_z(turned) + all_z(other)
    solved = solve_columns(col_panel, inverse)
    return finish(front, diagonal, arrived, row_panel, solved, own, child_map)


def solution(mesh):
    return jax.shard_map(
        per_device,
        mesh=mesh,
        in_specs=(P("prow", "pcol"), P(), P("prow", "pcol"), P()),
        out_specs=P("prow", "pcol"),
        check_vma=False,
    )
```

```python
import functools

import jax
import jax.numpy as jnp
from jax import lax
from jax.experimental import pallas as pl
from jax.experimental.pallas import tpu as pltpu
from jax.sharding import PartitionSpec as P

BLOCK = 128
HEAD = 8
F32 = jnp.float32
BF16 = jnp.bfloat16
HIGHEST = lax.Precision.HIGHEST
MIB = 1024 * 1024

PLANE_GROUPS = [[16 * p + 4 * x + w for w in range(4) for p in range(8)] for x in range(4)]


def pack_rows(child, child_map):
    def kernel(map_ref, child_ref, out_ref, buf, turned, sems):
        c = lax.axis_index("prow") // 4
        shift = map_ref[c * 64] % 16

        def fetch(i):
            rows = pl.ds(pl.multiple_of(i * BLOCK, BLOCK), BLOCK)
            return pltpu.make_async_copy(child_ref.at[rows], buf.at[i], sems.at[0, i])

        def store(i):
            residue = (i + shift) % 16
            return pltpu.make_async_copy(
                turned.at[i], out_ref.at[:, residue % 8, residue // 8], sems.at[1, i]
            )

        def forward(i):
            fetch(i).wait()
            for w in range(4):
                b = (w - shift + 16) % 4
                turned[i, w] = buf[i, :, pl.ds(pl.multiple_of(b * BLOCK, BLOCK), BLOCK)]
            store(i).start()

        pl.loop(0, 16)(lambda i: fetch(i).start())
        pl.loop(0, 16)(forward)
        pl.loop(0, 16)(lambda i: store(i).wait())

    return pl.pallas_call(
        kernel,
        out_shape=jax.ShapeDtypeStruct((4, 8, 2, BLOCK, BLOCK), F32),
        in_specs=[pl.BlockSpec(memory_space=pltpu.SMEM), pl.BlockSpec(memory_space=pl.ANY)],
        out_specs=pl.BlockSpec(memory_space=pl.ANY),
        scratch_shapes=[
            pltpu.VMEM((16, BLOCK, 4 * BLOCK), F32),
            pltpu.VMEM((16, 4, BLOCK, BLOCK), F32),
            pltpu.SemaphoreType.DMA((2, 16)),
        ],
        compiler_params=pltpu.CompilerParams(vmem_limit_bytes=16 * MIB),
        cost_estimate=pl.CostEstimate(flops=0, bytes_accessed=8 * MIB, transcendentals=0),
        name="pack_rows",
    )(child_map, child)


def pack_cols(arrived, child_map):
    def kernel(map_ref, in_ref, *refs):
        out_refs, (buf, sems) = refs[:4], refs[4:]
        q = lax.axis_index("pcol")
        x, w = q // 4, q % 4

        def fetch(k):
            d, c = k // 2, k % 2
            column = 4 * ((x + d) % 4) + w
            a = ((column - map_ref[c * 64] % 16 + 16) % 16) // 4
            return pltpu.make_async_copy(in_ref.at[a, c], buf.at[k], sems.at[0, k])

        def store(k):
            return pltpu.make_async_copy(buf.at[k], out_refs[k // 2].at[k % 2], sems.at[1, k])

        for k in range(8):
            fetch(k).start()
        for k in range(8):
            fetch(k).wait()
            store(k).start()
        for k in range(8):
            store(k).wait()

    return pl.pallas_call(
        kernel,
        out_shape=[jax.ShapeDtypeStruct((2, 4, 2, BLOCK, BLOCK), F32)] * 4,
        in_specs=[pl.BlockSpec(memory_space=pltpu.SMEM), pl.BlockSpec(memory_space=pl.ANY)],
        out_specs=[pl.BlockSpec(memory_space=pltpu.HBM)] * 4,
        scratch_shapes=[
            pltpu.VMEM((8, 4, 2, BLOCK, BLOCK), F32), pltpu.SemaphoreType.DMA((2, 8))
        ],
        compiler_params=pltpu.CompilerParams(vmem_limit_bytes=16 * MIB),
        cost_estimate=pl.CostEstimate(flops=0, bytes_accessed=8 * MIB, transcendentals=0),
        name="pack_cols",
    )(child_map, arrived)


def diag_block(values):
    rows = lax.broadcasted_iota(jnp.int32, (BLOCK, BLOCK), 0)
    cols = lax.broadcasted_iota(jnp.int32, (BLOCK, BLOCK), 1)
    return jnp.where(rows == cols, jnp.broadcast_to(values, (BLOCK, BLOCK)), 0.0)


def local_row(map_ref, c, h, n, p):
    shift = map_ref[c * 64] % 16
    i = (p + 8 * n - shift + 16) % 16
    return map_ref[c * 64 + 16 * h + i] // 8


def local_col(map_ref, c, t, q):
    shift = map_ref[c * 64] % 16
    return map_ref[c * 64 + 16 * t + (q - shift + 16) % 16] // 16


def panel_terms(front, diagonal, arrived, child_map):
    def kernel(map_ref, front_ref, diag_ref, in_ref, *refs):
        out_refs, head_ref, (total, buf, sems) = refs[:4], refs[4], refs[5:]
        p, q = lax.axis_index("prow"), lax.axis_index("pcol")
        x, w = q // 4, q % 4
        chosen, copies = [], []
        for e in range(2):
            for c in range(2):
                at = (4 * e + w - map_ref[c * 64] % 16 + 16) % 16
                chosen.append(map_ref[c * 64 + 16 * x + at] // 16 == 0)
                copies.append(
                    pltpu.make_async_copy(
                        in_ref.at[at // 4, c], buf.at[2 * e + c], sems.at[2 * e + c]
                    )
                )
                copies[-1].start()
        total[...] = jnp.zeros_like(total)

        @pl.when(x < 2)
        def _():
            for l in range(12):
                total[l % 2 * 2 + x, l // 2] = front_ref[l * BLOCK : (l + 1) * BLOCK, :]

        @pl.when(p == q)
        def _():
            total[x, 0] += diag_block(diag_ref[pl.ds(q, 1), :])

        for k in range(4):
            e, c = k // 2, k % 2
            copies[k].wait()

            @pl.when(chosen[k])
            def _():
                def add(i):
                    l = local_row(map_ref, c, i // 2, i % 2, p)
                    total[l % 2 * 2 + e, l // 2] += buf[k, i // 2, i % 2]

                pl.loop(0, 8)(add)

        for d in range(4):
            out_refs[d][...] = total[(x + d) % 4]
        for e in range(2):
            head_ref[e] = total[e, 0]

    return pl.pallas_call(
        kernel,
        out_shape=[jax.ShapeDtypeStruct((6, BLOCK, BLOCK), F32)] * 4
        + [jax.ShapeDtypeStruct((2, BLOCK, BLOCK), F32)],
        grid=(1,),
        in_specs=[
            pl.BlockSpec(memory_space=pltpu.SMEM),
            pl.BlockSpec((12 * BLOCK, BLOCK), lambda i: (0, 0)),
            pl.BlockSpec((96, BLOCK), lambda i: (0, 0)),
            pl.BlockSpec(memory_space=pl.ANY),
        ],
        out_specs=[pl.BlockSpec((6, BLOCK, BLOCK), lambda i: (0, 0, 0))] * 4
        + [pl.BlockSpec((2, BLOCK, BLOCK), lambda i: (0, 0, 0))],
        scratch_shapes=[
            pltpu.VMEM((4, 6, BLOCK, BLOCK), F32),
            pltpu.VMEM((4, 4, 2, BLOCK, BLOCK), F32),
            pltpu.SemaphoreType.DMA((4,)),
        ],
        compiler_params=pltpu.CompilerParams(vmem_limit_bytes=24 * MIB),
        cost_estimate=pl.CostEstimate(flops=0, bytes_accessed=5 * MIB, transcendentals=0),
        name="panel_terms",
    )(child_map, front, diagonal, arrived)


NN = ((1,), (0,))
NT = ((1,), (1,))
TN = ((0,), (0,))


def dot(a, b, contract):
    dims = (contract, ((), ()))
    return lax.dot_general(a, b, dims, precision=HIGHEST, preferred_element_type=F32)


def dot1(a, b, contract):
    return lax.dot_general(a, b, (contract, ((), ())), preferred_element_type=F32)


def split(value):
    high = value.astype(BF16)
    return high, (value - high.astype(F32)).astype(BF16)


def dot3(a, b, contract):
    (ah, al), (bh, bl) = a, b
    return dot1(ah, bl, contract) + dot1(al, bh, contract) + dot1(ah, bh, contract)


def square_iotas(size):
    shape = (size, size)
    return lax.broadcasted_iota(jnp.int32, shape, 0), lax.broadcasted_iota(jnp.int32, shape, 1)


def newton_factor(a_ref, x_ref):
    ri, ci = square_iotas(a_ref.shape[0])
    one = jnp.where(ri == ci, 1.0, 0.0)

    def lower_half(e):
        return jnp.where(ri > ci, e, jnp.where(ri == ci, 0.5 * e, 0.0))

    a = a_ref[...]
    pivots = jnp.where(ri == ci, a, 0.0)
    scale = lax.rsqrt(jnp.sum(pivots, axis=0, keepdims=True))
    f = split(jnp.where(ri > ci, a * lax.rsqrt(jnp.sum(pivots, axis=1, keepdims=True)) * scale, 0.0))
    x = (one - (f[0].astype(F32) + f[1].astype(F32)) + dot1(f[0], f[0], NN)) * scale
    xs = split(x)
    e = dot3(split(dot3(xs, split(a), NN)), xs, NT) - one
    f = split(lower_half(e))
    g = dot3(f, xs, NN)
    x = x - g + dot1(f[0], g.astype(BF16), NN)
    t = dot(x, a, NN)
    e = dot(t, x, NT) - one
    f = split(lower_half(e))
    x_ref[...] = x - dot3(f, split(x), NN)
    a_ref[...] = jnp.where(ci >= ri, t - dot3(f, split(t), NN), 0.0)
    return jnp.max(jnp.sum(jnp.abs(e), axis=1, keepdims=True))


def direct_factor(t_ref):
    size = t_ref.shape[0]
    ri, ci = square_iotas(size)
    lane = lax.broadcasted_iota(jnp.int32, (1, 2 * size), 1)
    down = lax.broadcasted_iota(jnp.int32, (size, 1), 0)

    def step(j):
        row = t_ref[pl.ds(j, 1), :]
        row = row * lax.rsqrt(jnp.sum(jnp.where(lane == j, row, 0.0), axis=1, keepdims=True))
        col = jnp.broadcast_to(row[:, :size], (size, size))
        col = jnp.sum(jnp.where(ri == ci, col, 0.0), axis=1, keepdims=True)
        t_ref[...] = t_ref[...] - jnp.where(down > j, col, 0.0) * row
        t_ref[pl.ds(j, 1), :] = row

    pl.loop(0, size)(step)


def head_factor(gathered):
    size, wide = HEAD * BLOCK, 2 * BLOCK

    def kernel(*refs):
        in_refs, (wh_ref, wl_ref, own_ref), scratch = refs[:8], refs[8:11], refs[11:]
        m_ref, u_ref, w_ref, a_ref, x_ref, t_ref = scratch
        p, q = lax.axis_index("prow"), lax.axis_index("pcol")

        def place(k, in_ref, core_back, y_back):
            core = (q + core_back) % 2
            y = (2 * (p // 4) + (q // 2) % 2 - y_back + 4) % 4
            z = (p - k // 2 + 4) % 4
            row, col = y // 2 * 4 + z, k % 2 * 4 + y % 2 * 2 + core
            rows = pl.ds(pl.multiple_of(row * BLOCK, BLOCK), BLOCK)
            cols = pl.ds(pl.multiple_of(col * BLOCK, BLOCK), BLOCK)
            m_ref[rows, cols] = in_ref[k]

        for at in range(8):
            pl.loop(0, 8)(
                functools.partial(place, in_ref=in_refs[at], core_back=at // 4, y_back=at % 4)
            )
        for i in range(HEAD):
            for j in range(i, HEAD):
                rows, cols = slice(i * BLOCK, (i + 1) * BLOCK), slice(j * BLOCK, (j + 1) * BLOCK)
                value = m_ref[cols, rows].T
                if i // 4 == j // 4:
                    value = 0.5 * (m_ref[rows, cols] + value)
                u_ref[rows, cols] = value
                if i // 2 == j // 2 and i != j:
                    u_ref[cols, rows] = value.T
        ri, ci = square_iotas(wide)
        for s in range(0, size, wide):
            e = s + wide
            a_ref[...] = u_ref[s:e, s:e]
            off = newton_factor(a_ref, x_ref)

            @pl.when(jnp.logical_not(off < 5e-4))
            def _():
                t_ref[:, :wide] = u_ref[s:e, s:e]
                t_ref[:, wide:] = jnp.where(ri == ci, 1.0, 0.0)
                direct_factor(t_ref)
                a_ref[...] = jnp.where(ci >= ri, t_ref[:, :wide], 0.0)
                x_ref[...] = jnp.where(ri >= ci, t_ref[:, wide:], 0.0)

            u_ref[s:e, s:e] = a_ref[...]
            w_ref[s:e, s:e] = x_ref[...]
            inverse = split(x_ref[...])
            if s:
                w_ref[s:e, 0:s] = dot3(inverse, split(w_ref[s:e, 0:s]), NN)
            done = split(w_ref[s:e, 0:e])
            wh_ref[s:e, 0:e], wl_ref[s:e, 0:e] = done
            if e < size:
                wh_ref[s:e, e:] = jnp.zeros((wide, size - e), BF16)
                wl_ref[s:e, e:] = jnp.zeros((wide, size - e), BF16)
                right = dot3(inverse, split(u_ref[s:e, e:]), NN)
                u_ref[s:e, e:] = right
                right = split(right)
                for j in range(e, size, wide):
                    left = tuple(v[:, j - e : j - e + wide] for v in right)
                    rest = tuple(v[:, j - e :] for v in right)
                    u_ref[j : j + wide, j:] = u_ref[j : j + wide, j:] - dot3(left, rest, TN)
                    change = dot3(left, done, TN)
                    if s:
                        w_ref[j : j + wide, 0:s] = w_ref[j : j + wide, 0:s] - change[:, 0:s]
                    w_ref[j : j + wide, s:e] = -change[:, s:e]
        own_ref[...] = jnp.zeros((BLOCK, BLOCK), F32)

        @pl.when(q <= p)
        def _():
            rows = pl.ds(pl.multiple_of(q * BLOCK, BLOCK), BLOCK)
            cols = pl.ds(pl.multiple_of(p * BLOCK, BLOCK), BLOCK)
            own_ref[...] = u_ref[rows, cols].T

    vmem = pl.BlockSpec(memory_space=pltpu.VMEM)
    square = pltpu.VMEM((size, size), F32)
    return pl.pallas_call(
        kernel,
        out_shape=[
            jax.ShapeDtypeStruct((size, size), BF16),
            jax.ShapeDtypeStruct((size, size), BF16),
            jax.ShapeDtypeStruct((BLOCK, BLOCK), F32),
        ],
        in_specs=[vmem] * 8,
        out_specs=[vmem] * 3,
        scratch_shapes=[square] * 3
        + [pltpu.VMEM((wide, wide), F32)] * 2
        + [pltpu.VMEM((wide, 2 * wide), F32)],
        compiler_params=pltpu.CompilerParams(vmem_limit_bytes=40 * MIB),
        cost_estimate=pl.CostEstimate(
            flops=20_000_000_000, bytes_accessed=8 * MIB, transcendentals=0
        ),
        name="head_factor",
    )(*gathered)


def solve_columns(col_panel, inverse):
    size, wide = HEAD * BLOCK, 6 * BLOCK

    def kernel(wh, wl, *refs):
        in_refs, out_refs, (ch, cl, yh, yl, sems) = refs[:8], refs[8:10], refs[10:]
        p, q = lax.axis_index("prow"), lax.axis_index("pcol")
        for k, in_ref in enumerate(in_refs):
            m = (p // 4 + k // 4) % 2 * 4 + (p + 4 - k % 4) % 4
            cols = pl.ds(pl.multiple_of(m * BLOCK, BLOCK), BLOCK)
            for s in range(6):
                rows = slice(s * BLOCK, (s + 1) * BLOCK)
                ch[rows, cols], cl[rows, cols] = split(in_ref[s])
        for i in range(0, size, 256):
            e = i + 256
            y = dot3((ch[:, 0:e], cl[:, 0:e]), (wh[i:e, 0:e], wl[i:e, 0:e]), NT)
            yh[:, i:e], yl[:, i:e] = split(y)
        for i in range(0, size, 256):
            e = i + 256
            z = dot3((yh[:, i:], yl[:, i:]), (wh[i:, i:e], wl[i:, i:e]), NN)
            ch[:, i:e], cl[:, i:e] = split(z)

        @pl.when(q < HEAD)
        def _():
            rows = pl.ds(pl.multiple_of(q * BLOCK, BLOCK), BLOCK)
            ch[0:BLOCK, :] = -wh[rows, :]
            cl[0:BLOCK, :] = -wl[rows, :]

        stores = [
            pltpu.make_async_copy(ch, out_refs[0], sems.at[0]),
            pltpu.make_async_copy(cl, out_refs[1], sems.at[1]),
        ]
        for store in stores:
            store.start()
        for store in stores:
            store.wait()

    vmem = pl.BlockSpec(memory_space=pltpu.VMEM)
    return pl.pallas_call(
        kernel,
        out_shape=[jax.ShapeDtypeStruct((wide, size), BF16)] * 2,
        in_specs=[vmem] * 10,
        out_specs=[pl.BlockSpec(memory_space=pltpu.HBM)] * 2,
        scratch_shapes=[pltpu.VMEM((wide, size), BF16)] * 4 + [pltpu.SemaphoreType.DMA((2,))],
        compiler_params=pltpu.CompilerParams(vmem_limit_bytes=32 * MIB),
        cost_estimate=pl.CostEstimate(
            flops=8_000_000_000, bytes_accessed=10 * MIB, transcendentals=0
        ),
        name="solve_columns",
    )(*inverse, *col_panel)


def finish(front, diagonal, arrived, row_panel, solved, own, child_map):
    size, group, wide = HEAD * BLOCK, 4, 6 * BLOCK

    def kernel(
        map_ref, own_ref, diag_ref, row_ref, front_ref, *refs
    ):
        sources, out_ref, (sh, sl, *in_refs), sems = refs[:6], refs[6], refs[7:13], refs[13]
        step = pl.program_id(0)

        def load(k):
            return pltpu.make_async_copy(sources[k], (sh, sl, *in_refs)[k], sems.at[k])

        @pl.when(step == 0)
        def _():
            for k in range(6):
                load(k).start()

        p, q = lax.axis_index("prow"), lax.axis_index("pcol")
        out_ref[...] = front_ref[...]
        for s in range(6):
            l = 2 * s + jnp.where(q >= 8, 1, 0)

            @pl.when((q % 8 == p) & (l // group == step))
            def _():
                rows = pl.ds(pl.multiple_of((l % group) * BLOCK, BLOCK), BLOCK)
                out_ref[rows, s * BLOCK : (s + 1) * BLOCK] += diag_block(
                    diag_ref[pl.ds(16 * s + q, 1), :]
                )

        @pl.when(step == 0)
        def _():
            for k in range(6):
                load(k).wait()

        for c in range(2):
            places = [local_col(map_ref, c, (q // 4 + 4 - d) % 4, q) for d in range(4)]

            def add(k):
                l = local_row(map_ref, c, k // 2, k % 2, p)

                @pl.when(l // group == step)
                def _():
                    rows = pl.ds(pl.multiple_of((l % group) * BLOCK, BLOCK), BLOCK)
                    for d in range(4):
                        cols = pl.ds(pl.multiple_of(places[d] * BLOCK, BLOCK), BLOCK)
                        out_ref[rows, cols] += in_refs[d][c, k // 2, k % 2]

            pl.loop(0, 8)(add)

        @pl.when(q < HEAD)
        def _():
            out_ref[:, 0:BLOCK] = jnp.zeros((group * BLOCK, BLOCK), F32)

        rows = []
        for k in range(group):
            rows.append(
                jnp.concatenate([row_ref[k % 2 * 8 + m, k // 2] for m in range(HEAD)], axis=1)
            )
        rows = split(jnp.concatenate(rows, axis=0))
        for j in range(0, wide, 256):
            e = j + 256
            out_ref[:, j:e] -= dot3(rows, (sh[j:e, :], sl[j:e, :]), NT)

        @pl.when(step == 0)
        def _():
            out_ref[0:BLOCK, :] = jnp.zeros((BLOCK, wide), F32)
            out_ref[0:BLOCK, 0:BLOCK] = own_ref[...]

    def whole(*shape):
        return pl.BlockSpec(shape, lambda i: (0,) * len(shape), pipeline_mode=pl.Buffered(1))

    return pl.pallas_call(
        kernel,
        out_shape=jax.ShapeDtypeStruct((12 * BLOCK, wide), F32),
        grid=(12 // group,),
        in_specs=[
            pl.BlockSpec(memory_space=pltpu.SMEM),
            whole(BLOCK, BLOCK),
            whole(96, BLOCK),
            pl.BlockSpec((16, group // 2, BLOCK, BLOCK), lambda i: (0, i, 0, 0)),
            pl.BlockSpec((group * BLOCK, wide), lambda i: (i, 0)),
            *[pl.BlockSpec(memory_space=pltpu.HBM)] * 6,
        ],
        out_specs=pl.BlockSpec((group * BLOCK, wide), lambda i: (i, 0)),
        scratch_shapes=[pltpu.VMEM((wide, size), BF16)] * 2
        + [pltpu.VMEM((2, 4, 2, BLOCK, BLOCK), F32)] * 4
        + [pltpu.SemaphoreType.DMA((6,))],
        compiler_params=pltpu.CompilerParams(vmem_limit_bytes=60 * MIB),
        cost_estimate=pl.CostEstimate(
            flops=8_000_000_000, bytes_accessed=24 * MIB, transcendentals=0
        ),
        name="finish",
    )(child_map, own, diagonal, row_panel, front, *solved, *arrived)


def ahead_x(d):
    return [(4 * x + w, 4 * ((x + d) % 4) + w) for x in range(4) for w in range(4)]


def ahead_z(d):
    return [(4 * h + z, 4 * h + (z + d) % 4) for h in range(2) for z in range(4)]


def ahead_y(d):
    def rank(y, z, x, core):
        return (4 * (y // 2) + z) * 16 + 4 * x + 2 * (y % 2) + core

    return [
        (rank(y, z, x, core), rank((y + d) % 4, z, x, core))
        for y in range(4) for z in range(4) for x in range(4) for core in range(2)
    ]


OTHER_CORE = [(k, k ^ 1) for k in range(16)]
BOTH = ("prow", "pcol")


def sum_head(terms):
    held = terms
    for d in (1, 2, 3):
        held = held + lax.ppermute(terms, "pcol", ahead_x(d))
    return all_z(held)


def gather_head(along_z, beside):
    held = jnp.concatenate(along_z, axis=0)
    along_y = [held] + [lax.ppermute(held, BOTH, ahead_y(d)) for d in (1, 2, 3)]
    along_y, beside = lax.optimization_barrier((along_y, beside))
    return along_y + [lax.ppermute(part, "pcol", OTHER_CORE) for part in along_y], beside


def all_z(value):
    return [value] + [lax.ppermute(value, "prow", ahead_z(d)) for d in (1, 2, 3)]


def turn(piece):
    return lax.ppermute(
        piece,
        BOTH,
        [
            (p * 16 + (2 * par + e) * 4 + w, (4 * e + w) * 16 + p + 8 * par)
            for p in range(8) for par in range(2) for e in range(2) for w in range(4)
        ],
    )


def per_device(front, diagonal, child, child_map):
    child_map = child_map.reshape(128)
    diagonal = diagonal.reshape(96, BLOCK)
    sent = pack_rows(child, child_map).reshape(64, BLOCK, BLOCK)
    sent = lax.all_to_all(sent, BOTH, 0, 0, axis_index_groups=PLANE_GROUPS, tiled=True)
    sent = sent.reshape(4, 2, 4, 2, BLOCK, BLOCK)
    *terms, head_terms = panel_terms(front, diagonal, sent, child_map)
    behind = [lax.ppermute(terms[d], "pcol", ahead_x(d)) for d in (1, 2, 3)]
    head = sum_head(head_terms)
    blocks = pack_cols(sent, child_map)
    behind, head = lax.optimization_barrier((behind, head))
    piece = terms[0] + behind[0] + behind[1] + behind[2]
    row_panel = lax.all_gather(piece, "pcol")
    turned = turn(piece)
    other = lax.ppermute(turned, "prow", [(p, p ^ 4) for p in range(8)])
    other, head = lax.optimization_barrier((other, head))
    gathered, col_panel = gather_head(head, all_z(turned))
    col_panel += all_z(other)
    gathered, ahead = lax.optimization_barrier((gathered, blocks[1:]))
    arrived = [blocks[0]]
    for d in (1, 2, 3):
        arrived.append(lax.ppermute(ahead[d - 1], "pcol", ahead_x(d)))
    *inverse, own = head_factor(gathered)
    solved = solve_columns(col_panel, inverse)
    return finish(front, diagonal, arrived, row_panel, solved, own, child_map)


def solution(mesh):
    return jax.shard_map(
        per_device,
        mesh=mesh,
        in_specs=(P("prow", "pcol"), P(), P("prow", "pcol"), P()),
        out_specs=P("prow", "pcol"),
        check_vma=False,
    )
```

```python
import functools

import jax
import jax.numpy as jnp
from jax import lax
from jax.experimental import pallas as pl
from jax.experimental.pallas import tpu as pltpu
from jax.sharding import PartitionSpec as P

BLOCK = 128
HEAD = 8
F32 = jnp.float32
BF16 = jnp.bfloat16
HIGHEST = lax.Precision.HIGHEST
MIB = 1024 * 1024

PLANE_GROUPS = [[16 * p + 4 * x + w for w in range(4) for p in range(8)] for x in range(4)]


def pack_rows(child, child_map):
    def kernel(map_ref, child_ref, out_ref, buf, turned, sems):
        c = lax.axis_index("prow") // 4
        shift = map_ref[c * 64] % 16

        def fetch(i):
            rows = pl.ds(pl.multiple_of(i * BLOCK, BLOCK), BLOCK)
            return pltpu.make_async_copy(child_ref.at[rows], buf.at[i], sems.at[0, i])

        def store(i):
            residue = (i + shift) % 16
            return pltpu.make_async_copy(
                turned.at[i], out_ref.at[:, residue % 8, residue // 8], sems.at[1, i]
            )

        def forward(i):
            fetch(i).wait()
            for w in range(4):
                b = (w - shift + 16) % 4
                turned[i, w] = buf[i, :, pl.ds(pl.multiple_of(b * BLOCK, BLOCK), BLOCK)]
            store(i).start()

        pl.loop(0, 16)(lambda i: fetch(i).start())
        pl.loop(0, 16)(forward)
        pl.loop(0, 16)(lambda i: store(i).wait())

    return pl.pallas_call(
        kernel,
        out_shape=jax.ShapeDtypeStruct((4, 8, 2, BLOCK, BLOCK), F32),
        in_specs=[pl.BlockSpec(memory_space=pltpu.SMEM), pl.BlockSpec(memory_space=pl.ANY)],
        out_specs=pl.BlockSpec(memory_space=pl.ANY),
        scratch_shapes=[
            pltpu.VMEM((16, BLOCK, 4 * BLOCK), F32),
            pltpu.VMEM((16, 4, BLOCK, BLOCK), F32),
            pltpu.SemaphoreType.DMA((2, 16)),
        ],
        compiler_params=pltpu.CompilerParams(vmem_limit_bytes=16 * MIB),
        cost_estimate=pl.CostEstimate(flops=0, bytes_accessed=8 * MIB, transcendentals=0),
        name="pack_rows",
    )(child_map, child)


def pack_cols(arrived, child_map):
    def kernel(map_ref, in_ref, *refs):
        out_refs, (buf, sems) = refs[:4], refs[4:]
        q = lax.axis_index("pcol")
        x, w = q // 4, q % 4

        def fetch(k):
            d, c = k // 2, k % 2
            column = 4 * ((x + d) % 4) + w
            a = ((column - map_ref[c * 64] % 16 + 16) % 16) // 4
            return pltpu.make_async_copy(in_ref.at[a, c], buf.at[k], sems.at[0, k])

        def store(k):
            return pltpu.make_async_copy(buf.at[k], out_refs[k // 2].at[k % 2], sems.at[1, k])

        for k in range(8):
            fetch(k).start()
        for k in range(8):
            fetch(k).wait()
            store(k).start()
        for k in range(8):
            store(k).wait()

    return pl.pallas_call(
        kernel,
        out_shape=[jax.ShapeDtypeStruct((2, 4, 2, BLOCK, BLOCK), F32)] * 4,
        in_specs=[pl.BlockSpec(memory_space=pltpu.SMEM), pl.BlockSpec(memory_space=pl.ANY)],
        out_specs=[pl.BlockSpec(memory_space=pl.ANY)] * 4,
        scratch_shapes=[
            pltpu.VMEM((8, 4, 2, BLOCK, BLOCK), F32), pltpu.SemaphoreType.DMA((2, 8))
        ],
        compiler_params=pltpu.CompilerParams(vmem_limit_bytes=16 * MIB),
        cost_estimate=pl.CostEstimate(flops=0, bytes_accessed=8 * MIB, transcendentals=0),
        name="pack_cols",
    )(child_map, arrived)


def diag_block(values):
    rows = lax.broadcasted_iota(jnp.int32, (BLOCK, BLOCK), 0)
    cols = lax.broadcasted_iota(jnp.int32, (BLOCK, BLOCK), 1)
    return jnp.where(rows == cols, jnp.broadcast_to(values, (BLOCK, BLOCK)), 0.0)


def local_row(map_ref, c, h, n, p):
    shift = map_ref[c * 64] % 16
    i = (p + 8 * n - shift + 16) % 16
    return map_ref[c * 64 + 16 * h + i] // 8


def local_col(map_ref, c, t, q):
    shift = map_ref[c * 64] % 16
    return map_ref[c * 64 + 16 * t + (q - shift + 16) % 16] // 16


def panel_terms(front, diagonal, arrived, child_map):
    def kernel(map_ref, front_ref, diag_ref, in_ref, *refs):
        out_refs, head_ref, (total, buf, sems) = refs[:4], refs[4], refs[5:]
        p, q = lax.axis_index("prow"), lax.axis_index("pcol")
        x, w = q // 4, q % 4
        chosen, copies = [], []
        for e in range(2):
            for c in range(2):
                at = (4 * e + w - map_ref[c * 64] % 16 + 16) % 16
                chosen.append(map_ref[c * 64 + 16 * x + at] // 16 == 0)
                copies.append(
                    pltpu.make_async_copy(
                        in_ref.at[at // 4, c], buf.at[2 * e + c], sems.at[2 * e + c]
                    )
                )
                copies[-1].start()
        total[...] = jnp.zeros_like(total)

        @pl.when(x < 2)
        def _():
            for l in range(12):
                total[l % 2 * 2 + x, l // 2] = front_ref[l * BLOCK : (l + 1) * BLOCK, :]

        @pl.when(p == q)
        def _():
            total[x, 0] += diag_block(diag_ref[pl.ds(q, 1), :])

        for k in range(4):
            e, c = k // 2, k % 2
            copies[k].wait()

            @pl.when(chosen[k])
            def _():
                def add(i):
                    l = local_row(map_ref, c, i // 2, i % 2, p)
                    total[l % 2 * 2 + e, l // 2] += buf[k, i // 2, i % 2]

                pl.loop(0, 8)(add)

        for d in range(4):
            out_refs[d][...] = total[(x + d) % 4]
        for e in range(2):
            head_ref[e] = total[e, 0]

    return pl.pallas_call(
        kernel,
        out_shape=[jax.ShapeDtypeStruct((6, BLOCK, BLOCK), F32)] * 4
        + [jax.ShapeDtypeStruct((2, BLOCK, BLOCK), F32)],
        grid=(1,),
        in_specs=[
            pl.BlockSpec(memory_space=pltpu.SMEM),
            pl.BlockSpec((12 * BLOCK, BLOCK), lambda i: (0, 0)),
            pl.BlockSpec((96, BLOCK), lambda i: (0, 0)),
            pl.BlockSpec(memory_space=pl.ANY),
        ],
        out_specs=[pl.BlockSpec((6, BLOCK, BLOCK), lambda i: (0, 0, 0))] * 4
        + [pl.BlockSpec((2, BLOCK, BLOCK), lambda i: (0, 0, 0))],
        scratch_shapes=[
            pltpu.VMEM((4, 6, BLOCK, BLOCK), F32),
            pltpu.VMEM((4, 4, 2, BLOCK, BLOCK), F32),
            pltpu.SemaphoreType.DMA((4,)),
        ],
        compiler_params=pltpu.CompilerParams(vmem_limit_bytes=24 * MIB),
        cost_estimate=pl.CostEstimate(flops=0, bytes_accessed=5 * MIB, transcendentals=0),
        name="panel_terms",
    )(child_map, front, diagonal, arrived)


NN = ((1,), (0,))
NT = ((1,), (1,))
TN = ((0,), (0,))


def dot(a, b, contract):
    dims = (contract, ((), ()))
    return lax.dot_general(a, b, dims, precision=HIGHEST, preferred_element_type=F32)


def dot1(a, b, contract):
    return lax.dot_general(a, b, (contract, ((), ())), preferred_element_type=F32)


def split(value):
    high = value.astype(BF16)
    return high, (value - high.astype(F32)).astype(BF16)


def dot3(a, b, contract):
    (ah, al), (bh, bl) = a, b
    return dot1(ah, bl, contract) + dot1(al, bh, contract) + dot1(ah, bh, contract)


def square_iotas(size):
    shape = (size, size)
    return lax.broadcasted_iota(jnp.int32, shape, 0), lax.broadcasted_iota(jnp.int32, shape, 1)


def newton_factor(a_ref, x_ref):
    ri, ci = square_iotas(a_ref.shape[0])
    one = jnp.where(ri == ci, 1.0, 0.0)

    def lower_half(e):
        return jnp.where(ri > ci, e, jnp.where(ri == ci, 0.5 * e, 0.0))

    a = a_ref[...]
    pivots = jnp.where(ri == ci, a, 0.0)
    scale = lax.rsqrt(jnp.sum(pivots, axis=0, keepdims=True))
    f = split(jnp.where(ri > ci, a * lax.rsqrt(jnp.sum(pivots, axis=1, keepdims=True)) * scale, 0.0))
    x = (one - (f[0].astype(F32) + f[1].astype(F32)) + dot1(f[0], f[0], NN)) * scale
    xs = split(x)
    e = dot3(split(dot3(xs, split(a), NN)), xs, NT) - one
    f = split(lower_half(e))
    g = dot3(f, xs, NN)
    x = x - g + dot1(f[0], g.astype(BF16), NN)
    t = dot(x, a, NN)
    e = dot(t, x, NT) - one
    f = split(lower_half(e))
    x_ref[...] = x - dot3(f, split(x), NN)
    a_ref[...] = jnp.where(ci >= ri, t - dot3(f, split(t), NN), 0.0)
    return jnp.max(jnp.sum(jnp.abs(e), axis=1, keepdims=True))


def direct_factor(t_ref):
    size = t_ref.shape[0]
    ri, ci = square_iotas(size)
    lane = lax.broadcasted_iota(jnp.int32, (1, 2 * size), 1)
    down = lax.broadcasted_iota(jnp.int32, (size, 1), 0)

    def step(j):
        row = t_ref[pl.ds(j, 1), :]
        row = row * lax.rsqrt(jnp.sum(jnp.where(lane == j, row, 0.0), axis=1, keepdims=True))
        col = jnp.broadcast_to(row[:, :size], (size, size))
        col = jnp.sum(jnp.where(ri == ci, col, 0.0), axis=1, keepdims=True)
        t_ref[...] = t_ref[...] - jnp.where(down > j, col, 0.0) * row
        t_ref[pl.ds(j, 1), :] = row

    pl.loop(0, size)(step)


def head_factor(gathered):
    size, wide = HEAD * BLOCK, 2 * BLOCK

    def kernel(*refs):
        in_refs, (wh_ref, wl_ref, own_ref), scratch = refs[:8], refs[8:11], refs[11:]
        m_ref, u_ref, w_ref, a_ref, x_ref, t_ref = scratch
        p, q = lax.axis_index("prow"), lax.axis_index("pcol")

        def place(k, in_ref, core_back, z_back):
            core = (q + core_back) % 2
            y = (2 * (p // 4) + (q // 2) % 2 - k // 2 + 4) % 4
            z = (p - z_back + 4) % 4
            row, col = y // 2 * 4 + z, k % 2 * 4 + y % 2 * 2 + core
            rows = pl.ds(pl.multiple_of(row * BLOCK, BLOCK), BLOCK)
            cols = pl.ds(pl.multiple_of(col * BLOCK, BLOCK), BLOCK)
            m_ref[rows, cols] = in_ref[k]

        for at in range(8):
            pl.loop(0, 8)(
                functools.partial(place, in_ref=in_refs[at], core_back=at // 4, z_back=at % 4)
            )
        for i in range(HEAD):
            for j in range(i, HEAD):
                rows, cols = slice(i * BLOCK, (i + 1) * BLOCK), slice(j * BLOCK, (j + 1) * BLOCK)
                value = m_ref[cols, rows].T
                if i // 4 == j // 4:
                    value = 0.5 * (m_ref[rows, cols] + value)
                u_ref[rows, cols] = value
                if i // 2 == j // 2 and i != j:
                    u_ref[cols, rows] = value.T
        ri, ci = square_iotas(wide)
        for s in range(0, size, wide):
            e = s + wide
            a_ref[...] = u_ref[s:e, s:e]
            off = newton_factor(a_ref, x_ref)

            @pl.when(jnp.logical_not(off < 5e-4))
            def _():
                t_ref[:, :wide] = u_ref[s:e, s:e]
                t_ref[:, wide:] = jnp.where(ri == ci, 1.0, 0.0)
                direct_factor(t_ref)
                a_ref[...] = jnp.where(ci >= ri, t_ref[:, :wide], 0.0)
                x_ref[...] = jnp.where(ri >= ci, t_ref[:, wide:], 0.0)

            u_ref[s:e, s:e] = a_ref[...]
            w_ref[s:e, s:e] = x_ref[...]
            inverse = split(x_ref[...])
            if s:
                w_ref[s:e, 0:s] = dot3(inverse, split(w_ref[s:e, 0:s]), NN)
            done = split(w_ref[s:e, 0:e])
            wh_ref[s:e, 0:e], wl_ref[s:e, 0:e] = done
            if e < size:
                wh_ref[s:e, e:] = jnp.zeros((wide, size - e), BF16)
                wl_ref[s:e, e:] = jnp.zeros((wide, size - e), BF16)
                right = dot3(inverse, split(u_ref[s:e, e:]), NN)
                u_ref[s:e, e:] = right
                right = split(right)
                for j in range(e, size, wide):
                    left = tuple(v[:, j - e : j - e + wide] for v in right)
                    rest = tuple(v[:, j - e :] for v in right)
                    u_ref[j : j + wide, j:] = u_ref[j : j + wide, j:] - dot3(left, rest, TN)
                    change = dot3(left, done, TN)
                    if s:
                        w_ref[j : j + wide, 0:s] = w_ref[j : j + wide, 0:s] - change[:, 0:s]
                    w_ref[j : j + wide, s:e] = -change[:, s:e]
        own_ref[...] = jnp.zeros((BLOCK, BLOCK), F32)

        @pl.when(q <= p)
        def _():
            rows = pl.ds(pl.multiple_of(q * BLOCK, BLOCK), BLOCK)
            cols = pl.ds(pl.multiple_of(p * BLOCK, BLOCK), BLOCK)
            own_ref[...] = u_ref[rows, cols].T

    vmem = pl.BlockSpec(memory_space=pltpu.VMEM)
    square = pltpu.VMEM((size, size), F32)
    return pl.pallas_call(
        kernel,
        out_shape=[
            jax.ShapeDtypeStruct((size, size), BF16),
            jax.ShapeDtypeStruct((size, size), BF16),
            jax.ShapeDtypeStruct((BLOCK, BLOCK), F32),
        ],
        in_specs=[vmem] * 8,
        out_specs=[vmem] * 3,
        scratch_shapes=[square] * 3
        + [pltpu.VMEM((wide, wide), F32)] * 2
        + [pltpu.VMEM((wide, 2 * wide), F32)],
        compiler_params=pltpu.CompilerParams(vmem_limit_bytes=40 * MIB),
        cost_estimate=pl.CostEstimate(
            flops=20_000_000_000, bytes_accessed=8 * MIB, transcendentals=0
        ),
        name="head_factor",
    )(*gathered)


def solve_columns(col_panel, inverse):
    size, wide = HEAD * BLOCK, 6 * BLOCK

    def kernel(wh, wl, *refs):
        in_refs, out_refs, (ch, cl, yh, yl, sems) = refs[:8], refs[8:10], refs[10:]
        p, q = lax.axis_index("prow"), lax.axis_index("pcol")
        for k, in_ref in enumerate(in_refs):
            m = (p // 4 + k // 4) % 2 * 4 + (p + 4 - k % 4) % 4
            cols = pl.ds(pl.multiple_of(m * BLOCK, BLOCK), BLOCK)
            for s in range(6):
                rows = slice(s * BLOCK, (s + 1) * BLOCK)
                ch[rows, cols], cl[rows, cols] = split(in_ref[s])
        for i in range(0, size, 256):
            e = i + 256
            y = dot3((ch[:, 0:e], cl[:, 0:e]), (wh[i:e, 0:e], wl[i:e, 0:e]), NT)
            yh[:, i:e], yl[:, i:e] = split(y)
        for i in range(0, size, 256):
            e = i + 256
            z = dot3((yh[:, i:], yl[:, i:]), (wh[i:, i:e], wl[i:, i:e]), NN)
            ch[:, i:e], cl[:, i:e] = split(z)

        @pl.when(q < HEAD)
        def _():
            rows = pl.ds(pl.multiple_of(q * BLOCK, BLOCK), BLOCK)
            ch[0:BLOCK, :] = -wh[rows, :]
            cl[0:BLOCK, :] = -wl[rows, :]

        stores = [
            pltpu.make_async_copy(ch, out_refs[0], sems.at[0]),
            pltpu.make_async_copy(cl, out_refs[1], sems.at[1]),
        ]
        for store in stores:
            store.start()
        for store in stores:
            store.wait()

    vmem = pl.BlockSpec(memory_space=pltpu.VMEM)
    return pl.pallas_call(
        kernel,
        out_shape=[jax.ShapeDtypeStruct((wide, size), BF16)] * 2,
        in_specs=[vmem] * 10,
        out_specs=[pl.BlockSpec(memory_space=pltpu.HBM)] * 2,
        scratch_shapes=[pltpu.VMEM((wide, size), BF16)] * 4 + [pltpu.SemaphoreType.DMA((2,))],
        compiler_params=pltpu.CompilerParams(vmem_limit_bytes=32 * MIB),
        cost_estimate=pl.CostEstimate(
            flops=8_000_000_000, bytes_accessed=10 * MIB, transcendentals=0
        ),
        name="solve_columns",
    )(*inverse, *col_panel)


def finish(front, diagonal, arrived, row_panel, solved, own, child_map):
    size, group, wide = HEAD * BLOCK, 4, 6 * BLOCK

    def kernel(
        map_ref, sh, sl, own_ref, diag_ref, in0, in1, in2, in3, row_ref, front_ref, out_ref
    ):
        step = pl.program_id(0)
        p, q = lax.axis_index("prow"), lax.axis_index("pcol")
        out_ref[...] = front_ref[...]
        for s in range(6):
            l = 2 * s + jnp.where(q >= 8, 1, 0)

            @pl.when((q % 8 == p) & (l // group == step))
            def _():
                rows = pl.ds(pl.multiple_of((l % group) * BLOCK, BLOCK), BLOCK)
                out_ref[rows, s * BLOCK : (s + 1) * BLOCK] += diag_block(
                    diag_ref[pl.ds(16 * s + q, 1), :]
                )

        in_refs = (in0, in1, in2, in3)
        for c in range(2):
            places = [local_col(map_ref, c, (q // 4 + 4 - d) % 4, q) for d in range(4)]

            def add(k):
                l = local_row(map_ref, c, k // 2, k % 2, p)

                @pl.when(l // group == step)
                def _():
                    rows = pl.ds(pl.multiple_of((l % group) * BLOCK, BLOCK), BLOCK)
                    for d in range(4):
                        cols = pl.ds(pl.multiple_of(places[d] * BLOCK, BLOCK), BLOCK)
                        out_ref[rows, cols] += in_refs[d][c, k // 2, k % 2]

            pl.loop(0, 8)(add)

        @pl.when(q < HEAD)
        def _():
            out_ref[:, 0:BLOCK] = jnp.zeros((group * BLOCK, BLOCK), F32)

        rows = []
        for k in range(group):
            rows.append(
                jnp.concatenate([row_ref[k % 2 * 8 + m, k // 2] for m in range(HEAD)], axis=1)
            )
        rows = split(jnp.concatenate(rows, axis=0))
        for j in range(0, wide, 256):
            e = j + 256
            out_ref[:, j:e] -= dot3(rows, (sh[j:e, :], sl[j:e, :]), NT)

        @pl.when(step == 0)
        def _():
            out_ref[0:BLOCK, :] = jnp.zeros((BLOCK, wide), F32)
            out_ref[0:BLOCK, 0:BLOCK] = own_ref[...]

    def whole(*shape):
        return pl.BlockSpec(shape, lambda i: (0,) * len(shape), pipeline_mode=pl.Buffered(1))

    return pl.pallas_call(
        kernel,
        out_shape=jax.ShapeDtypeStruct((12 * BLOCK, wide), F32),
        grid=(12 // group,),
        in_specs=[
            pl.BlockSpec(memory_space=pltpu.SMEM),
            whole(wide, size),
            whole(wide, size),
            whole(BLOCK, BLOCK),
            whole(96, BLOCK),
            *[whole(2, 4, 2, BLOCK, BLOCK)] * 4,
            pl.BlockSpec((16, group // 2, BLOCK, BLOCK), lambda i: (0, i, 0, 0)),
            pl.BlockSpec((group * BLOCK, wide), lambda i: (i, 0)),
        ],
        out_specs=pl.BlockSpec((group * BLOCK, wide), lambda i: (i, 0)),
        compiler_params=pltpu.CompilerParams(vmem_limit_bytes=60 * MIB),
        cost_estimate=pl.CostEstimate(
            flops=8_000_000_000, bytes_accessed=24 * MIB, transcendentals=0
        ),
        name="finish",
    )(child_map, *solved, own, diagonal, *arrived, row_panel, front)


def ahead_x(d):
    return [(4 * x + w, 4 * ((x + d) % 4) + w) for x in range(4) for w in range(4)]


def ahead_z(d):
    return [(4 * h + z, 4 * h + (z + d) % 4) for h in range(2) for z in range(4)]


def ahead_y(d):
    def rank(y, z, x, core):
        return (4 * (y // 2) + z) * 16 + 4 * x + 2 * (y % 2) + core

    return [
        (rank(y, z, x, core), rank((y + d) % 4, z, x, core))
        for y in range(4) for z in range(4) for x in range(4) for core in range(2)
    ]


OTHER_CORE = [(k, k ^ 1) for k in range(16)]
BOTH = ("prow", "pcol")


def gather_head(terms):
    held = terms
    for d in (1, 2, 3):
        held = held + lax.ppermute(terms, "pcol", ahead_x(d))
    summed = held
    along_y = [held] + [lax.ppermute(held, BOTH, ahead_y(d)) for d in (1, 2, 3)]
    held = jnp.concatenate(along_y, axis=0)
    along_z = [held] + [lax.ppermute(held, "prow", ahead_z(d)) for d in (1, 2, 3)]
    return summed, along_z, [lax.ppermute(part, "pcol", OTHER_CORE) for part in along_z]


def gather_columns(piece):
    turned = lax.ppermute(
        piece,
        BOTH,
        [
            (p * 16 + (2 * par + e) * 4 + w, (4 * e + w) * 16 + p + 8 * par)
            for p in range(8) for par in range(2) for e in range(2) for w in range(4)
        ],
    )
    other = lax.ppermute(turned, "prow", [(p, p ^ 4) for p in range(8)])
    near = [turned] + [lax.ppermute(turned, "prow", ahead_z(d)) for d in (1, 2, 3)]
    near, other = lax.optimization_barrier((near, other))
    return near + [other] + [lax.ppermute(other, "prow", ahead_z(d)) for d in (1, 2, 3)]


def per_device(front, diagonal, child, child_map):
    child_map = child_map.reshape(128)
    diagonal = diagonal.reshape(96, BLOCK)
    sent = pack_rows(child, child_map).reshape(64, BLOCK, BLOCK)
    sent = lax.all_to_all(sent, BOTH, 0, 0, axis_index_groups=PLANE_GROUPS, tiled=True)
    sent = sent.reshape(4, 2, 4, 2, BLOCK, BLOCK)
    *terms, head_terms = panel_terms(front, diagonal, sent, child_map)
    summed, along_z, twins = gather_head(head_terms)
    summed, *terms = lax.optimization_barrier([summed, *terms])
    behind = [lax.ppermute(terms[d], "pcol", ahead_x(d)) for d in (1, 2, 3)]
    behind, along_z = lax.optimization_barrier((behind, along_z))
    piece = terms[0] + behind[0] + behind[1] + behind[2]
    gathered = along_z + twins
    blocks = pack_cols(sent, child_map)
    piece, *ahead = lax.optimization_barrier([piece, *blocks[1:]])
    arrived = [blocks[0]]
    for d in (1, 2, 3):
        arrived.append(lax.ppermute(ahead[d - 1], "pcol", ahead_x(d)))
    row_panel = lax.all_gather(piece, "pcol")
    col_panel = gather_columns(piece)
    *inverse, own = head_factor(gathered)
    solved = solve_columns(col_panel, inverse)
    return finish(front, diagonal, arrived, row_panel, solved, own, child_map)


def solution(mesh):
    return jax.shard_map(
        per_device,
        mesh=mesh,
        in_specs=(P("prow", "pcol"), P(), P("prow", "pcol"), P()),
        out_specs=P("prow", "pcol"),
        check_vma=False,
    )
```
